256 devices in a mesh: replica: 2 (over x_hi), tm: 32 (over y, z), tensor: 4 (over x_lo, core).
Axes of the slice: x: 4 (x_hi: 2, x_lo: 2; x = x_hi * 2 + x_lo), y: 4, z: 8, core: 2. Of those that a mesh axis runs over, the one named last changes fastest.
Arguments:
- activations: bfloat16 [64, 128, 4096], P(('replica', 'tm'), None, 'tensor'), may hold values from -6 to 6
- action_codes: int32 [4, 16], P('replica'), may hold values from 0 to 7
- norm_gain: float32 [4096], replicated, may hold values from 0.5 to 1.5
- action_scale: float32 [8, 4096], replicated, may hold values from -1.5 to 1.5
- action_shift: float32 [8, 4096], replicated, may hold values from -3 to 3
- qkv_weight: bfloat16 [4096, 32, 384], P('tm', 'tensor'), may hold values from -0.09375 to 0.09375
- qk_gains: float32 [2, 128], replicated, may hold values from 0.5 to 1.5
- out_weight: bfloat16 [32, 128, 4096], P('tensor', None, 'tm'), may hold values from -0.09375 to 0.09375
- grad_output: bfloat16 [64, 128, 4096], P(('replica', 'tm'), None, 'tensor'), may hold values from -6 to 6
Outputs:
- block_output: bfloat16 [64, 128, 4096], P(('replica', 'tm'), None, 'tensor')
- grad_input: bfloat16 [64, 128, 4096], P(('replica', 'tm'), None, 'tensor')
- grad_scale: float32 [8, 4096], P(None, 'tensor')
- grad_shift: float32 [8, 4096], P(None, 'tensor')
The draws below stay inside these ranges and needn't reach their ends.
All inputs are finite; a program needn't handle non-finite values.
Results may differ from the reference program's by a relative error of at most 0.02.
Values may be sent and summed in bfloat16 or wider, within the bound.
No kernel may reach another device: no remote copies, remote signals or barrier semaphores. Data moves between devices by JAX's collectives and lax.ppermute only.
A program may use at most 192 MiB of HBM per device.

```python
import jax
import jax.numpy as jnp
from jax import lax

D = 4096
HEADS = 32
HS = 128
CODES = 8
FRAMES = 16
CLIPS = 4
ROWS = 64
PATCHES = 128


def place_ends(array, own_key, low, top_value):
    dims = array.shape
    place = [jax.random.randint(jax.random.fold_in(own_key, axis), (), 0, dims[axis]) for axis in range(len(dims))]
    array = array.at[tuple(place)].set(low)
    longest = dims.index(max(dims))
    place[longest] = (place[longest] + 1) % dims[longest]
    return array.at[tuple(place)].set(top_value)


def steps_of(rng, dims, split, least, high):
    loudness = 1.0
    for dim, parts in split:
        steps = jax.random.uniform(jax.random.fold_in(jax.random.fold_in(rng, 6), dim), (parts,), jnp.float32, least / len(split), high / len(split))
        loudness = loudness * jnp.repeat(jnp.exp(steps), dims[dim] // parts).reshape((-1,) + (1,) * (len(dims) - 1 - dim))
    return loudness


def centred(stream_key, dims, width, limit, pieces=(), kind=jnp.bfloat16):
    result = jax.random.normal(stream_key, dims, jnp.float32) * width
    if len(pieces) > 0:
        result = steps_of(stream_key, dims, pieces, -0.22, 0.18) * result
    return jnp.clip(result, min=-limit, max=limit).astype(kind)


def setup_inputs(seed: int = 0) -> dict:
    splits = jax.random.split(jax.random.key(seed), 10)
    activations = centred(splits[0], (ROWS, PATCHES, D), 1.0, 6.0, ((0, 64), (2, 4)))
    action_codes = place_ends(jax.random.randint(splits[1], (CLIPS, FRAMES), 0, CODES), jax.random.fold_in(splits[1], 1), 0, CODES - 1).astype(jnp.int32)
    norm_gain = jnp.clip(1.0 + 0.1 * jax.random.normal(splits[2], (D,), jnp.float32), 0.5, 1.5)
    action_scale = centred(splits[3], (CODES, D), 0.3, 1.5, (), jnp.float32)
    action_shift = centred(splits[4], (CODES, D), 0.5, 3.0, (), jnp.float32)
    qkv_weight = centred(splits[5], (D, HEADS, 3 * HS), D ** -0.5, 0.09375, ((0, 32), (1, 4)))
    qk_gains = jnp.clip(1.0 + 0.1 * jax.random.normal(splits[6], (2, HS), jnp.float32), 0.5, 1.5)
    out_weight = centred(splits[7], (HEADS, HS, D), (HEADS * HS) ** -0.5, 0.09375, ((0, 4), (2, 32)))
    grad_output = centred(splits[8], (ROWS, PATCHES, D), 1.0, 6.0, ((0, 64), (2, 4)))
    return {"activations": activations, "action_codes": action_codes, "norm_gain": norm_gain, "action_scale": action_scale, "action_shift": action_shift, "qkv_weight": qkv_weight, "qk_gains": qk_gains, "out_weight": out_weight, "grad_output": grad_output}


EPS = 1e-06

def attend(qkv, qk_gains):
    head_width = qkv.shape[-1] // 3
    queries = qkv[..., :head_width]
    key_rows = qkv[..., head_width:2 * head_width]
    values = qkv[..., 2 * head_width:]
    queries = queries * lax.rsqrt(lax.optimization_barrier(jnp.mean(queries * queries, -1, keepdims=True)) + EPS) * qk_gains[0]
    key_rows = key_rows * lax.rsqrt(lax.optimization_barrier(jnp.mean(key_rows * key_rows, -1, keepdims=True)) + EPS) * qk_gains[1]
    scores = jnp.einsum('cipht,cjpht->cphij', queries, key_rows) * head_width ** (-0.5)
    position = jnp.arange(qkv.shape[1])
    causal = position[None, :] <= position[:, None]
    weights = jnp.where(causal, jnp.exp(scores), 0.0)
    probabilities = weights / lax.optimization_barrier(jnp.sum(weights, -1, keepdims=True))
    return jnp.einsum('cphij,cjpht->cipht', probabilities, values)

def reference(activations, action_codes, norm_gain, action_scale, action_shift, qkv_weight, qk_gains, out_weight, grad_output):
    highest = lax.Precision.HIGHEST
    qkv_flat = qkv_weight.reshape(D, HEADS * 3 * HS)
    out_flat = out_weight.reshape(HEADS * HS, D)
    x_clips = activations.reshape(CLIPS, FRAMES, PATCHES, D)
    g_clips = grad_output.reshape(CLIPS, FRAMES, PATCHES, D)

    def one_clip(bundle):
        x_clip, grad_clip, code_clip = bundle
        x_float = x_clip.astype(jnp.float32)
        inverse = lax.rsqrt(lax.optimization_barrier(jnp.mean(x_float * x_float, -1, keepdims=True)) + EPS)
        x_hat = x_float * inverse
        normed = x_hat * norm_gain
        one_hot = (code_clip.astype(jnp.int32)[:, None] == jnp.arange(CODES).astype(jnp.int32)[None, :]).astype(jnp.float32)
        scale_rows = jnp.dot(one_hot, action_scale, precision=highest)[:, None, :]
        shift_rows = jnp.dot(one_hot, action_shift, precision=highest)[:, None, :]
        hidden = (normed * (1.0 + scale_rows) + shift_rows).astype(jnp.bfloat16)
        qkv = jnp.dot(hidden.reshape(FRAMES * PATCHES, D), qkv_flat, preferred_element_type=jnp.float32).astype(jnp.bfloat16)
        qkv_float = qkv.astype(jnp.float32).reshape(1, FRAMES, PATCHES, HEADS, 3 * HS)
        attended, pullback = jax.vjp(lambda inner: attend(inner, qk_gains), qkv_float)
        attended_bf = attended.astype(jnp.bfloat16).reshape(FRAMES * PATCHES, HEADS * HS)
        branch = jnp.dot(attended_bf, out_flat, preferred_element_type=jnp.float32).reshape(FRAMES, PATCHES, D)
        block_out = (x_float + branch).astype(jnp.bfloat16)
        d_attended = jnp.dot(grad_clip.reshape(FRAMES * PATCHES, D), out_flat.T, preferred_element_type=jnp.float32).astype(jnp.bfloat16)
        d_qkv = pullback(d_attended.astype(jnp.float32).reshape(attended.shape))[0].astype(jnp.bfloat16)
        d_hidden = jnp.dot(d_qkv.reshape(FRAMES * PATCHES, HEADS * 3 * HS), qkv_flat.T, preferred_element_type=jnp.float32).reshape(FRAMES, PATCHES, D)
        d_hat = d_hidden * (1.0 + scale_rows) * norm_gain
        row_term = lax.optimization_barrier(jnp.mean(d_hat * x_hat, -1, keepdims=True))
        grad_in = (grad_clip.astype(jnp.float32) + inverse * (d_hat - x_hat * row_term)).astype(jnp.bfloat16)
        d_scale = jnp.dot(one_hot.T, lax.optimization_barrier(jnp.sum(d_hidden * normed, 1)), precision=highest)
        d_shift = jnp.dot(one_hot.T, lax.optimization_barrier(jnp.sum(d_hidden, 1)), precision=highest)
        return (block_out, grad_in, d_scale, d_shift)
    outputs, grads, scale_terms, shift_terms = lax.map(one_clip, (x_clips, g_clips, action_codes))
    factor = (ROWS * PATCHES) ** (-0.5)
    block_output = outputs.reshape(ROWS, PATCHES, D)
    grad_input = grads.reshape(ROWS, PATCHES, D)
    grad_scale = lax.optimization_barrier(jnp.sum(scale_terms, 0)) * factor
    grad_shift = lax.optimization_barrier(jnp.sum(shift_terms, 0)) * factor
    return (block_output, grad_input, grad_scale, grad_shift)
```

```python
import functools

import jax
import jax.numpy as jnp
from jax import lax
from jax.experimental import pallas as pl
from jax.experimental.pallas import tpu as pltpu
from jax.sharding import PartitionSpec as P

EPS = 1e-06
BF = jnp.bfloat16
F32 = jnp.float32
EXTRA = 16


def dot_nn(a, b):
    return lax.dot_general(a, b, (((1,), (0,)), ((), ())), preferred_element_type=F32)


def dot_nt(a, b):
    return lax.dot_general(a, b, (((1,), (1,)), ((), ())), preferred_element_type=F32)


def dot_tn(a, b):
    return lax.dot_general(a, b, (((0,), (0,)), ((), ())), preferred_element_type=F32)


def halves(value):
    high = value.astype(BF)
    return high, (value - high.astype(F32)).astype(BF)


def block_kernel(
    patch_dev,
    frames,
    hidden_hbm,
    grad_hbm,
    normed_hbm,
    scaled_hbm,
    weight_hbm,
    gains_ref,
    hot_ref,
    y_ref,
    dh_ref,
    hidden,
    grad,
    normed,
    scaled,
    weight,
    qkv_acc,
    da_acc,
    attended,
    dqkv,
    sems,
):
    parts = hidden.shape[0]
    tokens = hidden.shape[1]
    quarter = hidden.shape[2]
    width = gains_ref.shape[1]
    wide = qkv_acc.shape[1]
    heads = wide // (3 * width)
    replicas = y_ref.shape[0]
    group = tokens // replicas

    def first(part):
        return [
            pltpu.make_async_copy(hidden_hbm.at[part], hidden.at[part], sems.at[part, 0]),
            pltpu.make_async_copy(weight_hbm.at[part], weight.at[part], sems.at[part, 1]),
            pltpu.make_async_copy(grad_hbm.at[part], grad.at[part], sems.at[part, 2]),
        ]

    def second(part):
        return [
            pltpu.make_async_copy(normed_hbm.at[part], normed.at[part], sems.at[part, 3]),
            pltpu.make_async_copy(scaled_hbm.at[part], scaled.at[part], sems.at[part, 4]),
        ]

    for part in range(parts):
        for copy in first(part):
            copy.start()
    for part in range(parts):
        for copy in second(part):
            copy.start()

    qkv_acc[...] = jnp.zeros_like(qkv_acc)
    da_acc[...] = jnp.zeros_like(da_acc)
    for part in range(parts):
        for copy in first(part):
            copy.wait()
        qkv_acc[...] += dot_nn(hidden[part], weight[part, :, :wide])
        da_acc[...] += dot_nn(grad[part], weight[part, :, wide:])

    gain_q = gains_ref[0:1, :]
    gain_k = gains_ref[1:2, :]
    row = lax.broadcasted_iota(jnp.int32, (group, group), 0)
    col = lax.broadcasted_iota(jnp.int32, (group, group), 1)
    clip_tokens = frames * patch_dev
    mask = (
        (row % patch_dev == col % patch_dev)
        & (row // clip_tokens == col // clip_tokens)
        & (col <= row)
    )
    factor = width ** (-0.5)
    for rep in range(replicas):
        rows = slice(rep * group, (rep + 1) * group)
        for head in range(heads):
            base = head * 3 * width
            take = lambda at: qkv_acc[rows, base + at * width : base + (at + 1) * width].astype(
                BF
            )
            q = take(0).astype(F32)
            k = take(1).astype(F32)
            value = take(2)
            d_out = da_acc[rows, head * width : (head + 1) * width].astype(BF)
            inv_q = lax.rsqrt(jnp.mean(q * q, -1, keepdims=True) + EPS)
            inv_k = lax.rsqrt(jnp.mean(k * k, -1, keepdims=True) + EPS)
            q_hat = q * inv_q
            k_hat = k * inv_k
            queries = (q_hat * gain_q).astype(BF)
            keys = (k_hat * gain_k).astype(BF)
            scores = dot_nt(queries, keys) * factor
            weights = jnp.where(mask, jnp.exp(scores), 0.0)
            probs = weights / jnp.sum(weights, -1, keepdims=True)
            probs_bf = probs.astype(BF)
            out = dot_nn(probs_bf, value)
            attended[rows, head * width : (head + 1) * width] = out.astype(BF)
            d_value = dot_tn(probs_bf, d_out)
            d_probs = dot_nt(d_out, value)
            d_scores = probs * (d_probs - jnp.sum(d_probs * probs, -1, keepdims=True))
            d_scores = (d_scores * factor).astype(BF)
            d_q = dot_nn(d_scores, keys) * gain_q
            d_k = dot_tn(d_scores, queries) * gain_k
            d_q = inv_q * (d_q - q_hat * jnp.mean(d_q * q_hat, -1, keepdims=True))
            d_k = inv_k * (d_k - k_hat * jnp.mean(d_k * k_hat, -1, keepdims=True))
            for at, item in enumerate((d_q, d_k, d_value)):
                dqkv[rows, base + at * width : base + (at + 1) * width] = item.astype(BF)

    for part in range(parts):
        for copy in second(part):
            copy.wait()
    block = min(quarter, 256)
    hot = hot_ref[...]
    codes = hot.shape[0]
    ones = jnp.ones((8, block), BF)
    tail = dh_ref.shape[2] - group
    terms = jnp.zeros((8, tokens), F32)
    for part in range(parts):
        for at in range(quarter // block):
            cols = slice(at * block, (at + 1) * block)
            w_block = weight[part, cols, :]
            y_block = dot_nt(attended[...], w_block[:, wide:]).astype(BF)
            d_block = dot_nt(dqkv[...], w_block[:, :wide])
            for rep in range(replicas):
                rows = slice(rep * group, (rep + 1) * group)
                y_ref[rep, part, :, cols] = y_block[rows]
                dh_ref[rep, part, 0:group, cols] = d_block[rows].astype(BF)
            high, low = halves(d_block * normed[part, :, cols].astype(F32))
            d_scale = dot_nn(hot, high) + dot_nn(hot, low)
            high, low = halves(d_block)
            d_shift = dot_nn(hot, high) + dot_nn(hot, low)
            high, low = halves(d_block * scaled[part, :, cols].astype(F32))
            terms += dot_nt(ones, high) + dot_nt(ones, low)
            for rep, item in enumerate((d_scale, d_shift)):
                dh_ref[rep, part, group : group + codes, cols] = item.astype(BF)
    high, low = halves(terms)
    sub = lax.broadcasted_iota(jnp.int32, (8, group), 0)
    for rep in range(replicas):
        lanes = slice(rep * group, (rep + 1) * group)
        both = jnp.where(
            sub == 0,
            high[:, lanes].astype(F32),
            jnp.where(sub == 1, low[:, lanes].astype(F32), 0.0),
        ).astype(BF)
        for part in range(parts):
            dh_ref[rep, part, group + codes :, :] = jnp.zeros((tail - codes, quarter), BF)
            dh_ref[rep, part, group + codes : group + codes + 8, 0:group] = both


def block(hidden, grad, normed, scaled, weight, gains, hot, patch_dev, frames, replicas):
    parts, tokens, quarter = hidden.shape
    total = weight.shape[-1]
    wide = total // 4 * 3
    narrow = total - wide
    group = tokens // replicas
    any_spec = pl.BlockSpec(memory_space=pl.ANY)
    vmem_spec = pl.BlockSpec(memory_space=pltpu.VMEM)
    flops = 4 * tokens * parts * quarter * total
    moved = 2 * (weight.size + 6 * hidden.size)
    return pl.pallas_call(
        functools.partial(block_kernel, patch_dev, frames),
        out_shape=(
            jax.ShapeDtypeStruct((replicas, parts, group, quarter), BF),
            jax.ShapeDtypeStruct((replicas, parts, group + EXTRA, quarter), BF),
        ),
        in_specs=[any_spec] * 5 + [vmem_spec] * 2,
        out_specs=(vmem_spec, vmem_spec),
        scratch_shapes=[
            pltpu.VMEM((parts, tokens, quarter), BF),
            pltpu.VMEM((parts, tokens, quarter), BF),
            pltpu.VMEM((parts, tokens, quarter), BF),
            pltpu.VMEM((parts, tokens, quarter), BF),
            pltpu.VMEM((parts, quarter, total), BF),
            pltpu.VMEM((tokens, wide), F32),
            pltpu.VMEM((tokens, narrow), F32),
            pltpu.VMEM((tokens, narrow), BF),
            pltpu.VMEM((tokens, wide), BF),
            pltpu.SemaphoreType.DMA((parts, 5)),
        ],
        compiler_params=pltpu.CompilerParams(vmem_limit_bytes=52 * 1024 * 1024),
        cost_estimate=pl.CostEstimate(flops=flops, bytes_accessed=moved, transcendentals=0),
        name="block",
    )(hidden, grad, normed, scaled, weight, gains, hot)


def shards(
    activations,
    action_codes,
    norm_gain,
    action_scale,
    action_shift,
    qkv_weight,
    qk_gains,
    out_weight,
    grad_output,
):
    highest = lax.Precision.HIGHEST
    replicas = lax.axis_size("replica")
    shards_tm = lax.axis_size("tm")
    parts = lax.axis_size("tensor")
    rep = lax.axis_index("replica")
    part = lax.axis_index("tensor")
    frames = action_codes.shape[1]
    quarter = activations.shape[2]
    patch_dev = activations.shape[1] // shards_tm
    depth = qkv_weight.shape[0]
    heads = qkv_weight.shape[1] // replicas
    triple = qkv_weight.shape[2]
    width = triple // 3
    code_count = action_scale.shape[0]
    d_model = parts * quarter
    group = shards_tm * patch_dev
    tokens = replicas * group

    qkv_mine = lax.dynamic_slice_in_dim(qkv_weight, rep * heads, heads, 1)
    out_mine = lax.dynamic_slice_in_dim(out_weight, rep * heads, heads, 0)
    mine = jnp.concatenate(
        [
            qkv_mine.reshape(depth, heads * triple),
            out_mine.reshape(heads * width, depth).T,
        ],
        axis=1,
    )
    weight = lax.all_gather(mine, "tm", axis=0, tiled=True).reshape(parts, quarter, -1)

    both = jnp.concatenate(
        [
            activations.reshape(shards_tm, patch_dev, quarter),
            grad_output.reshape(shards_tm, patch_dev, quarter),
        ],
        axis=1,
    )
    both = lax.all_to_all(both, "tm", split_axis=0, concat_axis=0, tiled=True)
    full = lax.all_gather(both, ("replica", "tensor"), axis=0)
    full = full.reshape(replicas, parts, shards_tm, 2, patch_dev, quarter)
    full = full.transpose(3, 1, 0, 2, 4, 5).reshape(2, parts, tokens, quarter)
    x_full = full[0].astype(F32)
    grad_full = full[1]

    other = lax.ppermute(action_codes, "replica", [(i, 1 - i) for i in range(2)])
    codes = jnp.where(
        rep == 0,
        jnp.concatenate([action_codes, other], 0),
        jnp.concatenate([other, action_codes], 0),
    ).reshape(-1)
    code_range = jnp.arange(code_count)
    one_hot = (codes[:, None] == code_range[None, :]).astype(F32)
    scale_rows = jnp.dot(one_hot, action_scale, precision=highest)
    shift_rows = jnp.dot(one_hot, action_shift, precision=highest)

    def spread(rows):
        rows = rows.reshape(rows.shape[0], parts, quarter).transpose(1, 0, 2)
        return jnp.repeat(rows, patch_dev, axis=1)

    inverse = lax.rsqrt(jnp.sum(x_full * x_full, (0, 2)) / d_model + EPS)
    normed = x_full * inverse[None, :, None] * norm_gain.reshape(parts, 1, quarter)
    scaled = normed * (1.0 + spread(scale_rows))
    hidden = (scaled + spread(shift_rows)).astype(BF)
    hot_tokens = jnp.repeat(one_hot, patch_dev, axis=0).T.astype(BF)

    y_part, dh_part = block(
        hidden,
        grad_full,
        normed.astype(BF),
        scaled.astype(BF),
        weight,
        qk_gains,
        hot_tokens,
        patch_dev,
        frames,
        replicas,
    )
    branch = lax.psum_scatter(
        y_part.reshape(replicas * parts, group, quarter),
        ("replica", "tensor"),
        scatter_dimension=0,
        tiled=True,
    )[0].astype(F32)
    dh_all = lax.all_to_all(
        dh_part.reshape(replicas * parts, group + EXTRA, quarter),
        ("replica", "tensor"),
        split_axis=0,
        concat_axis=0,
        tiled=True,
    )
    dh_sum = jnp.sum(dh_all.astype(F32), 0)
    d_hidden = dh_sum[:group]
    grads = dh_sum[group : group + code_count]
    row_term = dh_sum[group + code_count : group + code_count + 2, :group].sum(0) / d_model

    def own(rows):
        return lax.dynamic_slice_in_dim(rows, part * quarter, quarter, rows.ndim - 1)

    def own_rows(rows):
        rows = lax.dynamic_slice_in_dim(own(rows), rep * shards_tm, shards_tm, 0)
        return jnp.repeat(rows, patch_dev, axis=0)

    gain_own = own(norm_gain)
    x_own = both[:, :patch_dev].reshape(group, quarter).astype(F32)
    grad_own = both[:, patch_dev:].reshape(group, quarter).astype(F32)
    inv_own = lax.dynamic_slice_in_dim(inverse, rep * group, group, 0)[:, None]
    d_hat = d_hidden * (1.0 + own_rows(scale_rows)) * gain_own
    dx = grad_own + inv_own * (d_hat - x_own * inv_own * row_term[:, None])
    y = x_own + branch
    send = jnp.concatenate(
        [
            y.astype(BF).reshape(shards_tm, patch_dev, quarter),
            dx.astype(BF).reshape(shards_tm, patch_dev, quarter),
            jnp.broadcast_to(grads.astype(BF)[None], (shards_tm, code_count, quarter)),
        ],
        axis=1,
    )
    back = lax.all_to_all(send, "tm", split_axis=0, concat_axis=0, tiled=True)
    y_frames = back[:, :patch_dev].reshape(1, group, quarter)
    dx_frames = back[:, patch_dev : 2 * patch_dev].reshape(1, group, quarter)
    token_total = tokens * shards_tm
    grad_mine = jnp.sum(back[:, 2 * patch_dev :].astype(F32), 0) * token_total ** (-0.5)
    grad_other = lax.ppermute(grad_mine, "replica", [(i, 1 - i) for i in range(2)])
    d_scale = jnp.where(rep == 0, grad_mine, grad_other)
    d_shift = jnp.where(rep == 0, grad_other, grad_mine)
    return (y_frames, dx_frames, d_scale, d_shift)


def solution(mesh):
    placed = (
        P(("replica", "tm"), None, "tensor"),
        P("replica", None),
        P(),
        P(),
        P(),
        P("tm", "tensor", None),
        P(),
        P("tensor", None, "tm"),
        P(("replica", "tm"), None, "tensor"),
    )
    return jax.shard_map(
        shards,
        mesh=mesh,
        in_specs=placed,
        out_specs=(
            P(("replica", "tm"), None, "tensor"),
            P(("replica", "tm"), None, "tensor"),
            P(None, "tensor"),
            P(None, "tensor"),
        ),
        check_vma=False,
    )
```

```python
import functools

import jax
import jax.numpy as jnp
from jax import lax
from jax.experimental import pallas as pl
from jax.experimental.pallas import tpu as pltpu
from jax.sharding import PartitionSpec as P

EPS = 1e-06
BF = jnp.bfloat16
F32 = jnp.float32
EXTRA = 16


def dot_nn(a, b):
    return lax.dot_general(a, b, (((1,), (0,)), ((), ())), preferred_element_type=F32)


def dot_nt(a, b):
    return lax.dot_general(a, b, (((1,), (1,)), ((), ())), preferred_element_type=F32)


def dot_tn(a, b):
    return lax.dot_general(a, b, (((0,), (0,)), ((), ())), preferred_element_type=F32)


def halves(value):
    high = value.astype(BF)
    return high, (value - high.astype(F32)).astype(BF)


def selector(shape, pick):
    row = lax.broadcasted_iota(jnp.int32, shape, 0)
    col = lax.broadcasted_iota(jnp.int32, shape, 1)
    return jnp.where(pick(row, col), 1.0, 0.0).astype(BF)


def pack_kernel(patch_dev, place_ref, x_ref, g_ref, qkv_ref, out_ref, both_ref, near_ref, far_ref):
    rows = x_ref.shape[0]
    pair = 2 * patch_dev
    pick_x = selector(
        (2 * rows, rows),
        lambda m, n: (m % pair < patch_dev) & (m // pair * patch_dev + m % pair == n),
    )
    pick_g = selector(
        (2 * rows, rows),
        lambda m, n: (m % pair >= patch_dev)
        & (m // pair * patch_dev + m % pair - patch_dev == n),
    )
    both_ref[...] = (dot_nn(pick_x, x_ref[...]) + dot_nn(pick_g, g_ref[...])).astype(BF)
    depth = near_ref.shape[0] + far_ref.shape[0]
    near = near_ref.shape[0]
    all_heads = qkv_ref.shape[0] // depth
    heads = out_ref.shape[0] // 2
    triple = qkv_ref.shape[1]
    width = triple // 3
    rep = place_ref[0]
    for head in range(heads):
        own = rep * heads + head
        pick = selector(
            (depth, all_heads * depth),
            lambda m, n: m * all_heads + own == n,
        )
        part = dot_nn(pick, qkv_ref[...]).astype(BF)
        cols = slice(head * triple, (head + 1) * triple)
        near_ref[:, cols] = part[:near]
        far_ref[:, cols] = part[near:]
        eye = selector((depth, depth), lambda m, n: m == n)
        part = dot_nt(eye, out_ref[own]).astype(BF)
        cols = slice(heads * triple + head * width, heads * triple + (head + 1) * width)
        near_ref[:, cols] = part[:near]
        far_ref[:, cols] = part[near:]


def prep_kernel(
    patch_dev,
    place_ref,
    full_ref,
    hot_ref,
    gain_ref,
    scale_ref,
    shift_ref,
    hidden_ref,
    grad_ref,
    normed_ref,
    scaled_ref,
    coef_ref,
    xinv_ref,
    xown_ref,
    gown_ref,
):
    parts = full_ref.shape[1]
    group = hidden_ref.shape[1]
    quarter = full_ref.shape[3]
    pair = 2 * patch_dev
    pick_x = selector(
        (group, 2 * group), lambda m, n: m // patch_dev * pair + m % patch_dev == n
    )
    pick_g = selector(
        (group, 2 * group), lambda m, n: m // patch_dev * pair + m % patch_dev + patch_dev == n
    )
    hot = hot_ref[...]

    def rows_of(table):
        high, low = halves(table)
        return dot_nn(hot, high) + dot_nn(hot, low)

    square = jnp.zeros((group, 1), F32)
    for part in range(parts):
        x = dot_nn(pick_x, full_ref[0, part])
        square += jnp.sum(x * x, -1, keepdims=True)
    inverse = lax.rsqrt(square / (parts * quarter) + EPS)
    for part in range(parts):
        x = dot_nn(pick_x, full_ref[0, part])
        normed = x * inverse * gain_ref[part]
        scaled = normed * (1.0 + rows_of(scale_ref[part]))
        hidden_ref[part] = (scaled + rows_of(shift_ref[part])).astype(BF)
        normed_ref[part] = normed.astype(BF)
        scaled_ref[part] = scaled.astype(BF)
        grad_ref[part] = dot_nn(pick_g, full_ref[0, part]).astype(BF)

    @pl.when(pl.program_id(0) == place_ref[0])
    def _():
        own = place_ref[1]
        rows = full_ref[0, own]
        x = dot_nn(pick_x, rows)
        xown_ref[...] = x.astype(BF)
        gown_ref[...] = dot_nn(pick_g, rows).astype(BF)
        coef_ref[...] = inverse * (1.0 + rows_of(scale_ref[own])) * gain_ref[own]
        xinv_ref[...] = x * inverse * inverse


def block_kernel(
    patch_dev,
    frames,
    plan,
    place_ref,
    gains_ref,
    hot_ref,
    hidden_hbm,
    grad_hbm,
    normed_hbm,
    scaled_hbm,
    *refs,
):
    count = 1 + max(item[0] for item in plan)
    pieces = refs[:count]
    (
        y_keep,
        y_give,
        dh_keep,
        dh_give,
        hidden,
        grad,
        normed,
        scaled,
        weight,
        qkv_acc,
        da_acc,
        attended,
        dqkv,
        y_stage,
        dh_stage,
        sems,
        weight_sems,
        out_sems,
    ) = refs[count:]
    parts, tokens, quarter = hidden.shape
    width = gains_ref.shape[1]
    wide = qkv_acc.shape[1]
    heads = wide // (3 * width)
    cores, ring, group, _ = y_stage.shape
    replicas = tokens // group
    along = ring // replicas
    rows_y = place_ref[2]
    rows_z = place_ref[3]
    spot_x = place_ref[4]
    core = place_ref[5]
    depth = weight.shape[0] // (NY * NZ)

    def inputs(at):
        part = (rows_y + at) % NY
        result = [
            pltpu.make_async_copy(hidden_hbm.at[part], hidden.at[part], sems.at[at, 0]),
            pltpu.make_async_copy(grad_hbm.at[part], grad.at[part], sems.at[at, 1]),
        ]
        for number, (index, start, size, dy, dz, place) in enumerate(plan):
            if dy == at:
                owner = part * NZ + (rows_z + dz) % NZ
                target = pl.multiple_of(owner * depth + place, 16)
                result.append(
                    pltpu.make_async_copy(
                        pieces[index].at[pl.ds(start, size)],
                        weight.at[pl.ds(target, size)],
                        weight_sems.at[number],
                    )
                )
        return result

    def second(part):
        return [
            pltpu.make_async_copy(normed_hbm.at[part], normed.at[part], sems.at[part, 2]),
            pltpu.make_async_copy(scaled_hbm.at[part], scaled.at[part], sems.at[part, 3]),
        ]

    order = (0, 1, 3, 2)
    for at in order:
        for copy in inputs(at):
            copy.start()
    for part in range(parts):
        for copy in second(part):
            copy.start()

    qkv_acc[...] = jnp.zeros_like(qkv_acc)
    da_acc[...] = jnp.zeros_like(da_acc)
    for at in order:
        for copy in inputs(at):
            copy.wait()
        part = (rows_y + at) % NY
        rows = pl.ds(pl.multiple_of(part * quarter, quarter), quarter)
        qkv_acc[...] += dot_nn(hidden[part], weight[rows, :wide])
        da_acc[...] += dot_nn(grad[part], weight[rows, wide:])

    gain_q = gains_ref[0:1, :]
    gain_k = gains_ref[1:2, :]
    row = lax.broadcasted_iota(jnp.int32, (group, group), 0)
    col = lax.broadcasted_iota(jnp.int32, (group, group), 1)
    clip_tokens = frames * patch_dev
    mask = (
        (row % patch_dev == col % patch_dev)
        & (row // clip_tokens == col // clip_tokens)
        & (col <= row)
    )
    factor = width ** (-0.5)
    for rep in range(replicas):
        rows = slice(rep * group, (rep + 1) * group)
        for head in range(heads):
            base = head * 3 * width
            take = lambda at: qkv_acc[rows, base + at * width : base + (at + 1) * width].astype(
                BF
            )
            q = take(0).astype(F32)
            k = take(1).astype(F32)
            value = take(2)
            d_out = da_acc[rows, head * width : (head + 1) * width].astype(BF)
            inv_q = lax.rsqrt(jnp.mean(q * q, -1, keepdims=True) + EPS)
            inv_k = lax.rsqrt(jnp.mean(k * k, -1, keepdims=True) + EPS)
            q_hat = q * inv_q
            k_hat = k * inv_k
            queries = (q_hat * gain_q).astype(BF)
            keys = (k_hat * gain_k).astype(BF)
            scores = dot_nt(queries, keys) * factor
            weights = jnp.where(mask, jnp.exp(scores), 0.0)
            probs = weights / jnp.sum(weights, -1, keepdims=True)
            probs_bf = probs.astype(BF)
            out = dot_nn(probs_bf, value)
            attended[rows, head * width : (head + 1) * width] = out.astype(BF)
            d_value = dot_tn(probs_bf, d_out)
            d_probs = dot_nt(d_out, value)
            d_scores = probs * (d_probs - jnp.sum(d_probs * probs, -1, keepdims=True))
            d_scores = (d_scores * factor).astype(BF)
            d_q = dot_nn(d_scores, keys) * gain_q
            d_k = dot_tn(d_scores, queries) * gain_k
            d_q = inv_q * (d_q - q_hat * jnp.mean(d_q * q_hat, -1, keepdims=True))
            d_k = inv_k * (d_k - k_hat * jnp.mean(d_k * k_hat, -1, keepdims=True))
            for at, item in enumerate((d_q, d_k, d_value)):
                dqkv[rows, base + at * width : base + (at + 1) * width] = item.astype(BF)

    def outputs(stage, keep, give, base):
        result = []
        for step in range(ring):
            target = (spot_x + step) % ring
            for side, out in enumerate((keep, give)):
                result.append(
                    pltpu.make_async_copy(
                        stage.at[(core + side) % cores, target],
                        out.at[step],
                        out_sems.at[base, step, side],
                    )
                )
        return result

    block = min(quarter, 256)
    for part in range(parts):
        for at in range(quarter // block):
            cols = slice(at * block, (at + 1) * block)
            w_block = weight[part * quarter + at * block : part * quarter + (at + 1) * block, wide:]
            y_block = dot_nt(attended[...], w_block).astype(BF)
            for rep in range(replicas):
                rows = slice(rep * group, (rep + 1) * group)
                y_stage[part % cores, rep * along + part // cores, :, cols] = y_block[rows]
    y_copies = outputs(y_stage, y_keep, y_give, 0)
    for copy in y_copies:
        copy.start()

    for part in range(parts):
        for copy in second(part):
            copy.wait()
    hot = hot_ref[...]
    codes = hot.shape[0]
    ones = jnp.ones((8, block), BF)
    tail = dh_stage.shape[2] - group
    terms = jnp.zeros((8, tokens), F32)
    for part in range(parts):
        for at in range(quarter // block):
            cols = slice(at * block, (at + 1) * block)
            w_block = weight[part * quarter + at * block : part * quarter + (at + 1) * block, :wide]
            d_block = dot_nt(dqkv[...], w_block)
            high, low = halves(d_block * normed[part, :, cols].astype(F32))
            d_scale = dot_nn(hot, high) + dot_nn(hot, low)
            high, low = halves(d_block)
            d_shift = dot_nn(hot, high) + dot_nn(hot, low)
            for rep, item in enumerate((d_scale, d_shift)):
                where = (part % cores, rep * along + part // cores)
                rows = slice(rep * group, (rep + 1) * group)
                dh_stage[where[0], where[1], 0:group, cols] = high[rows]
                dh_stage[where[0], where[1], group : group + codes, cols] = item.astype(BF)
            high, low = halves(d_block * scaled[part, :, cols].astype(F32))
            terms += dot_nt(ones, high) + dot_nt(ones, low)
    high, low = halves(terms)
    sub = lax.broadcasted_iota(jnp.int32, (8, group), 0)
    for rep in range(replicas):
        lanes = slice(rep * group, (rep + 1) * group)
        both = jnp.where(
            sub == 0,
            high[:, lanes].astype(F32),
            jnp.where(sub == 1, low[:, lanes].astype(F32), 0.0),
        ).astype(BF)
        for part in range(parts):
            where = (part % cores, rep * along + part // cores)
            dh_stage[where[0], where[1], group + codes :, :] = jnp.zeros(
                (tail - codes, quarter), BF
            )
            dh_stage[where[0], where[1], group + codes : group + codes + 8, 0:group] = both
    dh_copies = outputs(dh_stage, dh_keep, dh_give, 1)
    for copy in dh_copies:
        copy.start()
    for copy in y_copies + dh_copies:
        copy.wait()


def finish_kernel(
    patch_dev,
    code_count,
    parts,
    yk_ref,
    yr_ref,
    ya_ref,
    yb_ref,
    dk_ref,
    dr_ref,
    da_ref,
    db_ref,
    coef_ref,
    xinv_ref,
    xown_ref,
    gown_ref,
    send_ref,
):
    group, quarter = xown_ref.shape
    y = (
        xown_ref[...].astype(F32)
        + (yk_ref[0].astype(F32) + yr_ref[0].astype(F32))
        + (ya_ref[...].astype(F32) + yb_ref[...].astype(F32))
    )
    total = (dk_ref[0].astype(F32) + dr_ref[0].astype(F32)) + (
        da_ref[...].astype(F32) + db_ref[...].astype(F32)
    )
    terms = total[group + code_count : group + code_count + 8, :group]
    term = (terms[0:1] + terms[1:2]) / (quarter * parts)
    term = jnp.broadcast_to(term, (group, group)).T[:, 0:1]
    dx = gown_ref[...].astype(F32) + (total[:group] * coef_ref[...] - xinv_ref[...] * term)
    grads = total[group : group + code_count].astype(BF)
    span = 2 * patch_dev + code_count
    rows = send_ref.shape[0]
    pick_y = selector(
        (rows, group),
        lambda m, n: (m % span < patch_dev) & (m // span * patch_dev + m % span == n),
    )
    pick_d = selector(
        (rows, group),
        lambda m, n: (m % span >= patch_dev)
        & (m % span < 2 * patch_dev)
        & (m // span * patch_dev + m % span - patch_dev == n),
    )
    pick_g = selector((rows, code_count), lambda m, n: m % span - 2 * patch_dev == n)
    send_ref[...] = (
        dot_nn(pick_y, y.astype(BF)) + dot_nn(pick_d, dx.astype(BF)) + dot_nn(pick_g, grads)
    ).astype(BF)


def unpack_kernel(patch_dev, factor, back_ref, y_ref, dx_ref, sum_ref):
    group = y_ref.shape[0]
    rows = back_ref.shape[0]
    codes = sum_ref.shape[0]
    span = 2 * patch_dev + codes
    back = back_ref[...]
    pick_y = selector((group, rows), lambda m, n: m // patch_dev * span + m % patch_dev == n)
    pick_d = selector(
        (group, rows), lambda m, n: m // patch_dev * span + m % patch_dev + patch_dev == n
    )
    pick_g = selector((codes, rows), lambda m, n: n % span - 2 * patch_dev == m)
    y_ref[...] = dot_nn(pick_y, back).astype(BF)
    dx_ref[...] = dot_nn(pick_d, back).astype(BF)
    sum_ref[...] = dot_nn(pick_g, back) * factor


NY = 4
NZ = 8
CORES = 2
VMEM = pl.BlockSpec(memory_space=pltpu.VMEM)
SMEM = pl.BlockSpec(memory_space=pltpu.SMEM)
ANY = pl.BlockSpec(memory_space=pl.ANY)


def fetch(value, dy, dz):
    pairs = []
    for y in range(NY):
        for z in range(NZ):
            pairs.append((((y + dy) % NY) * NZ + (z + dz) % NZ, y * NZ + z))
    return lax.ppermute(value, "tm", pairs)


def fetch_x(value, dx, ring):
    pairs = []
    for x in range(ring):
        for core in range(CORES):
            pairs.append((((x + dx) % ring) * CORES + core, x * CORES + core))
    return lax.ppermute(value, ("replica", "tensor"), pairs)


def swap_cores(value, ring):
    pairs = []
    for x in range(ring):
        for core in range(CORES):
            pairs.append((x * CORES + core, x * CORES + 1 - core))
    return lax.ppermute(value, ("replica", "tensor"), pairs)


def gather_weight(near, far):
    a = near.shape[0]
    b = far.shape[0]
    pieces = []
    plan = []

    def add(value, blocks):
        start = 0
        for size, dy, dz, place in blocks:
            plan.append((len(pieces), start, size, dy % NY, dz % NZ, place))
            start += size
        pieces.append(value)

    def near_block(dy, dzs):
        return [(a, dy, dz, 0) for dz in dzs]

    def far_block(dz):
        return [(b, dy, dz, a) for dy in (0, 1, -1, 2)]

    z_up = fetch(near, 0, 1)
    z_dn = fetch(near, 0, -1)
    fy_up = fetch(far, 1, 0)
    fy_dn = fetch(far, -1, 0)
    y_up = fetch(near, 1, 0)
    y_dn = fetch(near, -1, 0)
    add(near, near_block(0, (0,)))
    add(y_up, near_block(1, (0,)))
    add(y_dn, near_block(-1, (0,)))
    z_up2 = fetch(z_up, 0, 1)
    z_dn2 = fetch(z_dn, 0, -1)
    fy_low = fetch(fy_up[: b // 2], 1, 0)
    fy_high = fetch(fy_dn[b // 2 :], -1, 0)
    column = jnp.concatenate([far, fy_up, fy_dn, fy_low, fy_high], 0)
    add(column, far_block(0))
    add(fetch(y_dn, -1, 0), near_block(2, (0,)))
    c_up = fetch(column, 0, 1)
    c_dn = fetch(column, 0, -1)
    add(c_up, far_block(1))
    add(c_dn, far_block(-1))
    up = jnp.concatenate([z_up, z_up2], 0)
    dn = jnp.concatenate([z_dn, z_dn2], 0)
    z_up3 = fetch(z_up2, 0, 1)
    z_dn3 = fetch(z_dn2, 0, -1)
    add(up, near_block(0, (1, 2)))
    add(dn, near_block(0, (-1, -2)))
    up_u, up_d = fetch(up, 1, 0), fetch(up, -1, 0)
    dn_u, dn_d = fetch(dn, 1, 0), fetch(dn, -1, 0)
    add(up_u, near_block(1, (1, 2)))
    add(up_d, near_block(-1, (1, 2)))
    add(dn_u, near_block(1, (-1, -2)))
    add(dn_d, near_block(-1, (-1, -2)))
    z_low = fetch(z_up3[: a // 2], 0, 1)
    z_high = fetch(z_dn3[a // 2 :], 0, -1)
    c_up2 = fetch(c_up, 0, 1)
    c_dn2 = fetch(c_dn, 0, -1)
    add(c_up2, far_block(2))
    add(c_dn2, far_block(-2))
    add(fetch(up_u, 1, 0), near_block(2, (1, 2)))
    add(fetch(dn_d, -1, 0), near_block(2, (-1, -2)))
    up = jnp.concatenate([z_up3, z_low, z_high], 0)
    dn = z_dn3
    add(up, near_block(0, (3, 4)))
    add(dn, near_block(0, (-3,)))
    up_u, up_d = fetch(up, 1, 0), fetch(up, -1, 0)
    dn_u, dn_d = fetch(dn, 1, 0), fetch(dn, -1, 0)
    add(up_u, near_block(1, (3, 4)))
    add(up_d, near_block(-1, (3, 4)))
    add(dn_u, near_block(1, (-3,)))
    add(dn_d, near_block(-1, (-3,)))
    c_up3 = fetch(c_up2, 0, 1)
    c_dn3 = fetch(c_dn2, 0, -1)
    add(c_up3, far_block(3))
    add(c_dn3, far_block(-3))
    add(fetch(up_u, 1, 0), near_block(2, (3, 4)))
    add(fetch(dn_d, -1, 0), near_block(2, (-3,)))
    c_low = fetch(c_up3[: 2 * b], 0, 1)
    c_high = fetch(c_dn3[2 * b :], 0, -1)
    add(c_low, [(b, dy, 4, a) for dy in (0, 1)])
    add(c_high, [(b, dy, 4, a) for dy in (-1, 2)])
    return pieces, tuple(plan)


def reduce_ring(keep, give, ring):
    got = swap_cores(give, ring)
    rows = keep.shape[1]
    half = rows // 32 * 16

    def both(at, rows_from, rows_to):
        return keep[at, rows_from:rows_to].astype(F32) + got[at, rows_from:rows_to].astype(F32)

    low = fetch_x(both(2, 0, half).astype(BF), -1, ring)
    high = fetch_x(both(2, half, rows).astype(BF), 1, ring)
    up = jnp.concatenate(
        [both(1, 0, half) + low.astype(F32), both(1, half, rows)], 0
    ).astype(BF)
    dn = jnp.concatenate(
        [both(3, 0, half), both(3, half, rows) + high.astype(F32)], 0
    ).astype(BF)
    return keep, got, fetch_x(up, -1, ring), fetch_x(dn, 1, ring)


def shards(
    activations,
    action_codes,
    norm_gain,
    action_scale,
    action_shift,
    qkv_weight,
    qk_gains,
    out_weight,
    grad_output,
):
    replicas = lax.axis_size("replica")
    shards_tm = lax.axis_size("tm")
    parts = lax.axis_size("tensor")
    ring = replicas * parts // CORES
    rep = lax.axis_index("replica")
    part = lax.axis_index("tensor")
    spot = lax.axis_index("tm")
    frames = action_codes.shape[1]
    quarter = activations.shape[2]
    patches = activations.shape[1]
    patch_dev = patches // shards_tm
    depth = qkv_weight.shape[0]
    heads = qkv_weight.shape[1] // replicas
    triple = qkv_weight.shape[2]
    width = triple // 3
    wide = heads * triple
    narrow = heads * width
    code_count = action_scale.shape[0]
    group = shards_tm * patch_dev
    tokens = replicas * group
    near = depth // 8 * 5
    place = jnp.stack(
        [
            rep,
            part,
            spot // NZ,
            spot % NZ,
            rep * (ring // replicas) + part // CORES,
            part % CORES,
        ]
    ).astype(jnp.int32)

    both, weight_near, weight_far = pl.pallas_call(
        functools.partial(pack_kernel, patch_dev),
        out_shape=(
            jax.ShapeDtypeStruct((2 * patches, quarter), BF),
            jax.ShapeDtypeStruct((near, wide + narrow), BF),
            jax.ShapeDtypeStruct((depth - near, wide + narrow), BF),
        ),
        in_specs=[SMEM] + [VMEM] * 4,
        out_specs=(VMEM, VMEM, VMEM),
        compiler_params=pltpu.CompilerParams(vmem_limit_bytes=24 * 1024 * 1024),
        name="pack",
    )(
        place,
        activations.reshape(patches, quarter),
        grad_output.reshape(patches, quarter),
        qkv_weight.reshape(-1, triple),
        out_weight,
    )
    pieces, plan = gather_weight(weight_near, weight_far)

    both = lax.all_to_all(both, "tm", split_axis=0, concat_axis=0, tiled=True)
    full = lax.all_gather(both, ("replica", "tensor"), axis=0)
    full = full.reshape(replicas, parts, 2 * group, quarter)

    other = lax.ppermute(action_codes, "replica", [(i, 1 - i) for i in range(2)])
    codes = jnp.where(
        rep == 0,
        jnp.concatenate([action_codes, other], 0),
        jnp.concatenate([other, action_codes], 0),
    ).reshape(-1)
    codes = jnp.repeat(codes, patch_dev)
    code_range = jnp.arange(code_count)
    hot = (codes[:, None] == code_range[None, :]).astype(BF)
    hot_t = (codes[None, :] == code_range[:, None]).astype(BF)

    def by_part(table):
        return table.reshape(table.shape[0], parts, quarter).transpose(1, 0, 2)

    big = jax.ShapeDtypeStruct((parts, tokens, quarter), BF)
    big_spec = pl.BlockSpec((parts, group, quarter), lambda i: (0, i, 0))
    own_spec = pl.BlockSpec((group, quarter), lambda i: (0, 0))

    def whole(*shape):
        return pl.BlockSpec(shape, lambda i: (0,) * len(shape))

    hidden, grad, normed, scaled, coef, xinv, x_own, g_own = pl.pallas_call(
        functools.partial(prep_kernel, patch_dev),
        grid=(replicas,),
        out_shape=(big, big, big, big)
        + (jax.ShapeDtypeStruct((group, quarter), F32),) * 2
        + (jax.ShapeDtypeStruct((group, quarter), BF),) * 2,
        in_specs=[
            SMEM,
            pl.BlockSpec((1, parts, 2 * group, quarter), lambda i: (i, 0, 0, 0)),
            pl.BlockSpec((group, code_count), lambda i: (i, 0)),
            whole(parts, 1, quarter),
            whole(parts, code_count, quarter),
            whole(parts, code_count, quarter),
        ],
        out_specs=(big_spec,) * 4 + (own_spec,) * 4,
        compiler_params=pltpu.CompilerParams(vmem_limit_bytes=48 * 1024 * 1024),
        name="prep",
    )(
        place,
        full,
        hot,
        by_part(norm_gain[None]),
        by_part(action_scale),
        by_part(action_shift),
    )

    tail_rows = group + EXTRA
    y_shape = jax.ShapeDtypeStruct((ring, group, quarter), BF)
    dh_shape = jax.ShapeDtypeStruct((ring, tail_rows, quarter), BF)
    flops = 4 * tokens * parts * quarter * (wide + narrow)
    moved = 2 * parts * quarter * (wide + narrow + 6 * tokens)
    y_keep, y_give, dh_keep, dh_give = pl.pallas_call(
        functools.partial(block_kernel, patch_dev, frames, plan),
        out_shape=(y_shape, y_shape, dh_shape, dh_shape),
        in_specs=[SMEM, VMEM, VMEM] + [ANY] * (4 + len(pieces)),
        out_specs=(ANY,) * 4,
        scratch_shapes=[
            pltpu.VMEM((parts, tokens, quarter), BF),
            pltpu.VMEM((parts, tokens, quarter), BF),
            pltpu.VMEM((parts, tokens, quarter), BF),
            pltpu.VMEM((parts, tokens, quarter), BF),
            pltpu.VMEM((parts * quarter, wide + narrow), BF),
            pltpu.VMEM((tokens, wide), F32),
            pltpu.VMEM((tokens, narrow), F32),
            pltpu.VMEM((tokens, narrow), BF),
            pltpu.VMEM((tokens, wide), BF),
            pltpu.VMEM((CORES, ring, group, quarter), BF),
            pltpu.VMEM((CORES, ring, tail_rows, quarter), BF),
            pltpu.SemaphoreType.DMA((parts, 4)),
            pltpu.SemaphoreType.DMA((len(plan),)),
            pltpu.SemaphoreType.DMA((2, ring, CORES)),
        ],
        compiler_params=pltpu.CompilerParams(vmem_limit_bytes=52 * 1024 * 1024),
        cost_estimate=pl.CostEstimate(flops=flops, bytes_accessed=moved, transcendentals=0),
        name="block",
    )(place, qk_gains, hot_t, hidden, grad, normed, scaled, *pieces)

    dh_terms = reduce_ring(dh_keep, dh_give, ring)
    y_terms = reduce_ring(y_keep, y_give, ring)
    first_y = pl.BlockSpec((1, group, quarter), lambda i: (0, 0, 0))
    first_dh = pl.BlockSpec((1, tail_rows, quarter), lambda i: (0, 0, 0))
    span = 2 * patch_dev + code_count
    send = pl.pallas_call(
        functools.partial(finish_kernel, patch_dev, code_count, parts),
        grid=(1,),
        out_shape=jax.ShapeDtypeStruct((shards_tm * span, quarter), BF),
        in_specs=[first_y] * 2
        + [whole(group, quarter)] * 2
        + [first_dh] * 2
        + [whole(tail_rows, quarter)] * 2
        + [whole(group, quarter)] * 4,
        out_specs=whole(shards_tm * span, quarter),
        compiler_params=pltpu.CompilerParams(vmem_limit_bytes=24 * 1024 * 1024),
        name="finish",
    )(*y_terms, *dh_terms, coef, xinv, x_own, g_own)
    back = lax.all_to_all(send, "tm", split_axis=0, concat_axis=0, tiled=True)
    token_total = tokens * shards_tm
    y_frames, dx_frames, grad_mine = pl.pallas_call(
        functools.partial(unpack_kernel, patch_dev, token_total ** (-0.5)),
        out_shape=(
            jax.ShapeDtypeStruct((group, quarter), BF),
            jax.ShapeDtypeStruct((group, quarter), BF),
            jax.ShapeDtypeStruct((code_count, quarter), F32),
        ),
        in_specs=[VMEM],
        out_specs=(VMEM, VMEM, VMEM),
        compiler_params=pltpu.CompilerParams(vmem_limit_bytes=24 * 1024 * 1024),
        name="unpack",
    )(back)
    grad_other = lax.ppermute(grad_mine, "replica", [(i, 1 - i) for i in range(2)])
    d_scale = jnp.where(rep == 0, grad_mine, grad_other)
    d_shift = jnp.where(rep == 0, grad_other, grad_mine)
    return (y_frames[None], dx_frames[None], d_scale, d_shift)


def solution(mesh):
    placed = (
        P(("replica", "tm"), None, "tensor"),
        P("replica", None),
        P(),
        P(),
        P(),
        P("tm", "tensor", None),
        P(),
        P("tensor", None, "tm"),
        P(("replica", "tm"), None, "tensor"),
    )
    return jax.shard_map(
        shards,
        mesh=mesh,
        in_specs=placed,
        out_specs=(
            P(("replica", "tm"), None, "tensor"),
            P(("replica", "tm"), None, "tensor"),
            P(None, "tensor"),
            P(None, "tensor"),
        ),
        check_vma=False,
    )
```

```python
import functools

import jax
import jax.numpy as jnp
from jax import lax
from jax.experimental import pallas as pl
from jax.experimental.pallas import tpu as pltpu
from jax.sharding import PartitionSpec as P

EPS = 1e-06
BF = jnp.bfloat16
F32 = jnp.float32
EXTRA = 16


def dot_nn(a, b):
    return lax.dot_general(a, b, (((1,), (0,)), ((), ())), preferred_element_type=F32)


def dot_nt(a, b):
    return lax.dot_general(a, b, (((1,), (1,)), ((), ())), preferred_element_type=F32)


def dot_tn(a, b):
    return lax.dot_general(a, b, (((0,), (0,)), ((), ())), preferred_element_type=F32)


def halves(value):
    high = value.astype(BF)
    return high, (value - high.astype(F32)).astype(BF)


def selector(shape, pick):
    row = lax.broadcasted_iota(jnp.int32, shape, 0)
    col = lax.broadcasted_iota(jnp.int32, shape, 1)
    return jnp.where(pick(row, col), 1.0, 0.0).astype(BF)


def pack_kernel(patch_dev, place_ref, x_ref, g_ref, qkv_ref, out_ref, both_ref, near_ref, far_ref):
    rows = x_ref.shape[0]
    pair = 2 * patch_dev
    pick_x = selector(
        (2 * rows, rows),
        lambda m, n: (m % pair < patch_dev) & (m // pair * patch_dev + m % pair == n),
    )
    pick_g = selector(
        (2 * rows, rows),
        lambda m, n: (m % pair >= patch_dev)
        & (m // pair * patch_dev + m % pair - patch_dev == n),
    )
    both_ref[...] = (dot_nn(pick_x, x_ref[...]) + dot_nn(pick_g, g_ref[...])).astype(BF)
    depth = near_ref.shape[0] + far_ref.shape[0]
    near = near_ref.shape[0]
    all_heads = qkv_ref.shape[0] // depth
    heads = out_ref.shape[0] // 2
    triple = qkv_ref.shape[1]
    width = triple // 3
    rep = place_ref[0]
    for head in range(heads):
        own = rep * heads + head
        pick = selector(
            (depth, all_heads * depth),
            lambda m, n: m * all_heads + own == n,
        )
        part = dot_nn(pick, qkv_ref[...]).astype(BF)
        cols = slice(head * triple, (head + 1) * triple)
        near_ref[:, cols] = part[:near]
        far_ref[:, cols] = part[near:]
        eye = selector((depth, depth), lambda m, n: m == n)
        part = dot_nt(eye, out_ref[own]).astype(BF)
        cols = slice(heads * triple + head * width, heads * triple + (head + 1) * width)
        near_ref[:, cols] = part[:near]
        far_ref[:, cols] = part[near:]


def prep_kernel(
    patch_dev,
    place_ref,
    full_ref,
    hot_ref,
    gain_ref,
    scale_ref,
    shift_ref,
    hidden_ref,
    grad_ref,
    normed_ref,
    scaled_ref,
    coef_ref,
    xinv_ref,
    xown_ref,
    gown_ref,
):
    parts = full_ref.shape[1]
    group = hidden_ref.shape[1]
    quarter = full_ref.shape[3]
    pair = 2 * patch_dev
    pick_x = selector(
        (group, 2 * group), lambda m, n: m // patch_dev * pair + m % patch_dev == n
    )
    pick_g = selector(
        (group, 2 * group), lambda m, n: m // patch_dev * pair + m % patch_dev + patch_dev == n
    )
    hot = hot_ref[...]

    def rows_of(table):
        high, low = halves(table)
        return dot_nn(hot, high) + dot_nn(hot, low)

    square = jnp.zeros((group, 1), F32)
    for part in range(parts):
        x = dot_nn(pick_x, full_ref[0, part])
        square += jnp.sum(x * x, -1, keepdims=True)
    inverse = lax.rsqrt(square / (parts * quarter) + EPS)
    for part in range(parts):
        x = dot_nn(pick_x, full_ref[0, part])
        normed = x * inverse * gain_ref[part]
        scaled = normed * (1.0 + rows_of(scale_ref[part]))
        hidden_ref[part] = (scaled + rows_of(shift_ref[part])).astype(BF)
        normed_ref[part] = normed.astype(BF)
        scaled_ref[part] = scaled.astype(BF)
        grad_ref[part] = dot_nn(pick_g, full_ref[0, part]).astype(BF)

    @pl.when(pl.program_id(0) == place_ref[0])
    def _():
        own = place_ref[1]
        rows = full_ref[0, own]
        x = dot_nn(pick_x, rows)
        xown_ref[...] = x.astype(BF)
        gown_ref[...] = dot_nn(pick_g, rows).astype(BF)
        coef_ref[...] = inverse * (1.0 + rows_of(scale_ref[own])) * gain_ref[own]
        xinv_ref[...] = x * inverse * inverse


def block_kernel(
    patch_dev,
    frames,
    plan,
    place_ref,
    gains_ref,
    hot_ref,
    hidden_hbm,
    grad_hbm,
    normed_hbm,
    scaled_hbm,
    *refs,
):
    count = 1 + max(item[0] for item in plan)
    pieces = refs[:count]
    (
        y_keep,
        y_give,
        dh_keep,
        dh_give,
        hidden,
        grad,
        normed,
        scaled,
        weight,
        qkv_acc,
        da_acc,
        attended,
        dqkv,
        y_stage,
        dh_stage,
        sems,
        weight_sems,
        out_sems,
    ) = refs[count:]
    parts, tokens, quarter = hidden.shape
    width = gains_ref.shape[1]
    wide = qkv_acc.shape[1]
    heads = wide // (3 * width)
    cores, ring, group, _ = y_stage.shape
    replicas = tokens // group
    along = ring // replicas
    rows_y = place_ref[2]
    rows_z = place_ref[3]
    spot_x = place_ref[4]
    core = place_ref[5]
    depth = weight.shape[0] // (NY * NZ)

    def inputs(at):
        part = at
        result = [
            pltpu.make_async_copy(hidden_hbm.at[part], hidden.at[part], sems.at[at, 0]),
            pltpu.make_async_copy(grad_hbm.at[part], grad.at[part], sems.at[at, 1]),
        ]
        return result

    def weights_in(at):
        result = []
        for number, (index, start, size, y, z, relative, place) in enumerate(plan):
            if (at == NY) if relative else (y == at):
                owner = y * NZ + (rows_z + z) % NZ if relative else (rows_y + y) % NY * NZ + z
                target = pl.multiple_of(owner * depth + place, 16)
                result.append(
                    pltpu.make_async_copy(
                        pieces[index].at[pl.ds(start, size)],
                        weight.at[pl.ds(target, size)],
                        weight_sems.at[number],
                    )
                )
        return result

    def second(part):
        return [
            pltpu.make_async_copy(normed_hbm.at[part], normed.at[part], sems.at[part, 2]),
            pltpu.make_async_copy(scaled_hbm.at[part], scaled.at[part], sems.at[part, 3]),
        ]

    for copy in weights_in(NY):
        copy.start()
    for at in range(NY):
        for copy in inputs(at) + weights_in(at):
            copy.start()
    for part in range(parts):
        for copy in second(part):
            copy.start()

    qkv_acc[...] = jnp.zeros_like(qkv_acc)
    da_acc[...] = jnp.zeros_like(da_acc)
    for at in range(NY):
        for copy in inputs(at):
            copy.wait()
    for copy in weights_in(NY):
        copy.wait()
    for at in range(NY):
        for copy in weights_in(at):
            copy.wait()
        part = (rows_y + at) % NY
        rows = pl.ds(pl.multiple_of(part * quarter, quarter), quarter)
        qkv_acc[...] += dot_nn(hidden[part], weight[rows, :wide])
        da_acc[...] += dot_nn(grad[part], weight[rows, wide:])

    gain_q = gains_ref[0:1, :]
    gain_k = gains_ref[1:2, :]
    row = lax.broadcasted_iota(jnp.int32, (group, group), 0)
    col = lax.broadcasted_iota(jnp.int32, (group, group), 1)
    clip_tokens = frames * patch_dev
    mask = (
        (row % patch_dev == col % patch_dev)
        & (row // clip_tokens == col // clip_tokens)
        & (col <= row)
    )
    factor = width ** (-0.5)
    for rep in range(replicas):
        rows = slice(rep * group, (rep + 1) * group)
        for head in range(heads):
            base = head * 3 * width
            take = lambda at: qkv_acc[rows, base + at * width : base + (at + 1) * width].astype(
                BF
            )
            q = take(0).astype(F32)
            k = take(1).astype(F32)
            value = take(2)
            d_out = da_acc[rows, head * width : (head + 1) * width].astype(BF)
            inv_q = lax.rsqrt(jnp.mean(q * q, -1, keepdims=True) + EPS)
            inv_k = lax.rsqrt(jnp.mean(k * k, -1, keepdims=True) + EPS)
            q_hat = q * inv_q
            k_hat = k * inv_k
            queries = (q_hat * gain_q).astype(BF)
            keys = (k_hat * gain_k).astype(BF)
            scores = dot_nt(queries, keys) * factor
            weights = jnp.where(mask, jnp.exp(scores), 0.0)
            probs = weights / jnp.sum(weights, -1, keepdims=True)
            probs_bf = probs.astype(BF)
            out = dot_nn(probs_bf, value)
            attended[rows, head * width : (head + 1) * width] = out.astype(BF)
            d_value = dot_tn(probs_bf, d_out)
            d_probs = dot_nt(d_out, value)
            d_scores = probs * (d_probs - jnp.sum(d_probs * probs, -1, keepdims=True))
            d_scores = (d_scores * factor).astype(BF)
            d_q = dot_nn(d_scores, keys) * gain_q
            d_k = dot_tn(d_scores, queries) * gain_k
            d_q = inv_q * (d_q - q_hat * jnp.mean(d_q * q_hat, -1, keepdims=True))
            d_k = inv_k * (d_k - k_hat * jnp.mean(d_k * k_hat, -1, keepdims=True))
            for at, item in enumerate((d_q, d_k, d_value)):
                dqkv[rows, base + at * width : base + (at + 1) * width] = item.astype(BF)

    def outputs(stage, keep, give, base):
        result = []
        for step in range(ring):
            target = (spot_x + step) % ring
            for side, out in enumerate((keep, give)):
                result.append(
                    pltpu.make_async_copy(
                        stage.at[(core + side) % cores, target],
                        out.at[step],
                        out_sems.at[base, step, side],
                    )
                )
        return result

    block = min(quarter, 256)
    for part in range(parts):
        for at in range(quarter // block):
            cols = slice(at * block, (at + 1) * block)
            w_block = weight[part * quarter + at * block : part * quarter + (at + 1) * block, wide:]
            y_block = dot_nt(attended[...], w_block).astype(BF)
            for rep in range(replicas):
                rows = slice(rep * group, (rep + 1) * group)
                y_stage[part % cores, rep * along + part // cores, :, cols] = y_block[rows]
    y_copies = outputs(y_stage, y_keep, y_give, 0)
    for copy in y_copies:
        copy.start()

    for part in range(parts):
        for copy in second(part):
            copy.wait()
    hot = hot_ref[...]
    codes = hot.shape[0]
    tail = dh_stage.shape[2] - group
    lanes = min(block, 128)
    terms = jnp.zeros((tokens, lanes), F32)
    for part in range(parts):
        for at in range(quarter // block):
            cols = slice(at * block, (at + 1) * block)
            w_block = weight[part * quarter + at * block : part * quarter + (at + 1) * block, :wide]
            d_block = dot_nt(dqkv[...], w_block)
            d_rounded = d_block.astype(BF)
            d_scale = dot_nn(hot, (d_block * normed[part, :, cols].astype(F32)).astype(BF))
            d_shift = dot_nn(hot, d_rounded)
            for rep, item in enumerate((d_scale, d_shift)):
                where = (part % cores, rep * along + part // cores)
                rows = slice(rep * group, (rep + 1) * group)
                dh_stage[where[0], where[1], 0:group, cols] = d_rounded[rows]
                dh_stage[where[0], where[1], group : group + codes, cols] = item.astype(BF)
            product = d_block * scaled[part, :, cols].astype(F32)
            for lane in range(block // lanes):
                terms += product[:, lane * lanes : (lane + 1) * lanes]
    ones = jnp.ones((8, lanes), BF)
    high, low = halves(terms)
    high, low = halves(dot_nt(ones, high) + dot_nt(ones, low))
    sub = lax.broadcasted_iota(jnp.int32, (8, group), 0)
    for rep in range(replicas):
        mine = slice(rep * group, (rep + 1) * group)
        both = jnp.where(
            sub == 0,
            high[:, mine].astype(F32),
            jnp.where(sub == 1, low[:, mine].astype(F32), 0.0),
        ).astype(BF)
        for part in range(parts):
            where = (part % cores, rep * along + part // cores)
            dh_stage[where[0], where[1], group + codes :, :] = jnp.zeros(
                (tail - codes, quarter), BF
            )
            dh_stage[where[0], where[1], group + codes : group + codes + 8, 0:group] = both
    dh_copies = outputs(dh_stage, dh_keep, dh_give, 1)
    for copy in dh_copies:
        copy.start()
    for copy in y_copies + dh_copies:
        copy.wait()


def finish_kernel(
    patch_dev,
    code_count,
    parts,
    yk_ref,
    yr_ref,
    ya_ref,
    yb_ref,
    dk_ref,
    dr_ref,
    da_ref,
    db_ref,
    coef_ref,
    xinv_ref,
    xown_ref,
    gown_ref,
    send_ref,
):
    group, quarter = xown_ref.shape
    y = (
        xown_ref[...].astype(F32)
        + (yk_ref[0].astype(F32) + yr_ref[0].astype(F32))
        + (ya_ref[...].astype(F32) + yb_ref[...].astype(F32))
    )
    total = (dk_ref[0].astype(F32) + dr_ref[0].astype(F32)) + (
        da_ref[...].astype(F32) + db_ref[...].astype(F32)
    )
    terms = total[group + code_count : group + code_count + 8, :group]
    term = (terms[0:1] + terms[1:2]) / (quarter * parts)
    term = jnp.broadcast_to(term, (group, group)).T[:, 0:1]
    dx = gown_ref[...].astype(F32) + (total[:group] * coef_ref[...] - xinv_ref[...] * term)
    grads = total[group : group + code_count].astype(BF)
    span = 2 * patch_dev + code_count
    rows = send_ref.shape[0]
    pick_y = selector(
        (rows, group),
        lambda m, n: (m % span < patch_dev) & (m // span * patch_dev + m % span == n),
    )
    pick_d = selector(
        (rows, group),
        lambda m, n: (m % span >= patch_dev)
        & (m % span < 2 * patch_dev)
        & (m // span * patch_dev + m % span - patch_dev == n),
    )
    pick_g = selector((rows, code_count), lambda m, n: m % span - 2 * patch_dev == n)
    send_ref[...] = (
        dot_nn(pick_y, y.astype(BF)) + dot_nn(pick_d, dx.astype(BF)) + dot_nn(pick_g, grads)
    ).astype(BF)


def unpack_kernel(patch_dev, factor, back_ref, y_ref, dx_ref, sum_ref):
    group = y_ref.shape[0]
    rows = back_ref.shape[0]
    codes = sum_ref.shape[0]
    span = 2 * patch_dev + codes
    back = back_ref[...]
    pick_y = selector((group, rows), lambda m, n: m // patch_dev * span + m % patch_dev == n)
    pick_d = selector(
        (group, rows), lambda m, n: m // patch_dev * span + m % patch_dev + patch_dev == n
    )
    pick_g = selector((codes, rows), lambda m, n: n % span - 2 * patch_dev == m)
    y_ref[...] = dot_nn(pick_y, back).astype(BF)
    dx_ref[...] = dot_nn(pick_d, back).astype(BF)
    sum_ref[...] = dot_nn(pick_g, back) * factor


NY = 4
NZ = 8
CORES = 2
VMEM = pl.BlockSpec(memory_space=pltpu.VMEM)
SMEM = pl.BlockSpec(memory_space=pltpu.SMEM)
ANY = pl.BlockSpec(memory_space=pl.ANY)


def fetch(value, dy, dz):
    pairs = []
    for y in range(NY):
        for z in range(NZ):
            pairs.append((((y + dy) % NY) * NZ + (z + dz) % NZ, y * NZ + z))
    return lax.ppermute(value, "tm", pairs)


def fetch_x(value, dx, ring):
    pairs = []
    for x in range(ring):
        for core in range(CORES):
            pairs.append((((x + dx) % ring) * CORES + core, x * CORES + core))
    return lax.ppermute(value, ("replica", "tensor"), pairs)


def swap_cores(value, ring):
    pairs = []
    for x in range(ring):
        for core in range(CORES):
            pairs.append((x * CORES + core, x * CORES + 1 - core))
    return lax.ppermute(value, ("replica", "tensor"), pairs)


def gather_weight(near, far):
    a = near.shape[0]
    b = far.shape[0]
    pieces = []
    plan = []

    def add(value, blocks):
        start = 0
        for size, dy, z, relative, place in blocks:
            plan.append((len(pieces), start, size, dy % NY, z % NZ, relative, place))
            start += size
        pieces.append(value)

    def line(dy, zs):
        return [(a, dy, z, False, 0) for z in zs]

    def column(dz, ys=range(NY)):
        return [(b, y, dz, True, a) for y in ys]

    along_z = [[y * NZ + z for z in range(NZ)] for y in range(NY)]
    along_y = [[y * NZ + z for y in range(NY)] for z in range(NZ)]
    low, high = range(NZ // 2), range(NZ // 2, NZ)
    rows = lax.all_gather(near, "tm", axis_index_groups=along_z, axis=0, tiled=True)
    cols = lax.all_gather(far, "tm", axis_index_groups=along_y, axis=0, tiled=True)
    half = NZ // 2 * a
    first, last = rows[:half], rows[half:]
    add(rows, line(0, range(NZ)))
    up_first, dn_first = fetch(first, 1, 0), fetch(first, -1, 0)
    up_last, dn_last = fetch(last, 1, 0), fetch(last, -1, 0)
    add(up_first, line(1, low))
    add(up_last, line(1, high))
    add(dn_first, line(-1, low))
    add(dn_last, line(-1, high))
    add(fetch(up_first, 1, 0), line(2, low))
    add(fetch(dn_last, -1, 0), line(2, high))

    add(cols, column(0))
    up, dn = cols, cols
    for hop in range(1, NZ // 2):
        up, dn = fetch(up, 0, 1), fetch(dn, 0, -1)
        add(up, column(hop))
        add(dn, column(-hop))
    add(fetch(up[: 2 * b], 0, 1), column(NZ // 2, (0, 1)))
    add(fetch(dn[2 * b :], 0, -1), column(NZ // 2, (2, 3)))
    return pieces, tuple(plan)


def reduce_ring(keep, give, ring):
    got = swap_cores(give, ring)
    rows = keep.shape[1]
    half = rows // 32 * 16

    def both(at, rows_from, rows_to):
        return keep[at, rows_from:rows_to].astype(F32) + got[at, rows_from:rows_to].astype(F32)

    low = fetch_x(both(2, 0, half).astype(BF), -1, ring)
    high = fetch_x(both(2, half, rows).astype(BF), 1, ring)
    up = jnp.concatenate(
        [both(1, 0, half) + low.astype(F32), both(1, half, rows)], 0
    ).astype(BF)
    dn = jnp.concatenate(
        [both(3, 0, half), both(3, half, rows) + high.astype(F32)], 0
    ).astype(BF)
    return keep, got, fetch_x(up, -1, ring), fetch_x(dn, 1, ring)


def shards(
    activations,
    action_codes,
    norm_gain,
    action_scale,
    action_shift,
    qkv_weight,
    qk_gains,
    out_weight,
    grad_output,
):
    replicas = lax.axis_size("replica")
    shards_tm = lax.axis_size("tm")
    parts = lax.axis_size("tensor")
    ring = replicas * parts // CORES
    rep = lax.axis_index("replica")
    part = lax.axis_index("tensor")
    spot = lax.axis_index("tm")
    frames = action_codes.shape[1]
    quarter = activations.shape[2]
    patches = activations.shape[1]
    patch_dev = patches // shards_tm
    depth = qkv_weight.shape[0]
    heads = qkv_weight.shape[1] // replicas
    triple = qkv_weight.shape[2]
    width = triple // 3
    wide = heads * triple
    narrow = heads * width
    code_count = action_scale.shape[0]
    group = shards_tm * patch_dev
    tokens = replicas * group
    near = depth // 8 * 5
    place = jnp.stack(
        [
            rep,
            part,
            spot // NZ,
            spot % NZ,
            rep * (ring // replicas) + part // CORES,
            part % CORES,
        ]
    ).astype(jnp.int32)

    both, weight_near, weight_far = pl.pallas_call(
        functools.partial(pack_kernel, patch_dev),
        out_shape=(
            jax.ShapeDtypeStruct((2 * patches, quarter), BF),
            jax.ShapeDtypeStruct((near, wide + narrow), BF),
            jax.ShapeDtypeStruct((depth - near, wide + narrow), BF),
        ),
        in_specs=[SMEM] + [VMEM] * 4,
        out_specs=(VMEM, VMEM, VMEM),
        compiler_params=pltpu.CompilerParams(vmem_limit_bytes=24 * 1024 * 1024),
        name="pack",
    )(
        place,
        activations.reshape(patches, quarter),
        grad_output.reshape(patches, quarter),
        qkv_weight.reshape(-1, triple),
        out_weight,
    )
    pieces, plan = gather_weight(weight_near, weight_far)

    both = lax.all_to_all(both, "tm", split_axis=0, concat_axis=0, tiled=True)
    full = lax.all_gather(both, ("replica", "tensor"), axis=0)
    full = full.reshape(replicas, parts, 2 * group, quarter)

    other = lax.ppermute(action_codes, "replica", [(i, 1 - i) for i in range(2)])
    codes = jnp.where(
        rep == 0,
        jnp.concatenate([action_codes, other], 0),
        jnp.concatenate([other, action_codes], 0),
    ).reshape(-1)
    codes = jnp.repeat(codes, patch_dev)
    code_range = jnp.arange(code_count)
    hot = (codes[:, None] == code_range[None, :]).astype(BF)
    hot_t = (codes[None, :] == code_range[:, None]).astype(BF)

    def by_part(table):
        return table.reshape(table.shape[0], parts, quarter).transpose(1, 0, 2)

    big = jax.ShapeDtypeStruct((parts, tokens, quarter), BF)
    big_spec = pl.BlockSpec((parts, group, quarter), lambda i: (0, i, 0))
    own_spec = pl.BlockSpec((group, quarter), lambda i: (0, 0))

    def whole(*shape):
        return pl.BlockSpec(shape, lambda i: (0,) * len(shape))

    hidden, grad, normed, scaled, coef, xinv, x_own, g_own = pl.pallas_call(
        functools.partial(prep_kernel, patch_dev),
        grid=(replicas,),
        out_shape=(big, big, big, big)
        + (jax.ShapeDtypeStruct((group, quarter), F32),) * 2
        + (jax.ShapeDtypeStruct((group, quarter), BF),) * 2,
        in_specs=[
            SMEM,
            pl.BlockSpec((1, parts, 2 * group, quarter), lambda i: (i, 0, 0, 0)),
            pl.BlockSpec((group, code_count), lambda i: (i, 0)),
            whole(parts, 1, quarter),
            whole(parts, code_count, quarter),
            whole(parts, code_count, quarter),
        ],
        out_specs=(big_spec,) * 4 + (own_spec,) * 4,
        compiler_params=pltpu.CompilerParams(vmem_limit_bytes=48 * 1024 * 1024),
        name="prep",
    )(
        place,
        full,
        hot,
        by_part(norm_gain[None]),
        by_part(action_scale),
        by_part(action_shift),
    )

    tail_rows = group + EXTRA
    y_shape = jax.ShapeDtypeStruct((ring, group, quarter), BF)
    dh_shape = jax.ShapeDtypeStruct((ring, tail_rows, quarter), BF)
    flops = 4 * tokens * parts * quarter * (wide + narrow)
    moved = 2 * parts * quarter * (wide + narrow + 6 * tokens)
    y_keep, y_give, dh_keep, dh_give = pl.pallas_call(
        functools.partial(block_kernel, patch_dev, frames, plan),
        out_shape=(y_shape, y_shape, dh_shape, dh_shape),
        in_specs=[SMEM, VMEM, VMEM] + [ANY] * (4 + len(pieces)),
        out_specs=(ANY,) * 4,
        scratch_shapes=[
            pltpu.VMEM((parts, tokens, quarter), BF),
            pltpu.VMEM((parts, tokens, quarter), BF),
            pltpu.VMEM((parts, tokens, quarter), BF),
            pltpu.VMEM((parts, tokens, quarter), BF),
            pltpu.VMEM((parts * quarter, wide + narrow), BF),
            pltpu.VMEM((tokens, wide), F32),
            pltpu.VMEM((tokens, narrow), F32),
            pltpu.VMEM((tokens, narrow), BF),
            pltpu.VMEM((tokens, wide), BF),
            pltpu.VMEM((CORES, ring, group, quarter), BF),
            pltpu.VMEM((CORES, ring, tail_rows, quarter), BF),
            pltpu.SemaphoreType.DMA((parts, 4)),
            pltpu.SemaphoreType.DMA((len(plan),)),
            pltpu.SemaphoreType.DMA((2, ring, CORES)),
        ],
        compiler_params=pltpu.CompilerParams(vmem_limit_bytes=52 * 1024 * 1024),
        cost_estimate=pl.CostEstimate(flops=flops, bytes_accessed=moved, transcendentals=0),
        name="block",
    )(place, qk_gains, hot_t, hidden, grad, normed, scaled, *pieces)

    dh_terms = reduce_ring(dh_keep, dh_give, ring)
    y_terms = reduce_ring(y_keep, y_give, ring)
    first_y = pl.BlockSpec((1, group, quarter), lambda i: (0, 0, 0))
    first_dh = pl.BlockSpec((1, tail_rows, quarter), lambda i: (0, 0, 0))
    span = 2 * patch_dev + code_count
    send = pl.pallas_call(
        functools.partial(finish_kernel, patch_dev, code_count, parts),
        grid=(1,),
        out_shape=jax.ShapeDtypeStruct((shards_tm * span, quarter), BF),
        in_specs=[first_y] * 2
        + [whole(group, quarter)] * 2
        + [first_dh] * 2
        + [whole(tail_rows, quarter)] * 2
        + [whole(group, quarter)] * 4,
        out_specs=whole(shards_tm * span, quarter),
        compiler_params=pltpu.CompilerParams(vmem_limit_bytes=24 * 1024 * 1024),
        name="finish",
    )(*y_terms, *dh_terms, coef, xinv, x_own, g_own)
    back = lax.all_to_all(send, "tm", split_axis=0, concat_axis=0, tiled=True)
    token_total = tokens * shards_tm
    y_frames, dx_frames, grad_mine = pl.pallas_call(
        functools.partial(unpack_kernel, patch_dev, token_total ** (-0.5)),
        out_shape=(
            jax.ShapeDtypeStruct((group, quarter), BF),
            jax.ShapeDtypeStruct((group, quarter), BF),
            jax.ShapeDtypeStruct((code_count, quarter), F32),
        ),
        in_specs=[VMEM],
        out_specs=(VMEM, VMEM, VMEM),
        compiler_params=pltpu.CompilerParams(vmem_limit_bytes=24 * 1024 * 1024),
        name="unpack",
    )(back)
    grad_other = lax.ppermute(grad_mine, "replica", [(i, 1 - i) for i in range(2)])
    d_scale = jnp.where(rep == 0, grad_mine, grad_other)
    d_shift = jnp.where(rep == 0, grad_other, grad_mine)
    return (y_frames[None], dx_frames[None], d_scale, d_shift)


def solution(mesh):
    placed = (
        P(("replica", "tm"), None, "tensor"),
        P("replica", None),
        P(),
        P(),
        P(),
        P("tm", "tensor", None),
        P(),
        P("tensor", None, "tm"),
        P(("replica", "tm"), None, "tensor"),
    )
    return jax.shard_map(
        shards,
        mesh=mesh,
        in_specs=placed,
        out_specs=(
            P(("replica", "tm"), None, "tensor"),
            P(("replica", "tm"), None, "tensor"),
            P(None, "tensor"),
            P(None, "tensor"),
        ),
        check_vma=False,
    )
```

```python
import functools

import jax
import jax.numpy as jnp
from jax import lax
from jax.experimental import pallas as pl
from jax.experimental.pallas import tpu as pltpu
from jax.sharding import PartitionSpec as P

EPS = 1e-06
BF = jnp.bfloat16
F32 = jnp.float32
EXTRA = 16


def dot_nn(a, b):
    return lax.dot_general(a, b, (((1,), (0,)), ((), ())), preferred_element_type=F32)


def dot_nt(a, b):
    return lax.dot_general(a, b, (((1,), (1,)), ((), ())), preferred_element_type=F32)


def dot_tn(a, b):
    return lax.dot_general(a, b, (((0,), (0,)), ((), ())), preferred_element_type=F32)


def halves(value):
    high = value.astype(BF)
    return high, (value - high.astype(F32)).astype(BF)


def selector(shape, pick):
    row = lax.broadcasted_iota(jnp.int32, shape, 0)
    col = lax.broadcasted_iota(jnp.int32, shape, 1)
    return jnp.where(pick(row, col), 1.0, 0.0).astype(BF)


def tokens_kernel(patch_dev, x_ref, g_ref, hold_ref, both_ref):
    rows = x_ref.shape[0]
    pair = 2 * patch_dev
    pick_x = selector(
        (2 * rows, rows),
        lambda m, n: (m % pair < patch_dev) & (m // pair * patch_dev + m % pair == n),
    )
    pick_g = selector(
        (2 * rows, rows),
        lambda m, n: (m % pair >= patch_dev)
        & (m // pair * patch_dev + m % pair - patch_dev == n),
    )
    both_ref[...] = (dot_nn(pick_x, x_ref[...]) + dot_nn(pick_g, g_ref[...])).astype(BF)


def pack_kernel(place_ref, qkv_ref, out_ref, near_ref, far_ref):
    depth = near_ref.shape[0] + far_ref.shape[0]
    near = near_ref.shape[0]
    all_heads = qkv_ref.shape[0] // depth
    heads = out_ref.shape[0] // 2
    triple = qkv_ref.shape[1]
    width = triple // 3
    rep = place_ref[0]
    for head in range(heads):
        own = rep * heads + head
        pick = selector(
            (depth, all_heads * depth),
            lambda m, n: m * all_heads + own == n,
        )
        part = dot_nn(pick, qkv_ref[...]).astype(BF)
        cols = slice(head * triple, (head + 1) * triple)
        near_ref[:, cols] = part[:near]
        far_ref[:, cols] = part[near:]
        eye = selector((depth, depth), lambda m, n: m == n)
        part = dot_nt(eye, out_ref[own]).astype(BF)
        cols = slice(heads * triple + head * width, heads * triple + (head + 1) * width)
        near_ref[:, cols] = part[:near]
        far_ref[:, cols] = part[near:]


def prep_kernel(
    patch_dev,
    place_ref,
    full_ref,
    hot_ref,
    gain_ref,
    scale_ref,
    shift_ref,
    hidden_ref,
    grad_ref,
    normed_ref,
    scaled_ref,
    coef_ref,
    xinv_ref,
    xown_ref,
    gown_ref,
):
    parts = full_ref.shape[1]
    group = hidden_ref.shape[1]
    quarter = full_ref.shape[3]
    pair = 2 * patch_dev
    pick_x = selector(
        (group, 2 * group), lambda m, n: m // patch_dev * pair + m % patch_dev == n
    )
    pick_g = selector(
        (group, 2 * group), lambda m, n: m // patch_dev * pair + m % patch_dev + patch_dev == n
    )
    hot = hot_ref[...]

    def rows_of(table):
        high, low = halves(table)
        return dot_nn(hot, high) + dot_nn(hot, low)

    square = jnp.zeros((group, 1), F32)
    for part in range(parts):
        x = dot_nn(pick_x, full_ref[0, part])
        square += jnp.sum(x * x, -1, keepdims=True)
    inverse = lax.rsqrt(square / (parts * quarter) + EPS)
    for part in range(parts):
        x = dot_nn(pick_x, full_ref[0, part])
        normed = x * inverse * gain_ref[part]
        scaled = normed * (1.0 + rows_of(scale_ref[part]))
        hidden_ref[part] = (scaled + rows_of(shift_ref[part])).astype(BF)
        normed_ref[part] = normed.astype(BF)
        scaled_ref[part] = scaled.astype(BF)
        grad_ref[part] = dot_nn(pick_g, full_ref[0, part]).astype(BF)

    @pl.when(pl.program_id(0) == place_ref[0])
    def _():
        own = place_ref[1]
        rows = full_ref[0, own]
        x = dot_nn(pick_x, rows)
        xown_ref[...] = x.astype(BF)
        gown_ref[...] = dot_nn(pick_g, rows).astype(BF)
        coef_ref[...] = inverse * (1.0 + rows_of(scale_ref[own])) * gain_ref[own]
        xinv_ref[...] = x * inverse * inverse


def block_kernel(
    patch_dev,
    frames,
    plan,
    place_ref,
    gains_ref,
    hot_ref,
    hidden_hbm,
    grad_hbm,
    normed_hbm,
    scaled_hbm,
    *refs,
):
    count = 1 + max(item[0] for item in plan)
    pieces = refs[:count]
    (
        y_keep,
        y_give,
        dh_keep,
        dh_give,
        hidden,
        grad,
        normed,
        scaled,
        weight,
        qkv_acc,
        da_acc,
        attended,
        dqkv,
        y_stage,
        dh_stage,
        sems,
        weight_sems,
        out_sems,
    ) = refs[count:]
    parts, tokens, quarter = hidden.shape
    width = gains_ref.shape[1]
    wide = qkv_acc.shape[1]
    heads = wide // (3 * width)
    cores, ring, group, _ = y_stage.shape
    replicas = tokens // group
    along = ring // replicas
    rows_y = place_ref[2]
    rows_z = place_ref[3]
    spot_x = place_ref[4]
    core = place_ref[5]
    depth = weight.shape[0] // (NY * NZ)

    def inputs(at):
        part = (rows_y + at) % NY
        result = [
            pltpu.make_async_copy(hidden_hbm.at[part], hidden.at[part], sems.at[at, 0]),
            pltpu.make_async_copy(grad_hbm.at[part], grad.at[part], sems.at[at, 1]),
        ]
        for number, (index, start, size, dy, dz, place) in enumerate(plan):
            if dy == at:
                owner = part * NZ + (rows_z + dz) % NZ
                target = pl.multiple_of(owner * depth + place, 16)
                result.append(
                    pltpu.make_async_copy(
                        pieces[index].at[pl.ds(start, size)],
                        weight.at[pl.ds(target, size)],
                        weight_sems.at[number],
                    )
                )
        return result

    def second(part):
        return [
            pltpu.make_async_copy(normed_hbm.at[part], normed.at[part], sems.at[part, 2]),
            pltpu.make_async_copy(scaled_hbm.at[part], scaled.at[part], sems.at[part, 3]),
        ]

    for at in range(NY):
        for copy in inputs(at):
            copy.start()
    for part in range(parts):
        for copy in second(part):
            copy.start()

    qkv_acc[...] = jnp.zeros_like(qkv_acc)
    da_acc[...] = jnp.zeros_like(da_acc)
    for at in range(NY):
        for copy in inputs(at):
            copy.wait()
        part = (rows_y + at) % NY
        rows = pl.ds(pl.multiple_of(part * quarter, quarter), quarter)
        qkv_acc[...] += dot_nn(hidden[part], weight[rows, :wide])
        da_acc[...] += dot_nn(grad[part], weight[rows, wide:])

    gain_q = gains_ref[0:1, :]
    gain_k = gains_ref[1:2, :]
    row = lax.broadcasted_iota(jnp.int32, (group, group), 0)
    col = lax.broadcasted_iota(jnp.int32, (group, group), 1)
    clip_tokens = frames * patch_dev
    mask = (
        (row % patch_dev == col % patch_dev)
        & (row // clip_tokens == col // clip_tokens)
        & (col <= row)
    )
    factor = width ** (-0.5)
    for rep in range(replicas):
        rows = slice(rep * group, (rep + 1) * group)
        for head in range(heads):
            base = head * 3 * width
            take = lambda at: qkv_acc[rows, base + at * width : base + (at + 1) * width].astype(
                BF
            )
            q = take(0).astype(F32)
            k = take(1).astype(F32)
            value = take(2)
            d_out = da_acc[rows, head * width : (head + 1) * width].astype(BF)
            inv_q = lax.rsqrt(jnp.mean(q * q, -1, keepdims=True) + EPS)
            inv_k = lax.rsqrt(jnp.mean(k * k, -1, keepdims=True) + EPS)
            q_hat = q * inv_q
            k_hat = k * inv_k
            queries = (q_hat * gain_q).astype(BF)
            keys = (k_hat * gain_k).astype(BF)
            scores = dot_nt(queries, keys) * factor
            weights = jnp.where(mask, jnp.exp(scores), 0.0)
            probs = weights / jnp.sum(weights, -1, keepdims=True)
            probs_bf = probs.astype(BF)
            out = dot_nn(probs_bf, value)
            attended[rows, head * width : (head + 1) * width] = out.astype(BF)
            d_value = dot_tn(probs_bf, d_out)
            d_probs = dot_nt(d_out, value)
            d_scores = probs * (d_probs - jnp.sum(d_probs * probs, -1, keepdims=True))
            d_scores = (d_scores * factor).astype(BF)
            d_q = dot_nn(d_scores, keys) * gain_q
            d_k = dot_tn(d_scores, queries) * gain_k
            d_q = inv_q * (d_q - q_hat * jnp.mean(d_q * q_hat, -1, keepdims=True))
            d_k = inv_k * (d_k - k_hat * jnp.mean(d_k * k_hat, -1, keepdims=True))
            for at, item in enumerate((d_q, d_k, d_value)):
                dqkv[rows, base + at * width : base + (at + 1) * width] = item.astype(BF)

    def outputs(stage, keep, give, base):
        result = []
        for step in range(ring):
            target = (spot_x + step) % ring
            for side, out in enumerate((keep, give)):
                result.append(
                    pltpu.make_async_copy(
                        stage.at[(core + side) % cores, target],
                        out.at[step],
                        out_sems.at[base, step, side],
                    )
                )
        return result

    block = min(quarter, 256)
    for part in range(parts):
        for at in range(quarter // block):
            cols = slice(at * block, (at + 1) * block)
            w_block = weight[part * quarter + at * block : part * quarter + (at + 1) * block, wide:]
            y_block = dot_nt(attended[...], w_block).astype(BF)
            for rep in range(replicas):
                rows = slice(rep * group, (rep + 1) * group)
                y_stage[part % cores, rep * along + part // cores, :, cols] = y_block[rows]
    y_copies = outputs(y_stage, y_keep, y_give, 0)
    for copy in y_copies:
        copy.start()

    for part in range(parts):
        for copy in second(part):
            copy.wait()
    hot = hot_ref[...]
    codes = hot.shape[0]
    tail = dh_stage.shape[2] - group
    lanes = min(block, 128)
    terms = jnp.zeros((tokens, lanes), F32)
    for part in range(parts):
        for at in range(quarter // block):
            cols = slice(at * block, (at + 1) * block)
            w_block = weight[part * quarter + at * block : part * quarter + (at + 1) * block, :wide]
            d_block = dot_nt(dqkv[...], w_block)
            d_rounded = d_block.astype(BF)
            d_scale = dot_nn(hot, (d_block * normed[part, :, cols].astype(F32)).astype(BF))
            d_shift = dot_nn(hot, d_rounded)
            for rep, item in enumerate((d_scale, d_shift)):
                where = (part % cores, rep * along + part // cores)
                rows = slice(rep * group, (rep + 1) * group)
                dh_stage[where[0], where[1], 0:group, cols] = d_rounded[rows]
                dh_stage[where[0], where[1], group : group + codes, cols] = item.astype(BF)
            product = d_block * scaled[part, :, cols].astype(F32)
            for lane in range(block // lanes):
                terms += product[:, lane * lanes : (lane + 1) * lanes]
    ones = jnp.ones((8, lanes), BF)
    high, low = halves(terms)
    high, low = halves(dot_nt(ones, high) + dot_nt(ones, low))
    sub = lax.broadcasted_iota(jnp.int32, (8, group), 0)
    for rep in range(replicas):
        mine = slice(rep * group, (rep + 1) * group)
        both = jnp.where(
            sub == 0,
            high[:, mine].astype(F32),
            jnp.where(sub == 1, low[:, mine].astype(F32), 0.0),
        ).astype(BF)
        for part in range(parts):
            where = (part % cores, rep * along + part // cores)
            dh_stage[where[0], where[1], group + codes :, :] = jnp.zeros(
                (tail - codes, quarter), BF
            )
            dh_stage[where[0], where[1], group + codes : group + codes + 8, 0:group] = both
    dh_copies = outputs(dh_stage, dh_keep, dh_give, 1)
    for copy in dh_copies:
        copy.start()
    for copy in y_copies + dh_copies:
        copy.wait()


def finish_kernel(
    patch_dev,
    code_count,
    parts,
    yk_ref,
    yr_ref,
    ya_ref,
    yb_ref,
    dk_ref,
    dr_ref,
    da_ref,
    db_ref,
    coef_ref,
    xinv_ref,
    xown_ref,
    gown_ref,
    send_ref,
):
    group, quarter = xown_ref.shape
    y = (
        xown_ref[...].astype(F32)
        + (yk_ref[0].astype(F32) + yr_ref[0].astype(F32))
        + (ya_ref[...].astype(F32) + yb_ref[...].astype(F32))
    )
    total = (dk_ref[0].astype(F32) + dr_ref[0].astype(F32)) + (
        da_ref[...].astype(F32) + db_ref[...].astype(F32)
    )
    terms = total[group + code_count : group + code_count + 8, :group]
    term = (terms[0:1] + terms[1:2]) / (quarter * parts)
    term = jnp.broadcast_to(term, (group, group)).T[:, 0:1]
    dx = gown_ref[...].astype(F32) + (total[:group] * coef_ref[...] - xinv_ref[...] * term)
    grads = total[group : group + code_count].astype(BF)
    span = 2 * patch_dev + code_count
    rows = send_ref.shape[0]
    pick_y = selector(
        (rows, group),
        lambda m, n: (m % span < patch_dev) & (m // span * patch_dev + m % span == n),
    )
    pick_d = selector(
        (rows, group),
        lambda m, n: (m % span >= patch_dev)
        & (m % span < 2 * patch_dev)
        & (m // span * patch_dev + m % span - patch_dev == n),
    )
    pick_g = selector((rows, code_count), lambda m, n: m % span - 2 * patch_dev == n)
    send_ref[...] = (
        dot_nn(pick_y, y.astype(BF)) + dot_nn(pick_d, dx.astype(BF)) + dot_nn(pick_g, grads)
    ).astype(BF)


def unpack_kernel(patch_dev, factor, back_ref, y_ref, dx_ref, sum_ref):
    group = y_ref.shape[0]
    rows = back_ref.shape[0]
    codes = sum_ref.shape[0]
    span = 2 * patch_dev + codes
    back = back_ref[...]
    pick_y = selector((group, rows), lambda m, n: m // patch_dev * span + m % patch_dev == n)
    pick_d = selector(
        (group, rows), lambda m, n: m // patch_dev * span + m % patch_dev + patch_dev == n
    )
    pick_g = selector((codes, rows), lambda m, n: n % span - 2 * patch_dev == m)
    y_ref[...] = dot_nn(pick_y, back).astype(BF)
    dx_ref[...] = dot_nn(pick_d, back).astype(BF)
    sum_ref[...] = dot_nn(pick_g, back) * factor


NY = 4
NZ = 8
CORES = 2
VMEM = pl.BlockSpec(memory_space=pltpu.VMEM)
SMEM = pl.BlockSpec(memory_space=pltpu.SMEM)
ANY = pl.BlockSpec(memory_space=pl.ANY)


def fetch(value, dy, dz):
    pairs = []
    for y in range(NY):
        for z in range(NZ):
            pairs.append((((y + dy) % NY) * NZ + (z + dz) % NZ, y * NZ + z))
    return lax.ppermute(value, "tm", pairs)


def fetch_x(value, dx, ring):
    pairs = []
    for x in range(ring):
        for core in range(CORES):
            pairs.append((((x + dx) % ring) * CORES + core, x * CORES + core))
    return lax.ppermute(value, ("replica", "tensor"), pairs)


def swap_cores(value, ring):
    pairs = []
    for x in range(ring):
        for core in range(CORES):
            pairs.append((x * CORES + core, x * CORES + 1 - core))
    return lax.ppermute(value, ("replica", "tensor"), pairs)


def gate(*values):
    return lax.optimization_barrier(values)


def gather_weight(near, far, tokens_in, tokens_ready):
    a = near.shape[0]
    b = far.shape[0]
    pieces = []
    plan = []

    def add(value, blocks):
        start = 0
        for size, dy, dz, place in blocks:
            plan.append((len(pieces), start, size, dy % NY, dz % NZ, place))
            start += size
        pieces.append(value)

    def line(dy, *dzs):
        return [(a, dy, dz, 0) for dz in dzs]

    def column(dz, ys=(0, 1, -1, 2)):
        return [(b, dy, dz, a) for dy in ys]

    def pair(value, *dzs):
        up, dn = fetch(value, 1, 0), fetch(value, -1, 0)
        add(up, line(1, *dzs))
        add(dn, line(-1, *dzs))
        return up, dn

    def across(up, dn, *dzs):
        half = up.shape[0] // 2
        low, high = fetch(up[:half], 1, 0), fetch(dn[half:], -1, 0)
        if len(dzs) > 1:
            add(low, line(2, dzs[0]))
            add(high, line(2, dzs[1]))
        else:
            add(jnp.concatenate([low, high], 0), line(2, *dzs))
        return low, high

    add(near, line(0, 0))
    zu, zd = fetch(near, 0, 1), fetch(near, 0, -1)
    fu, fd = fetch(far, 1, 0), fetch(far, -1, 0)
    ou, od = pair(near, 0)
    zu, zd, fu, fd, ou, od = gate(zu, zd, fu, fd, ou, od)
    zu2, zd2 = fetch(zu, 0, 1), fetch(zd, 0, -1)
    fl, fh = fetch(fu[: b // 2], 1, 0), fetch(fd[b // 2 :], -1, 0)
    one = jnp.concatenate([zu, zd], 0)
    add(one, line(0, 1, -1))
    u1, d1 = pair(one, 1, -1)
    zu2, zd2, fl, fh, u1, d1 = gate(zu2, zd2, fl, fh, u1, d1)
    cols = jnp.concatenate([far, fu, fd, fl, fh], 0)
    two = jnp.concatenate([zu2, zd2], 0)
    add(cols, column(0))
    add(two, line(0, 2, -2))
    cu, cd = fetch(cols, 0, 1), fetch(cols, 0, -1)
    zu3, zd3 = fetch(zu2, 0, 1), fetch(zd2, 0, -1)
    u2, d2 = pair(two, 2, -2)
    x1, w1 = across(u1, d1, 1, -1)
    token = tokens_in(zu2)
    cu, cd, zu3, zd3, u2, d2, x1, w1, token = gate(cu, cd, zu3, zd3, u2, d2, x1, w1, token)
    add(cu, column(1))
    add(cd, column(-1))
    three = jnp.concatenate([zu3, zd3], 0)
    add(three, line(0, 3, -3))
    cu2, cd2 = fetch(cu, 0, 1), fetch(cd, 0, -1)
    z4l, z4h = fetch(zu3[: a // 2], 0, 1), fetch(zd3[a // 2 :], 0, -1)
    u3, d3 = pair(three, 3, -3)
    x2, w2 = across(u2, d2, 2, -2)
    cu2, cd2, z4l, z4h, u3, d3, x2, w2 = gate(cu2, cd2, z4l, z4h, u3, d3, x2, w2)
    add(cu2, column(2))
    add(cd2, column(-2))
    four = jnp.concatenate([z4l, z4h], 0)
    add(four, line(0, 4))
    cu3, cd3 = fetch(cu2, 0, 1), fetch(cd2, 0, -1)
    u4, d4 = pair(four, 4)
    x3, w3 = across(u3, d3, 3, -3)
    x0, w0 = across(ou, od, 0)
    ready = tokens_ready(token)
    cu3, cd3, u4, d4, x3, w3, x0, w0, *ready = gate(cu3, cd3, u4, d4, x3, w3, x0, w0, *ready)
    add(cu3, column(3))
    add(cd3, column(-3))
    add(fetch(cu3[: 2 * b], 0, 1), column(4, (0, 1)))
    add(fetch(cd3[2 * b :], 0, -1), column(4, (-1, 2)))
    across(u4, d4, 4)
    return pieces, tuple(plan), ready


def reduce_ring(keep, give, ring):
    got = swap_cores(give, ring)
    rows = keep.shape[1]
    half = rows // 32 * 16

    def both(at, rows_from, rows_to):
        return keep[at, rows_from:rows_to].astype(F32) + got[at, rows_from:rows_to].astype(F32)

    low = fetch_x(both(2, 0, half).astype(BF), -1, ring)
    high = fetch_x(both(2, half, rows).astype(BF), 1, ring)
    up = jnp.concatenate(
        [both(1, 0, half) + low.astype(F32), both(1, half, rows)], 0
    ).astype(BF)
    dn = jnp.concatenate(
        [both(3, 0, half), both(3, half, rows) + high.astype(F32)], 0
    ).astype(BF)
    return keep, got, fetch_x(up, -1, ring), fetch_x(dn, 1, ring)


def shards(
    activations,
    action_codes,
    norm_gain,
    action_scale,
    action_shift,
    qkv_weight,
    qk_gains,
    out_weight,
    grad_output,
):
    replicas = lax.axis_size("replica")
    shards_tm = lax.axis_size("tm")
    parts = lax.axis_size("tensor")
    ring = replicas * parts // CORES
    rep = lax.axis_index("replica")
    part = lax.axis_index("tensor")
    spot = lax.axis_index("tm")
    frames = action_codes.shape[1]
    quarter = activations.shape[2]
    patches = activations.shape[1]
    patch_dev = patches // shards_tm
    depth = qkv_weight.shape[0]
    heads = qkv_weight.shape[1] // replicas
    triple = qkv_weight.shape[2]
    width = triple // 3
    wide = heads * triple
    narrow = heads * width
    code_count = action_scale.shape[0]
    group = shards_tm * patch_dev
    tokens = replicas * group
    near = depth // 8 * 5
    place = jnp.stack(
        [
            rep,
            part,
            spot // NZ,
            spot % NZ,
            rep * (ring // replicas) + part // CORES,
            part % CORES,
        ]
    ).astype(jnp.int32)

    weight_near, weight_far = pl.pallas_call(
        pack_kernel,
        out_shape=(
            jax.ShapeDtypeStruct((near, wide + narrow), BF),
            jax.ShapeDtypeStruct((depth - near, wide + narrow), BF),
        ),
        in_specs=[SMEM] + [VMEM] * 2,
        out_specs=(VMEM, VMEM),
        compiler_params=pltpu.CompilerParams(vmem_limit_bytes=24 * 1024 * 1024),
        name="pack",
    )(place, qkv_weight.reshape(-1, triple), out_weight)

    def tokens_in(hold):
        both = pl.pallas_call(
            functools.partial(tokens_kernel, patch_dev),
            out_shape=jax.ShapeDtypeStruct((2 * patches, quarter), BF),
            in_specs=[VMEM] * 2 + [ANY],
            out_specs=VMEM,
            compiler_params=pltpu.CompilerParams(vmem_limit_bytes=24 * 1024 * 1024),
            name="tokens",
        )(activations.reshape(patches, quarter), grad_output.reshape(patches, quarter), hold)
        return lax.all_to_all(both, "tm", split_axis=0, concat_axis=0, tiled=True)

    other = lax.ppermute(action_codes, "replica", [(i, 1 - i) for i in range(2)])
    codes = jnp.where(
        rep == 0,
        jnp.concatenate([action_codes, other], 0),
        jnp.concatenate([other, action_codes], 0),
    ).reshape(-1)
    codes = jnp.repeat(codes, patch_dev)
    code_range = jnp.arange(code_count)
    hot = (codes[:, None] == code_range[None, :]).astype(BF)
    hot_t = (codes[None, :] == code_range[:, None]).astype(BF)

    def by_part(table):
        return table.reshape(table.shape[0], parts, quarter).transpose(1, 0, 2)

    big = jax.ShapeDtypeStruct((parts, tokens, quarter), BF)
    big_spec = pl.BlockSpec((parts, group, quarter), lambda i: (0, i, 0))
    own_spec = pl.BlockSpec((group, quarter), lambda i: (0, 0))

    def whole(*shape):
        return pl.BlockSpec(shape, lambda i: (0,) * len(shape))

    def tokens_ready(both):
        full = lax.all_gather(both, ("replica", "tensor"), axis=0)
        full = full.reshape(replicas, parts, 2 * group, quarter)
        return pl.pallas_call(
            functools.partial(prep_kernel, patch_dev),
            grid=(replicas,),
            out_shape=(big, big, big, big)
            + (jax.ShapeDtypeStruct((group, quarter), F32),) * 2
            + (jax.ShapeDtypeStruct((group, quarter), BF),) * 2,
            in_specs=[
                SMEM,
                pl.BlockSpec((1, parts, 2 * group, quarter), lambda i: (i, 0, 0, 0)),
                pl.BlockSpec((group, code_count), lambda i: (i, 0)),
                whole(parts, 1, quarter),
                whole(parts, code_count, quarter),
                whole(parts, code_count, quarter),
            ],
            out_specs=(big_spec,) * 4 + (own_spec,) * 4,
            compiler_params=pltpu.CompilerParams(vmem_limit_bytes=48 * 1024 * 1024),
            name="prep",
        )(
            place,
            full,
            hot,
            by_part(norm_gain[None]),
            by_part(action_scale),
            by_part(action_shift),
        )

    pieces, plan, ready = gather_weight(weight_near, weight_far, tokens_in, tokens_ready)
    hidden, grad, normed, scaled, coef, xinv, x_own, g_own = ready

    tail_rows = group + EXTRA
    y_shape = jax.ShapeDtypeStruct((ring, group, quarter), BF)
    dh_shape = jax.ShapeDtypeStruct((ring, tail_rows, quarter), BF)
    flops = 4 * tokens * parts * quarter * (wide + narrow)
    moved = 2 * parts * quarter * (wide + narrow + 6 * tokens)
    y_keep, y_give, dh_keep, dh_give = pl.pallas_call(
        functools.partial(block_kernel, patch_dev, frames, plan),
        out_shape=(y_shape, y_shape, dh_shape, dh_shape),
        in_specs=[SMEM, VMEM, VMEM] + [ANY] * (4 + len(pieces)),
        out_specs=(ANY,) * 4,
        scratch_shapes=[
            pltpu.VMEM((parts, tokens, quarter), BF),
            pltpu.VMEM((parts, tokens, quarter), BF),
            pltpu.VMEM((parts, tokens, quarter), BF),
            pltpu.VMEM((parts, tokens, quarter), BF),
            pltpu.VMEM((parts * quarter, wide + narrow), BF),
            pltpu.VMEM((tokens, wide), F32),
            pltpu.VMEM((tokens, narrow), F32),
            pltpu.VMEM((tokens, narrow), BF),
            pltpu.VMEM((tokens, wide), BF),
            pltpu.VMEM((CORES, ring, group, quarter), BF),
            pltpu.VMEM((CORES, ring, tail_rows, quarter), BF),
            pltpu.SemaphoreType.DMA((parts, 4)),
            pltpu.SemaphoreType.DMA((len(plan),)),
            pltpu.SemaphoreType.DMA((2, ring, CORES)),
        ],
        compiler_params=pltpu.CompilerParams(vmem_limit_bytes=52 * 1024 * 1024),
        cost_estimate=pl.CostEstimate(flops=flops, bytes_accessed=moved, transcendentals=0),
        name="block",
    )(place, qk_gains, hot_t, hidden, grad, normed, scaled, *pieces)

    dh_terms = reduce_ring(dh_keep, dh_give, ring)
    y_terms = reduce_ring(y_keep, y_give, ring)
    first_y = pl.BlockSpec((1, group, quarter), lambda i: (0, 0, 0))
    first_dh = pl.BlockSpec((1, tail_rows, quarter), lambda i: (0, 0, 0))
    span = 2 * patch_dev + code_count
    send = pl.pallas_call(
        functools.partial(finish_kernel, patch_dev, code_count, parts),
        grid=(1,),
        out_shape=jax.ShapeDtypeStruct((shards_tm * span, quarter), BF),
        in_specs=[first_y] * 2
        + [whole(group, quarter)] * 2
        + [first_dh] * 2
        + [whole(tail_rows, quarter)] * 2
        + [whole(group, quarter)] * 4,
        out_specs=whole(shards_tm * span, quarter),
        compiler_params=pltpu.CompilerParams(vmem_limit_bytes=24 * 1024 * 1024),
        name="finish",
    )(*y_terms, *dh_terms, coef, xinv, x_own, g_own)
    back = lax.all_to_all(send, "tm", split_axis=0, concat_axis=0, tiled=True)
    token_total = tokens * shards_tm
    y_frames, dx_frames, grad_mine = pl.pallas_call(
        functools.partial(unpack_kernel, patch_dev, token_total ** (-0.5)),
        out_shape=(
            jax.ShapeDtypeStruct((group, quarter), BF),
            jax.ShapeDtypeStruct((group, quarter), BF),
            jax.ShapeDtypeStruct((code_count, quarter), F32),
        ),
        in_specs=[VMEM],
        out_specs=(VMEM, VMEM, VMEM),
        compiler_params=pltpu.CompilerParams(vmem_limit_bytes=24 * 1024 * 1024),
        name="unpack",
    )(back)
    grad_other = lax.ppermute(grad_mine, "replica", [(i, 1 - i) for i in range(2)])
    d_scale = jnp.where(rep == 0, grad_mine, grad_other)
    d_shift = jnp.where(rep == 0, grad_other, grad_mine)
    return (y_frames[None], dx_frames[None], d_scale, d_shift)


def solution(mesh):
    placed = (
        P(("replica", "tm"), None, "tensor"),
        P("replica", None),
        P(),
        P(),
        P(),
        P("tm", "tensor", None),
        P(),
        P("tensor", None, "tm"),
        P(("replica", "tm"), None, "tensor"),
    )
    return jax.shard_map(
        shards,
        mesh=mesh,
        in_specs=placed,
        out_specs=(
            P(("replica", "tm"), None, "tensor"),
            P(("replica", "tm"), None, "tensor"),
            P(None, "tensor"),
            P(None, "tensor"),
        ),
        check_vma=False,
    )
```

```python
import functools

import jax
import jax.numpy as jnp
from jax import lax
from jax.experimental import pallas as pl
from jax.experimental.pallas import tpu as pltpu
from jax.sharding import PartitionSpec as P

EPS = 1e-06
BF = jnp.bfloat16
F32 = jnp.float32
EXTRA = 16


def dot_nn(a, b):
    return lax.dot_general(a, b, (((1,), (0,)), ((), ())), preferred_element_type=F32)


def dot_nt(a, b):
    return lax.dot_general(a, b, (((1,), (1,)), ((), ())), preferred_element_type=F32)


def dot_tn(a, b):
    return lax.dot_general(a, b, (((0,), (0,)), ((), ())), preferred_element_type=F32)


def halves(value):
    high = value.astype(BF)
    return high, (value - high.astype(F32)).astype(BF)


def selector(shape, pick):
    row = lax.broadcasted_iota(jnp.int32, shape, 0)
    col = lax.broadcasted_iota(jnp.int32, shape, 1)
    return jnp.where(pick(row, col), 1.0, 0.0).astype(BF)


def tokens_kernel(patch_dev, x_ref, g_ref, hold_ref, both_ref):
    rows = x_ref.shape[0]
    pair = 2 * patch_dev
    pick_x = selector(
        (2 * rows, rows),
        lambda m, n: (m % pair < patch_dev) & (m // pair * patch_dev + m % pair == n),
    )
    pick_g = selector(
        (2 * rows, rows),
        lambda m, n: (m % pair >= patch_dev)
        & (m // pair * patch_dev + m % pair - patch_dev == n),
    )
    both_ref[...] = (dot_nn(pick_x, x_ref[...]) + dot_nn(pick_g, g_ref[...])).astype(BF)


def pack_kernel(place_ref, qkv_ref, out_ref, near_ref, far_ref):
    depth = near_ref.shape[0] + far_ref.shape[0]
    near = near_ref.shape[0]
    all_heads = qkv_ref.shape[0] // depth
    heads = out_ref.shape[0] // 2
    triple = qkv_ref.shape[1]
    width = triple // 3
    rep = place_ref[0]
    for head in range(heads):
        own = rep * heads + head
        pick = selector(
            (depth, all_heads * depth),
            lambda m, n: m * all_heads + own == n,
        )
        part = dot_nn(pick, qkv_ref[...]).astype(BF)
        cols = slice(head * triple, (head + 1) * triple)
        near_ref[:, cols] = part[:near]
        far_ref[:, cols] = part[near:]
        eye = selector((depth, depth), lambda m, n: m == n)
        part = dot_nt(eye, out_ref[own]).astype(BF)
        cols = slice(heads * triple + head * width, heads * triple + (head + 1) * width)
        near_ref[:, cols] = part[:near]
        far_ref[:, cols] = part[near:]


def prep_kernel(
    patch_dev,
    place_ref,
    full_ref,
    hot_ref,
    gain_ref,
    scale_ref,
    shift_ref,
    hidden_ref,
    grad_ref,
    normed_ref,
    scaled_ref,
    coef_ref,
    xinv_ref,
    xown_ref,
    gown_ref,
):
    parts = full_ref.shape[1]
    group = hidden_ref.shape[1]
    quarter = full_ref.shape[3]
    pair = 2 * patch_dev
    pick_x = selector(
        (group, 2 * group), lambda m, n: m // patch_dev * pair + m % patch_dev == n
    )
    pick_g = selector(
        (group, 2 * group), lambda m, n: m // patch_dev * pair + m % patch_dev + patch_dev == n
    )
    hot = hot_ref[...]

    def rows_of(table):
        high, low = halves(table)
        return dot_nn(hot, high) + dot_nn(hot, low)

    square = jnp.zeros((group, 1), F32)
    for part in range(parts):
        x = dot_nn(pick_x, full_ref[0, part])
        square += jnp.sum(x * x, -1, keepdims=True)
    inverse = lax.rsqrt(square / (parts * quarter) + EPS)
    for part in range(parts):
        x = dot_nn(pick_x, full_ref[0, part])
        normed = x * inverse * gain_ref[part]
        scaled = normed * (1.0 + rows_of(scale_ref[part]))
        hidden_ref[part] = (scaled + rows_of(shift_ref[part])).astype(BF)
        normed_ref[part] = normed.astype(BF)
        scaled_ref[part] = scaled.astype(BF)
        grad_ref[part] = dot_nn(pick_g, full_ref[0, part]).astype(BF)

    @pl.when(pl.program_id(0) == place_ref[0])
    def _():
        own = place_ref[1]
        rows = full_ref[0, own]
        x = dot_nn(pick_x, rows)
        xown_ref[...] = x.astype(BF)
        gown_ref[...] = dot_nn(pick_g, rows).astype(BF)
        coef_ref[...] = inverse * (1.0 + rows_of(scale_ref[own])) * gain_ref[own]
        xinv_ref[...] = x * inverse * inverse


def block_kernel(
    patch_dev,
    frames,
    plan,
    place_ref,
    gains_ref,
    hot_ref,
    hidden_hbm,
    grad_hbm,
    normed_hbm,
    scaled_hbm,
    *refs,
):
    count = 1 + max(item[0] for item in plan)
    pieces = refs[:count]
    (
        y_keep,
        y_give,
        dh_keep,
        dh_give,
        hidden,
        grad,
        normed,
        scaled,
        weight,
        qkv_acc,
        da_acc,
        attended,
        dqkv,
        y_stage,
        dh_stage,
        sems,
        weight_sems,
        out_sems,
    ) = refs[count:]
    parts, tokens, quarter = hidden.shape
    width = gains_ref.shape[1]
    wide = qkv_acc.shape[1]
    heads = wide // (3 * width)
    cores, ring, group, _ = y_stage.shape
    replicas = tokens // group
    along = ring // replicas
    rows_y = place_ref[2]
    rows_z = place_ref[3]
    spot_x = place_ref[4]
    core = place_ref[5]
    depth = weight.shape[0] // (NY * NZ)

    def inputs(at):
        part = (rows_y + at) % NY
        result = [
            pltpu.make_async_copy(hidden_hbm.at[part], hidden.at[part], sems.at[at, 0]),
            pltpu.make_async_copy(grad_hbm.at[part], grad.at[part], sems.at[at, 1]),
        ]
        for number, (index, start, size, dy, dz, place) in enumerate(plan):
            if dy == at:
                owner = part * NZ + (rows_z + dz) % NZ
                target = pl.multiple_of(owner * depth + place, 16)
                result.append(
                    pltpu.make_async_copy(
                        pieces[index].at[pl.ds(start, size)],
                        weight.at[pl.ds(target, size)],
                        weight_sems.at[number],
                    )
                )
        return result

    def second(part):
        return [
            pltpu.make_async_copy(normed_hbm.at[part], normed.at[part], sems.at[part, 2]),
            pltpu.make_async_copy(scaled_hbm.at[part], scaled.at[part], sems.at[part, 3]),
        ]

    for at in range(NY):
        for copy in inputs(at):
            copy.start()
    for part in range(parts):
        for copy in second(part):
            copy.start()

    qkv_acc[...] = jnp.zeros_like(qkv_acc)
    da_acc[...] = jnp.zeros_like(da_acc)
    for at in range(NY):
        for copy in inputs(at):
            copy.wait()
        part = (rows_y + at) % NY
        rows = pl.ds(pl.multiple_of(part * quarter, quarter), quarter)
        qkv_acc[...] += dot_nn(hidden[part], weight[rows, :wide])
        da_acc[...] += dot_nn(grad[part], weight[rows, wide:])

    gain_q = gains_ref[0:1, :]
    gain_k = gains_ref[1:2, :]
    row = lax.broadcasted_iota(jnp.int32, (group, group), 0)
    col = lax.broadcasted_iota(jnp.int32, (group, group), 1)
    clip_tokens = frames * patch_dev
    mask = (
        (row % patch_dev == col % patch_dev)
        & (row // clip_tokens == col // clip_tokens)
        & (col <= row)
    )
    factor = width ** (-0.5)
    for rep in range(replicas):
        rows = slice(rep * group, (rep + 1) * group)
        for head in range(heads):
            base = head * 3 * width
            take = lambda at: qkv_acc[rows, base + at * width : base + (at + 1) * width].astype(
                BF
            )
            q = take(0).astype(F32)
            k = take(1).astype(F32)
            value = take(2)
            d_out = da_acc[rows, head * width : (head + 1) * width].astype(BF)
            inv_q = lax.rsqrt(jnp.mean(q * q, -1, keepdims=True) + EPS)
            inv_k = lax.rsqrt(jnp.mean(k * k, -1, keepdims=True) + EPS)
            q_hat = q * inv_q
            k_hat = k * inv_k
            queries = (q_hat * gain_q).astype(BF)
            keys = (k_hat * gain_k).astype(BF)
            scores = dot_nt(queries, keys) * factor
            weights = jnp.where(mask, jnp.exp(scores), 0.0)
            probs = weights / jnp.sum(weights, -1, keepdims=True)
            probs_bf = probs.astype(BF)
            out = dot_nn(probs_bf, value)
            attended[rows, head * width : (head + 1) * width] = out.astype(BF)
            d_value = dot_tn(probs_bf, d_out)
            d_probs = dot_nt(d_out, value)
            d_scores = probs * (d_probs - jnp.sum(d_probs * probs, -1, keepdims=True))
            d_scores = (d_scores * factor).astype(BF)
            d_q = dot_nn(d_scores, keys) * gain_q
            d_k = dot_tn(d_scores, queries) * gain_k
            d_q = inv_q * (d_q - q_hat * jnp.mean(d_q * q_hat, -1, keepdims=True))
            d_k = inv_k * (d_k - k_hat * jnp.mean(d_k * k_hat, -1, keepdims=True))
            for at, item in enumerate((d_q, d_k, d_value)):
                dqkv[rows, base + at * width : base + (at + 1) * width] = item.astype(BF)

    def outputs(stage, keep, give, base):
        result = []
        for step in range(ring):
            target = (spot_x + step) % ring
            for side, out in enumerate((keep, give)):
                result.append(
                    pltpu.make_async_copy(
                        stage.at[(core + side) % cores, target],
                        out.at[step],
                        out_sems.at[base, step, side],
                    )
                )
        return result

    block = min(quarter, 256)
    for part in range(parts):
        for at in range(quarter // block):
            cols = slice(at * block, (at + 1) * block)
            w_block = weight[part * quarter + at * block : part * quarter + (at + 1) * block, wide:]
            y_block = dot_nt(attended[...], w_block).astype(BF)
            for rep in range(replicas):
                rows = slice(rep * group, (rep + 1) * group)
                y_stage[part % cores, rep * along + part // cores, :, cols] = y_block[rows]
    y_copies = outputs(y_stage, y_keep, y_give, 0)
    for copy in y_copies:
        copy.start()

    for part in range(parts):
        for copy in second(part):
            copy.wait()
    hot = hot_ref[...]
    codes = hot.shape[0]
    tail = dh_stage.shape[2] - group
    lanes = min(block, 128)
    terms = jnp.zeros((tokens, lanes), F32)
    for part in range(parts):
        for at in range(quarter // block):
            cols = slice(at * block, (at + 1) * block)
            w_block = weight[part * quarter + at * block : part * quarter + (at + 1) * block, :wide]
            d_block = dot_nt(dqkv[...], w_block)
            d_rounded = d_block.astype(BF)
            d_scale = dot_nn(hot, (d_block * normed[part, :, cols].astype(F32)).astype(BF))
            d_shift = dot_nn(hot, d_rounded)
            for rep, item in enumerate((d_scale, d_shift)):
                where = (part % cores, rep * along + part // cores)
                rows = slice(rep * group, (rep + 1) * group)
                dh_stage[where[0], where[1], 0:group, cols] = d_rounded[rows]
                dh_stage[where[0], where[1], group : group + codes, cols] = item.astype(BF)
            product = d_block * scaled[part, :, cols].astype(F32)
            for lane in range(block // lanes):
                terms += product[:, lane * lanes : (lane + 1) * lanes]
    ones = jnp.ones((8, lanes), BF)
    high, low = halves(terms)
    high, low = halves(dot_nt(ones, high) + dot_nt(ones, low))
    sub = lax.broadcasted_iota(jnp.int32, (8, group), 0)
    for rep in range(replicas):
        mine = slice(rep * group, (rep + 1) * group)
        both = jnp.where(
            sub == 0,
            high[:, mine].astype(F32),
            jnp.where(sub == 1, low[:, mine].astype(F32), 0.0),
        ).astype(BF)
        for part in range(parts):
            where = (part % cores, rep * along + part // cores)
            dh_stage[where[0], where[1], group + codes :, :] = jnp.zeros(
                (tail - codes, quarter), BF
            )
            dh_stage[where[0], where[1], group + codes : group + codes + 8, 0:group] = both
    dh_copies = outputs(dh_stage, dh_keep, dh_give, 1)
    for copy in dh_copies:
        copy.start()
    for copy in y_copies + dh_copies:
        copy.wait()


def finish_kernel(
    patch_dev,
    code_count,
    parts,
    yk_ref,
    yr_ref,
    ya_ref,
    yb_ref,
    dk_ref,
    dr_ref,
    da_ref,
    db_ref,
    coef_ref,
    xinv_ref,
    xown_ref,
    gown_ref,
    send_ref,
):
    group, quarter = xown_ref.shape
    y = (
        xown_ref[...].astype(F32)
        + (yk_ref[0].astype(F32) + yr_ref[0].astype(F32))
        + (ya_ref[...].astype(F32) + yb_ref[...].astype(F32))
    )
    total = (dk_ref[0].astype(F32) + dr_ref[0].astype(F32)) + (
        da_ref[...].astype(F32) + db_ref[...].astype(F32)
    )
    terms = total[group + code_count : group + code_count + 8, :group]
    term = (terms[0:1] + terms[1:2]) / (quarter * parts)
    term = jnp.broadcast_to(term, (group, group)).T[:, 0:1]
    dx = gown_ref[...].astype(F32) + (total[:group] * coef_ref[...] - xinv_ref[...] * term)
    grads = total[group : group + code_count].astype(BF)
    span = 2 * patch_dev + code_count
    rows = send_ref.shape[0]
    pick_y = selector(
        (rows, group),
        lambda m, n: (m % span < patch_dev) & (m // span * patch_dev + m % span == n),
    )
    pick_d = selector(
        (rows, group),
        lambda m, n: (m % span >= patch_dev)
        & (m % span < 2 * patch_dev)
        & (m // span * patch_dev + m % span - patch_dev == n),
    )
    pick_g = selector((rows, code_count), lambda m, n: m % span - 2 * patch_dev == n)
    send_ref[...] = (
        dot_nn(pick_y, y.astype(BF)) + dot_nn(pick_d, dx.astype(BF)) + dot_nn(pick_g, grads)
    ).astype(BF)


def unpack_kernel(patch_dev, factor, back_ref, y_ref, dx_ref, sum_ref):
    group = y_ref.shape[0]
    rows = back_ref.shape[0]
    codes = sum_ref.shape[0]
    span = 2 * patch_dev + codes
    back = back_ref[...]
    pick_y = selector((group, rows), lambda m, n: m // patch_dev * span + m % patch_dev == n)
    pick_d = selector(
        (group, rows), lambda m, n: m // patch_dev * span + m % patch_dev + patch_dev == n
    )
    pick_g = selector((codes, rows), lambda m, n: n % span - 2 * patch_dev == m)
    y_ref[...] = dot_nn(pick_y, back).astype(BF)
    dx_ref[...] = dot_nn(pick_d, back).astype(BF)
    sum_ref[...] = dot_nn(pick_g, back) * factor


NY = 4
NZ = 8
CORES = 2
VMEM = pl.BlockSpec(memory_space=pltpu.VMEM)
SMEM = pl.BlockSpec(memory_space=pltpu.SMEM)
ANY = pl.BlockSpec(memory_space=pl.ANY)


def fetch(value, dy, dz):
    pairs = []
    for y in range(NY):
        for z in range(NZ):
            pairs.append((((y + dy) % NY) * NZ + (z + dz) % NZ, y * NZ + z))
    return lax.ppermute(value, "tm", pairs)


def fetch_x(value, dx, ring):
    pairs = []
    for x in range(ring):
        for core in range(CORES):
            pairs.append((((x + dx) % ring) * CORES + core, x * CORES + core))
    return lax.ppermute(value, ("replica", "tensor"), pairs)


def swap_cores(value, ring):
    pairs = []
    for x in range(ring):
        for core in range(CORES):
            pairs.append((x * CORES + core, x * CORES + 1 - core))
    return lax.ppermute(value, ("replica", "tensor"), pairs)


def gate(*values):
    return lax.optimization_barrier(values)


def gather_weight(near, far, tokens_in, tokens_ready):
    a = near.shape[0]
    b = far.shape[0]
    pieces = []
    plan = []

    def add(value, blocks):
        start = 0
        for size, dy, dz, place in blocks:
            plan.append((len(pieces), start, size, dy % NY, dz % NZ, place))
            start += size
        pieces.append(value)

    def line(dy, *dzs):
        return [(a, dy, dz, 0) for dz in dzs]

    def column(dz, ys=(0, 1, -1, 2)):
        return [(b, dy, dz, a) for dy in ys]

    def pair(value, dzs):
        up, dn = fetch(value, 1, 0), fetch(value, -1, 0)
        add(value, line(0, *dzs))
        add(up, line(1, *dzs))
        add(dn, line(-1, *dzs))
        return up, dn

    def across(up, dn, count, dzs):
        low, high = fetch(up[: count * a], 1, 0), fetch(dn[count * a :], -1, 0)
        add(low, line(2, *dzs[:count]))
        add(high, line(2, *dzs[count:]))
        return low, high

    zu, zd = fetch(near, 0, 1), fetch(near, 0, -1)
    fu, fd, fo = fetch(far, 1, 0), fetch(far, -1, 0), fetch(far, 2, 0)
    near, far, zu, zd, fu, fd, fo = gate(near, far, zu, zd, fu, fd, fo)
    cols = jnp.concatenate([far, fu, fd, fo], 0)
    add(cols, column(0))
    first_at = (0, 1, -1)
    up1, dn1 = pair(jnp.concatenate([near, zu, zd], 0), first_at)
    zu2, zd2 = fetch(zu, 0, 1), fetch(zd, 0, -1)
    zu3, zd3 = fetch(zu2, 0, 1), fetch(zd2, 0, -1)
    cu, cd = fetch(cols, 0, 1), fetch(cols, 0, -1)
    token = tokens_in(zu2)
    up1, dn1, zu2, zd2, zu3, zd3, cu, cd, token = gate(
        up1, dn1, zu2, zd2, zu3, zd3, cu, cd, token
    )
    add(cu, column(1))
    add(cd, column(-1))
    second_at = (2, -2, 3, -3)
    up2, dn2 = pair(jnp.concatenate([zu2, zd2, zu3, zd3], 0), second_at)
    z4l, z4h = fetch(zu3[: a // 2], 0, 1), fetch(zd3[a // 2 :], 0, -1)
    cu2, cd2 = fetch(cu, 0, 1), fetch(cd, 0, -1)
    up2, dn2, z4l, z4h, cu2, cd2 = gate(up2, dn2, z4l, z4h, cu2, cd2)
    add(cu2, column(2))
    add(cd2, column(-2))
    up3, dn3 = pair(jnp.concatenate([z4l, z4h], 0), (4,))
    cu3, cd3 = fetch(cu2, 0, 1), fetch(cd2, 0, -1)
    across(up2, dn2, 2, second_at)
    ready = tokens_ready(token)
    up3, dn3, cu3, cd3, *ready = gate(up3, dn3, cu3, cd3, *ready)
    across(up1, dn1, 2, first_at)
    add(cu3, column(3))
    add(cd3, column(-3))
    add(fetch(cu3[: 2 * b], 0, 1), column(4, (0, 1)))
    add(fetch(cd3[2 * b :], 0, -1), column(4, (-1, 2)))
    add(fetch(dn3, -1, 0), line(2, 4))
    return pieces, tuple(plan), ready


def reduce_ring(keep, give, ring):
    got = swap_cores(give, ring)
    rows = keep.shape[1]
    half = rows // 32 * 16

    def both(at, rows_from, rows_to):
        return keep[at, rows_from:rows_to].astype(F32) + got[at, rows_from:rows_to].astype(F32)

    low = fetch_x(both(2, 0, half).astype(BF), -1, ring)
    high = fetch_x(both(2, half, rows).astype(BF), 1, ring)
    up = jnp.concatenate(
        [both(1, 0, half) + low.astype(F32), both(1, half, rows)], 0
    ).astype(BF)
    dn = jnp.concatenate(
        [both(3, 0, half), both(3, half, rows) + high.astype(F32)], 0
    ).astype(BF)
    return keep, got, fetch_x(up, -1, ring), fetch_x(dn, 1, ring)


def shards(
    activations,
    action_codes,
    norm_gain,
    action_scale,
    action_shift,
    qkv_weight,
    qk_gains,
    out_weight,
    grad_output,
):
    replicas = lax.axis_size("replica")
    shards_tm = lax.axis_size("tm")
    parts = lax.axis_size("tensor")
    ring = replicas * parts // CORES
    rep = lax.axis_index("replica")
    part = lax.axis_index("tensor")
    spot = lax.axis_index("tm")
    frames = action_codes.shape[1]
    quarter = activations.shape[2]
    patches = activations.shape[1]
    patch_dev = patches // shards_tm
    depth = qkv_weight.shape[0]
    heads = qkv_weight.shape[1] // replicas
    triple = qkv_weight.shape[2]
    width = triple // 3
    wide = heads * triple
    narrow = heads * width
    code_count = action_scale.shape[0]
    group = shards_tm * patch_dev
    tokens = replicas * group
    near = depth // 8 * 5
    place = jnp.stack(
        [
            rep,
            part,
            spot // NZ,
            spot % NZ,
            rep * (ring // replicas) + part // CORES,
            part % CORES,
        ]
    ).astype(jnp.int32)

    weight_near, weight_far = pl.pallas_call(
        pack_kernel,
        out_shape=(
            jax.ShapeDtypeStruct((near, wide + narrow), BF),
            jax.ShapeDtypeStruct((depth - near, wide + narrow), BF),
        ),
        in_specs=[SMEM] + [VMEM] * 2,
        out_specs=(VMEM, VMEM),
        compiler_params=pltpu.CompilerParams(vmem_limit_bytes=24 * 1024 * 1024),
        name="pack",
    )(place, qkv_weight.reshape(-1, triple), out_weight)

    def tokens_in(hold):
        both = pl.pallas_call(
            functools.partial(tokens_kernel, patch_dev),
            out_shape=jax.ShapeDtypeStruct((2 * patches, quarter), BF),
            in_specs=[VMEM] * 2 + [ANY],
            out_specs=VMEM,
            compiler_params=pltpu.CompilerParams(vmem_limit_bytes=24 * 1024 * 1024),
            name="tokens",
        )(activations.reshape(patches, quarter), grad_output.reshape(patches, quarter), hold)
        return lax.all_to_all(both, "tm", split_axis=0, concat_axis=0, tiled=True)

    other = lax.ppermute(action_codes, "replica", [(i, 1 - i) for i in range(2)])
    codes = jnp.where(
        rep == 0,
        jnp.concatenate([action_codes, other], 0),
        jnp.concatenate([other, action_codes], 0),
    ).reshape(-1)
    codes = jnp.repeat(codes, patch_dev)
    code_range = jnp.arange(code_count)
    hot = (codes[:, None] == code_range[None, :]).astype(BF)
    hot_t = (codes[None, :] == code_range[:, None]).astype(BF)

    def by_part(table):
        return table.reshape(table.shape[0], parts, quarter).transpose(1, 0, 2)

    big = jax.ShapeDtypeStruct((parts, tokens, quarter), BF)
    big_spec = pl.BlockSpec((parts, group, quarter), lambda i: (0, i, 0))
    own_spec = pl.BlockSpec((group, quarter), lambda i: (0, 0))

    def whole(*shape):
        return pl.BlockSpec(shape, lambda i: (0,) * len(shape))

    def tokens_ready(both):
        full = lax.all_gather(both, ("replica", "tensor"), axis=0)
        full = full.reshape(replicas, parts, 2 * group, quarter)
        return pl.pallas_call(
            functools.partial(prep_kernel, patch_dev),
            grid=(replicas,),
            out_shape=(big, big, big, big)
            + (jax.ShapeDtypeStruct((group, quarter), F32),) * 2
            + (jax.ShapeDtypeStruct((group, quarter), BF),) * 2,
            in_specs=[
                SMEM,
                pl.BlockSpec((1, parts, 2 * group, quarter), lambda i: (i, 0, 0, 0)),
                pl.BlockSpec((group, code_count), lambda i: (i, 0)),
                whole(parts, 1, quarter),
                whole(parts, code_count, quarter),
                whole(parts, code_count, quarter),
            ],
            out_specs=(big_spec,) * 4 + (own_spec,) * 4,
            compiler_params=pltpu.CompilerParams(vmem_limit_bytes=48 * 1024 * 1024),
            name="prep",
        )(
            place,
            full,
            hot,
            by_part(norm_gain[None]),
            by_part(action_scale),
            by_part(action_shift),
        )

    pieces, plan, ready = gather_weight(weight_near, weight_far, tokens_in, tokens_ready)
    hidden, grad, normed, scaled, coef, xinv, x_own, g_own = ready

    tail_rows = group + EXTRA
    y_shape = jax.ShapeDtypeStruct((ring, group, quarter), BF)
    dh_shape = jax.ShapeDtypeStruct((ring, tail_rows, quarter), BF)
    flops = 4 * tokens * parts * quarter * (wide + narrow)
    moved = 2 * parts * quarter * (wide + narrow + 6 * tokens)
    y_keep, y_give, dh_keep, dh_give = pl.pallas_call(
        functools.partial(block_kernel, patch_dev, frames, plan),
        out_shape=(y_shape, y_shape, dh_shape, dh_shape),
        in_specs=[SMEM, VMEM, VMEM] + [ANY] * (4 + len(pieces)),
        out_specs=(ANY,) * 4,
        scratch_shapes=[
            pltpu.VMEM((parts, tokens, quarter), BF),
            pltpu.VMEM((parts, tokens, quarter), BF),
            pltpu.VMEM((parts, tokens, quarter), BF),
            pltpu.VMEM((parts, tokens, quarter), BF),
            pltpu.VMEM((parts * quarter, wide + narrow), BF),
            pltpu.VMEM((tokens, wide), F32),
            pltpu.VMEM((tokens, narrow), F32),
            pltpu.VMEM((tokens, narrow), BF),
            pltpu.VMEM((tokens, wide), BF),
            pltpu.VMEM((CORES, ring, group, quarter), BF),
            pltpu.VMEM((CORES, ring, tail_rows, quarter), BF),
            pltpu.SemaphoreType.DMA((parts, 4)),
            pltpu.SemaphoreType.DMA((len(plan),)),
            pltpu.SemaphoreType.DMA((2, ring, CORES)),
        ],
        compiler_params=pltpu.CompilerParams(vmem_limit_bytes=52 * 1024 * 1024),
        cost_estimate=pl.CostEstimate(flops=flops, bytes_accessed=moved, transcendentals=0),
        name="block",
    )(place, qk_gains, hot_t, hidden, grad, normed, scaled, *pieces)

    dh_terms = reduce_ring(dh_keep, dh_give, ring)
    y_terms = reduce_ring(y_keep, y_give, ring)
    first_y = pl.BlockSpec((1, group, quarter), lambda i: (0, 0, 0))
    first_dh = pl.BlockSpec((1, tail_rows, quarter), lambda i: (0, 0, 0))
    span = 2 * patch_dev + code_count
    send = pl.pallas_call(
        functools.partial(finish_kernel, patch_dev, code_count, parts),
        grid=(1,),
        out_shape=jax.ShapeDtypeStruct((shards_tm * span, quarter), BF),
        in_specs=[first_y] * 2
        + [whole(group, quarter)] * 2
        + [first_dh] * 2
        + [whole(tail_rows, quarter)] * 2
        + [whole(group, quarter)] * 4,
        out_specs=whole(shards_tm * span, quarter),
        compiler_params=pltpu.CompilerParams(vmem_limit_bytes=24 * 1024 * 1024),
        name="finish",
    )(*y_terms, *dh_terms, coef, xinv, x_own, g_own)
    back = lax.all_to_all(send, "tm", split_axis=0, concat_axis=0, tiled=True)
    token_total = tokens * shards_tm
    y_frames, dx_frames, grad_mine = pl.pallas_call(
        functools.partial(unpack_kernel, patch_dev, token_total ** (-0.5)),
        out_shape=(
            jax.ShapeDtypeStruct((group, quarter), BF),
            jax.ShapeDtypeStruct((group, quarter), BF),
            jax.ShapeDtypeStruct((code_count, quarter), F32),
        ),
        in_specs=[VMEM],
        out_specs=(VMEM, VMEM, VMEM),
        compiler_params=pltpu.CompilerParams(vmem_limit_bytes=24 * 1024 * 1024),
        name="unpack",
    )(back)
    grad_other = lax.ppermute(grad_mine, "replica", [(i, 1 - i) for i in range(2)])
    d_scale = jnp.where(rep == 0, grad_mine, grad_other)
    d_shift = jnp.where(rep == 0, grad_other, grad_mine)
    return (y_frames[None], dx_frames[None], d_scale, d_shift)


def solution(mesh):
    placed = (
        P(("replica", "tm"), None, "tensor"),
        P("replica", None),
        P(),
        P(),
        P(),
        P("tm", "tensor", None),
        P(),
        P("tensor", None, "tm"),
        P(("replica", "tm"), None, "tensor"),
    )
    return jax.shard_map(
        shards,
        mesh=mesh,
        in_specs=placed,
        out_specs=(
            P(("replica", "tm"), None, "tensor"),
            P(("replica", "tm"), None, "tensor"),
            P(None, "tensor"),
            P(None, "tensor"),
        ),
        check_vma=False,
    )
```

```python
import functools

import jax
import jax.numpy as jnp
from jax import lax
from jax.experimental import pallas as pl
from jax.experimental.pallas import tpu as pltpu
from jax.sharding import PartitionSpec as P

EPS = 1e-06
BF = jnp.bfloat16
F32 = jnp.float32
EXTRA = 16


def dot_nn(a, b):
    return lax.dot_general(a, b, (((1,), (0,)), ((), ())), preferred_element_type=F32)


def dot_nt(a, b):
    return lax.dot_general(a, b, (((1,), (1,)), ((), ())), preferred_element_type=F32)


def dot_tn(a, b):
    return lax.dot_general(a, b, (((0,), (0,)), ((), ())), preferred_element_type=F32)


def halves(value):
    high = value.astype(BF)
    return high, (value - high.astype(F32)).astype(BF)


def selector(shape, pick):
    row = lax.broadcasted_iota(jnp.int32, shape, 0)
    col = lax.broadcasted_iota(jnp.int32, shape, 1)
    return jnp.where(pick(row, col), 1.0, 0.0).astype(BF)


def tokens_kernel(patch_dev, x_ref, g_ref, hold_ref, both_ref):
    rows = x_ref.shape[0]
    pair = 2 * patch_dev
    pick_x = selector(
        (2 * rows, rows),
        lambda m, n: (m % pair < patch_dev) & (m // pair * patch_dev + m % pair == n),
    )
    pick_g = selector(
        (2 * rows, rows),
        lambda m, n: (m % pair >= patch_dev)
        & (m // pair * patch_dev + m % pair - patch_dev == n),
    )
    both_ref[...] = (dot_nn(pick_x, x_ref[...]) + dot_nn(pick_g, g_ref[...])).astype(BF)


def pack_kernel(place_ref, qkv_ref, out_ref, near_ref, far_ref):
    depth = near_ref.shape[0] + far_ref.shape[0]
    near = near_ref.shape[0]
    all_heads = qkv_ref.shape[0] // depth
    heads = out_ref.shape[0] // 2
    triple = qkv_ref.shape[1]
    width = triple // 3
    rep = place_ref[0]
    for head in range(heads):
        own = rep * heads + head
        pick = selector(
            (depth, all_heads * depth),
            lambda m, n: m * all_heads + own == n,
        )
        part = dot_nn(pick, qkv_ref[...]).astype(BF)
        cols = slice(head * triple, (head + 1) * triple)
        near_ref[:, cols] = part[:near]
        far_ref[:, cols] = part[near:]
        eye = selector((depth, depth), lambda m, n: m == n)
        part = dot_nt(eye, out_ref[own]).astype(BF)
        cols = slice(heads * triple + head * width, heads * triple + (head + 1) * width)
        near_ref[:, cols] = part[:near]
        far_ref[:, cols] = part[near:]


def prep_kernel(
    patch_dev,
    place_ref,
    full_ref,
    hot_ref,
    gain_ref,
    scale_ref,
    shift_ref,
    hidden_ref,
    grad_ref,
    normed_ref,
    scaled_ref,
    coef_ref,
    xinv_ref,
    xown_ref,
    gown_ref,
):
    parts = full_ref.shape[1]
    group = hidden_ref.shape[1]
    quarter = full_ref.shape[3]
    pair = 2 * patch_dev
    pick_x = selector(
        (group, 2 * group), lambda m, n: m // patch_dev * pair + m % patch_dev == n
    )
    pick_g = selector(
        (group, 2 * group), lambda m, n: m // patch_dev * pair + m % patch_dev + patch_dev == n
    )
    hot = hot_ref[...]

    def rows_of(table):
        high, low = halves(table)
        return dot_nn(hot, high) + dot_nn(hot, low)

    square = jnp.zeros((group, 1), F32)
    for part in range(parts):
        x = dot_nn(pick_x, full_ref[0, part])
        square += jnp.sum(x * x, -1, keepdims=True)
    inverse = lax.rsqrt(square / (parts * quarter) + EPS)
    for part in range(parts):
        x = dot_nn(pick_x, full_ref[0, part])
        normed = x * inverse * gain_ref[part]
        scaled = normed * (1.0 + rows_of(scale_ref[part]))
        hidden_ref[part] = (scaled + rows_of(shift_ref[part])).astype(BF)
        normed_ref[part] = normed.astype(BF)
        scaled_ref[part] = scaled.astype(BF)
        grad_ref[part] = dot_nn(pick_g, full_ref[0, part]).astype(BF)

    @pl.when(pl.program_id(0) == place_ref[0])
    def _():
        own = place_ref[1]
        rows = full_ref[0, own]
        x = dot_nn(pick_x, rows)
        xown_ref[...] = x.astype(BF)
        gown_ref[...] = dot_nn(pick_g, rows).astype(BF)
        coef_ref[...] = inverse * (1.0 + rows_of(scale_ref[own])) * gain_ref[own]
        xinv_ref[...] = x * inverse * inverse


def block_kernel(
    patch_dev,
    frames,
    plan,
    place_ref,
    gains_ref,
    hot_ref,
    hidden_hbm,
    grad_hbm,
    normed_hbm,
    scaled_hbm,
    *refs,
):
    count = 1 + max(item[0] for item in plan)
    pieces = refs[:count]
    (
        y_keep,
        y_give,
        dh_keep,
        dh_give,
        hidden,
        grad,
        normed,
        scaled,
        weight,
        qkv_acc,
        da_acc,
        attended,
        dqkv,
        y_stage,
        dh_stage,
        sems,
        weight_sems,
        out_sems,
    ) = refs[count:]
    parts, tokens, quarter = hidden.shape
    width = gains_ref.shape[1]
    wide = qkv_acc.shape[1]
    heads = wide // (3 * width)
    cores, ring, group, _ = y_stage.shape
    replicas = tokens // group
    along = ring // replicas
    rows_y = place_ref[2]
    rows_z = place_ref[3]
    spot_x = place_ref[4]
    core = place_ref[5]
    depth = weight.shape[0] // (NY * NZ)

    def inputs(at):
        part = (rows_y + at) % NY
        result = [
            pltpu.make_async_copy(hidden_hbm.at[part], hidden.at[part], sems.at[at, 0]),
            pltpu.make_async_copy(grad_hbm.at[part], grad.at[part], sems.at[at, 1]),
        ]
        for number, (index, start, size, dy, dz, place) in enumerate(plan):
            if dy == at:
                owner = part * NZ + (rows_z + dz) % NZ
                target = pl.multiple_of(owner * depth + place, 16)
                result.append(
                    pltpu.make_async_copy(
                        pieces[index].at[pl.ds(start, size)],
                        weight.at[pl.ds(target, size)],
                        weight_sems.at[number],
                    )
                )
        return result

    def second(part):
        return [
            pltpu.make_async_copy(normed_hbm.at[part], normed.at[part], sems.at[part, 2]),
            pltpu.make_async_copy(scaled_hbm.at[part], scaled.at[part], sems.at[part, 3]),
        ]

    for at in range(NY):
        for copy in inputs(at):
            copy.start()
    for part in range(parts):
        for copy in second(part):
            copy.start()

    qkv_acc[...] = jnp.zeros_like(qkv_acc)
    da_acc[...] = jnp.zeros_like(da_acc)
    for at in range(NY):
        for copy in inputs(at):
            copy.wait()
        part = (rows_y + at) % NY
        rows = pl.ds(pl.multiple_of(part * quarter, quarter), quarter)
        qkv_acc[...] += dot_nn(hidden[part], weight[rows, :wide])
        da_acc[...] += dot_nn(grad[part], weight[rows, wide:])

    gain_q = gains_ref[0:1, :]
    gain_k = gains_ref[1:2, :]
    row = lax.broadcasted_iota(jnp.int32, (group, group), 0)
    col = lax.broadcasted_iota(jnp.int32, (group, group), 1)
    clip_tokens = frames * patch_dev
    mask = (
        (row % patch_dev == col % patch_dev)
        & (row // clip_tokens == col // clip_tokens)
        & (col <= row)
    )
    factor = width ** (-0.5)
    for rep in range(replicas):
        rows = slice(rep * group, (rep + 1) * group)
        for head in range(heads):
            base = head * 3 * width
            take = lambda at: qkv_acc[rows, base + at * width : base + (at + 1) * width].astype(
                BF
            )
            q = take(0).astype(F32)
            k = take(1).astype(F32)
            value = take(2)
            d_out = da_acc[rows, head * width : (head + 1) * width].astype(BF)
            inv_q = lax.rsqrt(jnp.mean(q * q, -1, keepdims=True) + EPS)
            inv_k = lax.rsqrt(jnp.mean(k * k, -1, keepdims=True) + EPS)
            q_hat = q * inv_q
            k_hat = k * inv_k
            queries = (q_hat * gain_q).astype(BF)
            keys = (k_hat * gain_k).astype(BF)
            scores = dot_nt(queries, keys) * factor
            weights = jnp.where(mask, jnp.exp(scores), 0.0)
            probs = weights / jnp.sum(weights, -1, keepdims=True)
            probs_bf = probs.astype(BF)
            out = dot_nn(probs_bf, value)
            attended[rows, head * width : (head + 1) * width] = out.astype(BF)
            d_value = dot_tn(probs_bf, d_out)
            d_probs = dot_nt(d_out, value)
            d_scores = probs * (d_probs - jnp.sum(d_probs * probs, -1, keepdims=True))
            d_scores = (d_scores * factor).astype(BF)
            d_q = dot_nn(d_scores, keys) * gain_q
            d_k = dot_tn(d_scores, queries) * gain_k
            d_q = inv_q * (d_q - q_hat * jnp.mean(d_q * q_hat, -1, keepdims=True))
            d_k = inv_k * (d_k - k_hat * jnp.mean(d_k * k_hat, -1, keepdims=True))
            for at, item in enumerate((d_q, d_k, d_value)):
                dqkv[rows, base + at * width : base + (at + 1) * width] = item.astype(BF)

    def outputs(stage, keep, give, base):
        result = []
        for step in range(ring):
            target = (spot_x + step) % ring
            for side, out in enumerate((keep, give)):
                result.append(
                    pltpu.make_async_copy(
                        stage.at[(core + side) % cores, target],
                        out.at[step],
                        out_sems.at[base, step, side],
                    )
                )
        return result

    block = min(quarter, 256)
    for part in range(parts):
        for at in range(quarter // block):
            cols = slice(at * block, (at + 1) * block)
            w_block = weight[part * quarter + at * block : part * quarter + (at + 1) * block, wide:]
            y_block = dot_nt(attended[...], w_block).astype(BF)
            for rep in range(replicas):
                rows = slice(rep * group, (rep + 1) * group)
                y_stage[part % cores, rep * along + part // cores, :, cols] = y_block[rows]
    y_copies = outputs(y_stage, y_keep, y_give, 0)
    for copy in y_copies:
        copy.start()

    for part in range(parts):
        for copy in second(part):
            copy.wait()
    hot = hot_ref[...]
    codes = hot.shape[0]
    tail = dh_stage.shape[2] - group
    lanes = min(block, 128)
    terms = jnp.zeros((tokens, lanes), F32)
    for part in range(parts):
        for at in range(quarter // block):
            cols = slice(at * block, (at + 1) * block)
            w_block = weight[part * quarter + at * block : part * quarter + (at + 1) * block, :wide]
            d_block = dot_nt(dqkv[...], w_block)
            d_rounded = d_block.astype(BF)
            d_scale = dot_nn(hot, (d_block * normed[part, :, cols].astype(F32)).astype(BF))
            d_shift = dot_nn(hot, d_rounded)
            for rep, item in enumerate((d_scale, d_shift)):
                where = (part % cores, rep * along + part // cores)
                rows = slice(rep * group, (rep + 1) * group)
                dh_stage[where[0], where[1], 0:group, cols] = d_rounded[rows]
                dh_stage[where[0], where[1], group : group + codes, cols] = item.astype(BF)
            product = d_block * scaled[part, :, cols].astype(F32)
            for lane in range(block // lanes):
                terms += product[:, lane * lanes : (lane + 1) * lanes]
    ones = jnp.ones((8, lanes), BF)
    high, low = halves(terms)
    high, low = halves(dot_nt(ones, high) + dot_nt(ones, low))
    sub = lax.broadcasted_iota(jnp.int32, (8, group), 0)
    for rep in range(replicas):
        mine = slice(rep * group, (rep + 1) * group)
        both = jnp.where(
            sub == 0,
            high[:, mine].astype(F32),
            jnp.where(sub == 1, low[:, mine].astype(F32), 0.0),
        ).astype(BF)
        for part in range(parts):
            where = (part % cores, rep * along + part // cores)
            dh_stage[where[0], where[1], group + codes :, :] = jnp.zeros(
                (tail - codes, quarter), BF
            )
            dh_stage[where[0], where[1], group + codes : group + codes + 8, 0:group] = both
    dh_copies = outputs(dh_stage, dh_keep, dh_give, 1)
    for copy in dh_copies:
        copy.start()
    for copy in y_copies + dh_copies:
        copy.wait()


def finish_kernel(
    patch_dev,
    code_count,
    parts,
    yk_ref,
    yr_ref,
    ya_ref,
    yb_ref,
    dk_ref,
    dr_ref,
    da_ref,
    db_ref,
    coef_ref,
    xinv_ref,
    xown_ref,
    gown_ref,
    send_ref,
):
    group, quarter = xown_ref.shape
    y = (
        xown_ref[...].astype(F32)
        + (yk_ref[0].astype(F32) + yr_ref[0].astype(F32))
        + (ya_ref[...].astype(F32) + yb_ref[...].astype(F32))
    )
    total = (dk_ref[0].astype(F32) + dr_ref[0].astype(F32)) + (
        da_ref[...].astype(F32) + db_ref[...].astype(F32)
    )
    terms = total[group + code_count : group + code_count + 8, :group]
    term = (terms[0:1] + terms[1:2]) / (quarter * parts)
    term = jnp.broadcast_to(term, (group, group)).T[:, 0:1]
    dx = gown_ref[...].astype(F32) + (total[:group] * coef_ref[...] - xinv_ref[...] * term)
    grads = total[group : group + code_count].astype(BF)
    span = 2 * patch_dev + code_count
    rows = send_ref.shape[0]
    pick_y = selector(
        (rows, group),
        lambda m, n: (m % span < patch_dev) & (m // span * patch_dev + m % span == n),
    )
    pick_d = selector(
        (rows, group),
        lambda m, n: (m % span >= patch_dev)
        & (m % span < 2 * patch_dev)
        & (m // span * patch_dev + m % span - patch_dev == n),
    )
    pick_g = selector((rows, code_count), lambda m, n: m % span - 2 * patch_dev == n)
    send_ref[...] = (
        dot_nn(pick_y, y.astype(BF)) + dot_nn(pick_d, dx.astype(BF)) + dot_nn(pick_g, grads)
    ).astype(BF)


def unpack_kernel(patch_dev, factor, back_ref, y_ref, dx_ref, sum_ref):
    group = y_ref.shape[0]
    rows = back_ref.shape[0]
    codes = sum_ref.shape[0]
    span = 2 * patch_dev + codes
    back = back_ref[...]
    pick_y = selector((group, rows), lambda m, n: m // patch_dev * span + m % patch_dev == n)
    pick_d = selector(
        (group, rows), lambda m, n: m // patch_dev * span + m % patch_dev + patch_dev == n
    )
    pick_g = selector((codes, rows), lambda m, n: n % span - 2 * patch_dev == m)
    y_ref[...] = dot_nn(pick_y, back).astype(BF)
    dx_ref[...] = dot_nn(pick_d, back).astype(BF)
    sum_ref[...] = dot_nn(pick_g, back) * factor


NY = 4
NZ = 8
CORES = 2
VMEM = pl.BlockSpec(memory_space=pltpu.VMEM)
SMEM = pl.BlockSpec(memory_space=pltpu.SMEM)
ANY = pl.BlockSpec(memory_space=pl.ANY)


def fetch(value, dy, dz):
    pairs = []
    for y in range(NY):
        for z in range(NZ):
            pairs.append((((y + dy) % NY) * NZ + (z + dz) % NZ, y * NZ + z))
    return lax.ppermute(value, "tm", pairs)


def fetch_x(value, dx, ring):
    pairs = []
    for x in range(ring):
        for core in range(CORES):
            pairs.append((((x + dx) % ring) * CORES + core, x * CORES + core))
    return lax.ppermute(value, ("replica", "tensor"), pairs)


def swap_cores(value, ring):
    pairs = []
    for x in range(ring):
        for core in range(CORES):
            pairs.append((x * CORES + core, x * CORES + 1 - core))
    return lax.ppermute(value, ("replica", "tensor"), pairs)


def gate(*values):
    return lax.optimization_barrier(values)


def gather_weight(near, far, codes_in, tokens_in, tokens_ready):
    a = near.shape[0]
    b = far.shape[0]
    pieces = []
    plan = []

    def add(value, blocks):
        start = 0
        for size, dy, dz, place in blocks:
            plan.append((len(pieces), start, size, dy % NY, dz % NZ, place))
            start += size
        pieces.append(value)

    def line(dy, *dzs):
        return [(a, dy, dz, 0) for dz in dzs]

    def column(dz, ys=(0, 1, -1, 2)):
        return [(b, dy, dz, a) for dy in ys]

    def pair(value, dzs):
        up, dn = fetch(value, 1, 0), fetch(value, -1, 0)
        add(value, line(0, *dzs))
        add(up, line(1, *dzs))
        add(dn, line(-1, *dzs))
        return up, dn

    def across(up, dn, count, dzs):
        low, high = fetch(up[: count * a], 1, 0), fetch(dn[count * a :], -1, 0)
        add(low, line(2, *dzs[:count]))
        add(high, line(2, *dzs[count:]))
        return low, high

    zu, zd = fetch(near, 0, 1), fetch(near, 0, -1)
    fu, fd, fo = fetch(far, 1, 0), fetch(far, -1, 0), fetch(far, 2, 0)
    codes = codes_in()
    near, far, zu, zd, fu, fd, fo, codes = gate(near, far, zu, zd, fu, fd, fo, codes)
    cols = jnp.concatenate([far, fu, fd, fo], 0)
    add(cols, column(0))
    first_at = (0, 1, -1)
    up1, dn1 = pair(jnp.concatenate([near, zu, zd], 0), first_at)
    zu2, zd2 = fetch(zu, 0, 1), fetch(zd, 0, -1)
    zu3, zd3 = fetch(zu2, 0, 1), fetch(zd2, 0, -1)
    zu2, zd2, zu3, zd3, cols = gate(zu2, zd2, zu3, zd3, cols)
    second_at = (2, -2, 3, -3)
    up2, dn2 = pair(jnp.concatenate([zu2, zd2, zu3, zd3], 0), second_at)
    z4l, z4h = fetch(zu3[: a // 2], 0, 1), fetch(zd3[a // 2 :], 0, -1)
    cu, cd = fetch(cols, 0, 1), fetch(cols, 0, -1)
    token = tokens_in(z4l)
    add(cu, column(1))
    add(cd, column(-1))
    cu2, cd2 = fetch(cu, 0, 1), fetch(cd, 0, -1)
    low, high = across(up1, dn1, 2, first_at)
    up2, dn2, z4l, z4h, cu2, cd2, token, low, high = gate(
        up2, dn2, z4l, z4h, cu2, cd2, token, low, high
    )
    add(cu2, column(2))
    add(cd2, column(-2))
    cu3, cd3 = fetch(cu2, 0, 1), fetch(cd2, 0, -1)
    up3, dn3 = pair(jnp.concatenate([z4l, z4h], 0), (4,))
    across(up2, dn2, 2, second_at)
    add(cu3, column(3))
    add(cd3, column(-3))
    add(fetch(cu3[: 2 * b], 0, 1), column(4, (0, 1)))
    add(fetch(cd3[2 * b :], 0, -1), column(4, (-1, 2)))
    add(fetch(dn3, -1, 0), line(2, 4))
    return pieces, tuple(plan), tokens_ready(token, codes)


def reduce_ring(keep, give, ring):
    got = swap_cores(give, ring)
    rows = keep.shape[1]
    half = rows // 32 * 16

    def both(at, rows_from, rows_to):
        return keep[at, rows_from:rows_to].astype(F32) + got[at, rows_from:rows_to].astype(F32)

    low = fetch_x(both(2, 0, half).astype(BF), -1, ring)
    high = fetch_x(both(2, half, rows).astype(BF), 1, ring)
    up = jnp.concatenate(
        [both(1, 0, half) + low.astype(F32), both(1, half, rows)], 0
    ).astype(BF)
    dn = jnp.concatenate(
        [both(3, 0, half), both(3, half, rows) + high.astype(F32)], 0
    ).astype(BF)
    return keep, got, fetch_x(up, -1, ring), fetch_x(dn, 1, ring)


def shards(
    activations,
    action_codes,
    norm_gain,
    action_scale,
    action_shift,
    qkv_weight,
    qk_gains,
    out_weight,
    grad_output,
):
    replicas = lax.axis_size("replica")
    shards_tm = lax.axis_size("tm")
    parts = lax.axis_size("tensor")
    ring = replicas * parts // CORES
    rep = lax.axis_index("replica")
    part = lax.axis_index("tensor")
    spot = lax.axis_index("tm")
    frames = action_codes.shape[1]
    quarter = activations.shape[2]
    patches = activations.shape[1]
    patch_dev = patches // shards_tm
    depth = qkv_weight.shape[0]
    heads = qkv_weight.shape[1] // replicas
    triple = qkv_weight.shape[2]
    width = triple // 3
    wide = heads * triple
    narrow = heads * width
    code_count = action_scale.shape[0]
    group = shards_tm * patch_dev
    tokens = replicas * group
    near = depth // 8 * 5
    place = jnp.stack(
        [
            rep,
            part,
            spot // NZ,
            spot % NZ,
            rep * (ring // replicas) + part // CORES,
            part % CORES,
        ]
    ).astype(jnp.int32)

    weight_near, weight_far = pl.pallas_call(
        pack_kernel,
        out_shape=(
            jax.ShapeDtypeStruct((near, wide + narrow), BF),
            jax.ShapeDtypeStruct((depth - near, wide + narrow), BF),
        ),
        in_specs=[SMEM] + [VMEM] * 2,
        out_specs=(VMEM, VMEM),
        compiler_params=pltpu.CompilerParams(vmem_limit_bytes=24 * 1024 * 1024),
        name="pack",
    )(place, qkv_weight.reshape(-1, triple), out_weight)

    def tokens_in(hold):
        both = pl.pallas_call(
            functools.partial(tokens_kernel, patch_dev),
            out_shape=jax.ShapeDtypeStruct((2 * patches, quarter), BF),
            in_specs=[VMEM] * 2 + [ANY],
            out_specs=VMEM,
            compiler_params=pltpu.CompilerParams(vmem_limit_bytes=24 * 1024 * 1024),
            name="tokens",
        )(activations.reshape(patches, quarter), grad_output.reshape(patches, quarter), hold)
        return lax.all_to_all(both, "tm", split_axis=0, concat_axis=0, tiled=True)

    def codes_in():
        return lax.ppermute(action_codes, "replica", [(i, 1 - i) for i in range(2)])

    def by_part(table):
        return table.reshape(table.shape[0], parts, quarter).transpose(1, 0, 2)

    big = jax.ShapeDtypeStruct((parts, tokens, quarter), BF)
    big_spec = pl.BlockSpec((parts, group, quarter), lambda i: (0, i, 0))
    own_spec = pl.BlockSpec((group, quarter), lambda i: (0, 0))

    def whole(*shape):
        return pl.BlockSpec(shape, lambda i: (0,) * len(shape))

    def tokens_ready(both, other):
        codes = jnp.where(
            rep == 0,
            jnp.concatenate([action_codes, other], 0),
            jnp.concatenate([other, action_codes], 0),
        ).reshape(-1)
        codes = jnp.repeat(codes, patch_dev)
        code_range = jnp.arange(code_count)
        hot = (codes[:, None] == code_range[None, :]).astype(BF)
        hot_t = (codes[None, :] == code_range[:, None]).astype(BF)
        full = lax.all_gather(both, ("replica", "tensor"), axis=0)
        full = full.reshape(replicas, parts, 2 * group, quarter)
        return hot_t, *pl.pallas_call(
            functools.partial(prep_kernel, patch_dev),
            grid=(replicas,),
            out_shape=(big, big, big, big)
            + (jax.ShapeDtypeStruct((group, quarter), F32),) * 2
            + (jax.ShapeDtypeStruct((group, quarter), BF),) * 2,
            in_specs=[
                SMEM,
                pl.BlockSpec((1, parts, 2 * group, quarter), lambda i: (i, 0, 0, 0)),
                pl.BlockSpec((group, code_count), lambda i: (i, 0)),
                whole(parts, 1, quarter),
                whole(parts, code_count, quarter),
                whole(parts, code_count, quarter),
            ],
            out_specs=(big_spec,) * 4 + (own_spec,) * 4,
            compiler_params=pltpu.CompilerParams(vmem_limit_bytes=48 * 1024 * 1024),
            name="prep",
        )(
            place,
            full,
            hot,
            by_part(norm_gain[None]),
            by_part(action_scale),
            by_part(action_shift),
        )

    pieces, plan, ready = gather_weight(
        weight_near, weight_far, codes_in, tokens_in, tokens_ready
    )
    hot_t, hidden, grad, normed, scaled, coef, xinv, x_own, g_own = ready

    tail_rows = group + EXTRA
    y_shape = jax.ShapeDtypeStruct((ring, group, quarter), BF)
    dh_shape = jax.ShapeDtypeStruct((ring, tail_rows, quarter), BF)
    flops = 4 * tokens * parts * quarter * (wide + narrow)
    moved = 2 * parts * quarter * (wide + narrow + 6 * tokens)
    y_keep, y_give, dh_keep, dh_give = pl.pallas_call(
        functools.partial(block_kernel, patch_dev, frames, plan),
        out_shape=(y_shape, y_shape, dh_shape, dh_shape),
        in_specs=[SMEM, VMEM, VMEM] + [ANY] * (4 + len(pieces)),
        out_specs=(ANY,) * 4,
        scratch_shapes=[
            pltpu.VMEM((parts, tokens, quarter), BF),
            pltpu.VMEM((parts, tokens, quarter), BF),
            pltpu.VMEM((parts, tokens, quarter), BF),
            pltpu.VMEM((parts, tokens, quarter), BF),
            pltpu.VMEM((parts * quarter, wide + narrow), BF),
            pltpu.VMEM((tokens, wide), F32),
            pltpu.VMEM((tokens, narrow), F32),
            pltpu.VMEM((tokens, narrow), BF),
            pltpu.VMEM((tokens, wide), BF),
            pltpu.VMEM((CORES, ring, group, quarter), BF),
            pltpu.VMEM((CORES, ring, tail_rows, quarter), BF),
            pltpu.SemaphoreType.DMA((parts, 4)),
            pltpu.SemaphoreType.DMA((len(plan),)),
            pltpu.SemaphoreType.DMA((2, ring, CORES)),
        ],
        compiler_params=pltpu.CompilerParams(vmem_limit_bytes=52 * 1024 * 1024),
        cost_estimate=pl.CostEstimate(flops=flops, bytes_accessed=moved, transcendentals=0),
        name="block",
    )(place, qk_gains, hot_t, hidden, grad, normed, scaled, *pieces)

    dh_terms = reduce_ring(dh_keep, dh_give, ring)
    y_terms = reduce_ring(y_keep, y_give, ring)
    first_y = pl.BlockSpec((1, group, quarter), lambda i: (0, 0, 0))
    first_dh = pl.BlockSpec((1, tail_rows, quarter), lambda i: (0, 0, 0))
    span = 2 * patch_dev + code_count
    send = pl.pallas_call(
        functools.partial(finish_kernel, patch_dev, code_count, parts),
        grid=(1,),
        out_shape=jax.ShapeDtypeStruct((shards_tm * span, quarter), BF),
        in_specs=[first_y] * 2
        + [whole(group, quarter)] * 2
        + [first_dh] * 2
        + [whole(tail_rows, quarter)] * 2
        + [whole(group, quarter)] * 4,
        out_specs=whole(shards_tm * span, quarter),
        compiler_params=pltpu.CompilerParams(vmem_limit_bytes=24 * 1024 * 1024),
        name="finish",
    )(*y_terms, *dh_terms, coef, xinv, x_own, g_own)
    back = lax.all_to_all(send, "tm", split_axis=0, concat_axis=0, tiled=True)
    token_total = tokens * shards_tm
    y_frames, dx_frames, grad_mine = pl.pallas_call(
        functools.partial(unpack_kernel, patch_dev, token_total ** (-0.5)),
        out_shape=(
            jax.ShapeDtypeStruct((group, quarter), BF),
            jax.ShapeDtypeStruct((group, quarter), BF),
            jax.ShapeDtypeStruct((code_count, quarter), F32),
        ),
        in_specs=[VMEM],
        out_specs=(VMEM, VMEM, VMEM),
        compiler_params=pltpu.CompilerParams(vmem_limit_bytes=24 * 1024 * 1024),
        name="unpack",
    )(back)
    grad_other = lax.ppermute(grad_mine, "replica", [(i, 1 - i) for i in range(2)])
    d_scale = jnp.where(rep == 0, grad_mine, grad_other)
    d_shift = jnp.where(rep == 0, grad_other, grad_mine)
    return (y_frames[None], dx_frames[None], d_scale, d_shift)


def solution(mesh):
    placed = (
        P(("replica", "tm"), None, "tensor"),
        P("replica", None),
        P(),
        P(),
        P(),
        P("tm", "tensor", None),
        P(),
        P("tensor", None, "tm"),
        P(("replica", "tm"), None, "tensor"),
    )
    return jax.shard_map(
        shards,
        mesh=mesh,
        in_specs=placed,
        out_specs=(
            P(("replica", "tm"), None, "tensor"),
            P(("replica", "tm"), None, "tensor"),
            P(None, "tensor"),
            P(None, "tensor"),
        ),
        check_vma=False,
    )
```

```python
import functools

import jax
import jax.numpy as jnp
from jax import lax
from jax.experimental import pallas as pl
from jax.experimental.pallas import tpu as pltpu
from jax.sharding import PartitionSpec as P

EPS = 1e-06
BF = jnp.bfloat16
F32 = jnp.float32
EXTRA = 16


def dot_nn(a, b):
    return lax.dot_general(a, b, (((1,), (0,)), ((), ())), preferred_element_type=F32)


def dot_nt(a, b):
    return lax.dot_general(a, b, (((1,), (1,)), ((), ())), preferred_element_type=F32)


def dot_tn(a, b):
    return lax.dot_general(a, b, (((0,), (0,)), ((), ())), preferred_element_type=F32)


def halves(value):
    high = value.astype(BF)
    return high, (value - high.astype(F32)).astype(BF)


def selector(shape, pick):
    row = lax.broadcasted_iota(jnp.int32, shape, 0)
    col = lax.broadcasted_iota(jnp.int32, shape, 1)
    return jnp.where(pick(row, col), 1.0, 0.0).astype(BF)


def tokens_kernel(patch_dev, x_ref, g_ref, hold_ref, both_ref):
    rows = x_ref.shape[0]
    pair = 2 * patch_dev
    pick_x = selector(
        (2 * rows, rows),
        lambda m, n: (m % pair < patch_dev) & (m // pair * patch_dev + m % pair == n),
    )
    pick_g = selector(
        (2 * rows, rows),
        lambda m, n: (m % pair >= patch_dev)
        & (m // pair * patch_dev + m % pair - patch_dev == n),
    )
    both_ref[...] = (dot_nn(pick_x, x_ref[...]) + dot_nn(pick_g, g_ref[...])).astype(BF)


def pack_kernel(place_ref, qkv_ref, out_ref, near_ref, far_ref):
    depth = near_ref.shape[0] + far_ref.shape[0]
    near = near_ref.shape[0]
    all_heads = qkv_ref.shape[0] // depth
    heads = out_ref.shape[0] // 2
    triple = qkv_ref.shape[1]
    width = triple // 3
    rep = place_ref[0]
    for head in range(heads):
        own = rep * heads + head
        pick = selector(
            (depth, all_heads * depth),
            lambda m, n: m * all_heads + own == n,
        )
        part = dot_nn(pick, qkv_ref[...]).astype(BF)
        cols = slice(head * triple, (head + 1) * triple)
        near_ref[:, cols] = part[:near]
        far_ref[:, cols] = part[near:]
        eye = selector((depth, depth), lambda m, n: m == n)
        part = dot_nt(eye, out_ref[own]).astype(BF)
        cols = slice(heads * triple + head * width, heads * triple + (head + 1) * width)
        near_ref[:, cols] = part[:near]
        far_ref[:, cols] = part[near:]


def prep_kernel(
    patch_dev,
    place_ref,
    full_ref,
    hot_ref,
    gain_ref,
    scale_ref,
    shift_ref,
    hidden_ref,
    grad_ref,
    normed_ref,
    coef_ref,
    xinv_ref,
    xown_ref,
    gown_ref,
):
    parts = full_ref.shape[1]
    group = hidden_ref.shape[1]
    quarter = full_ref.shape[3]
    pair = 2 * patch_dev
    pick_x = selector(
        (group, 2 * group), lambda m, n: m // patch_dev * pair + m % patch_dev == n
    )
    pick_g = selector(
        (group, 2 * group), lambda m, n: m // patch_dev * pair + m % patch_dev + patch_dev == n
    )
    hot = hot_ref[...]

    def rows_of(table):
        high, low = halves(table)
        return dot_nn(hot, high) + dot_nn(hot, low)

    square = jnp.zeros((group, 1), F32)
    for part in range(parts):
        x = dot_nn(pick_x, full_ref[0, part])
        square += jnp.sum(x * x, -1, keepdims=True)
    inverse = lax.rsqrt(square / (parts * quarter) + EPS)
    for part in range(parts):
        x = dot_nn(pick_x, full_ref[0, part])
        normed = x * inverse * gain_ref[part]
        scaled = normed * (1.0 + rows_of(scale_ref[part]))
        hidden_ref[part] = (scaled + rows_of(shift_ref[part])).astype(BF)
        normed_ref[part] = normed.astype(BF)
        grad_ref[part] = dot_nn(pick_g, full_ref[0, part]).astype(BF)

    @pl.when(pl.program_id(0) == place_ref[0])
    def _():
        own = place_ref[1]
        rows = full_ref[0, own]
        x = dot_nn(pick_x, rows)
        xown_ref[...] = x.astype(BF)
        gown_ref[...] = dot_nn(pick_g, rows).astype(BF)
        coef_ref[...] = inverse * (1.0 + rows_of(scale_ref[own])) * gain_ref[own]
        xinv_ref[...] = x * inverse * inverse


def block_kernel(
    patch_dev,
    frames,
    plan,
    place_ref,
    gains_ref,
    hot_ref,
    shift_ref,
    hidden_hbm,
    grad_hbm,
    normed_hbm,
    *refs,
):
    count = 1 + max(item[0] for item in plan)
    pieces = refs[:count]
    (
        y_keep,
        y_give,
        dh_keep,
        dh_give,
        hidden,
        grad,
        normed,
        weight,
        qkv_acc,
        da_acc,
        attended,
        dqkv,
        y_stage,
        dh_stage,
        sems,
        weight_sems,
        out_sems,
    ) = refs[count:]
    parts, tokens, quarter = grad.shape
    codes = hot_ref.shape[0]
    width = gains_ref.shape[1]
    wide = qkv_acc.shape[1]
    heads = wide // (3 * width)
    cores, ring, group, _ = y_stage.shape
    replicas = tokens // group
    along = ring // replicas
    rows_y = place_ref[2]
    rows_z = place_ref[3]
    spot_x = place_ref[4]
    core = place_ref[5]
    depth = weight.shape[0] // (NY * NZ)

    def inputs(at):
        part = (rows_y + at) % NY
        result = [
            pltpu.make_async_copy(
                hidden_hbm.at[part], hidden.at[part, pl.ds(0, tokens)], sems.at[at, 0]
            ),
            pltpu.make_async_copy(grad_hbm.at[part], grad.at[part], sems.at[at, 1]),
        ]
        for number, (index, start, size, dy, dz, place) in enumerate(plan):
            if dy == at:
                owner = part * NZ + (rows_z + dz) % NZ
                target = pl.multiple_of(owner * depth + place, 16)
                result.append(
                    pltpu.make_async_copy(
                        pieces[index].at[pl.ds(start, size)],
                        weight.at[pl.ds(target, size)],
                        weight_sems.at[number],
                    )
                )
        return result

    def second(part):
        return [pltpu.make_async_copy(normed_hbm.at[part], normed.at[part], sems.at[part, 2])]

    for at in range(NY):
        for copy in inputs(at):
            copy.start()
    for part in range(parts):
        for copy in second(part):
            copy.start()

    hidden[:, tokens:, :] = shift_ref[...]
    qkv_acc[...] = jnp.zeros_like(qkv_acc)
    da_acc[...] = jnp.zeros_like(da_acc)
    for at in range(NY):
        for copy in inputs(at):
            copy.wait()
        part = (rows_y + at) % NY
        rows = pl.ds(pl.multiple_of(part * quarter, quarter), quarter)
        qkv_acc[...] += dot_nn(hidden[part], weight[rows, :wide])
        da_acc[...] += dot_nn(grad[part], weight[rows, wide:])

    gain_q = gains_ref[0:1, :]
    gain_k = gains_ref[1:2, :]
    row = lax.broadcasted_iota(jnp.int32, (group, group), 0)
    col = lax.broadcasted_iota(jnp.int32, (group, group), 1)
    clip_tokens = frames * patch_dev
    mask = (
        (row % patch_dev == col % patch_dev)
        & (row // clip_tokens == col // clip_tokens)
        & (col <= row)
    )
    factor = width ** (-0.5)
    for rep in range(replicas):
        rows = slice(rep * group, (rep + 1) * group)
        for head in range(heads):
            base = head * 3 * width
            take = lambda at: qkv_acc[rows, base + at * width : base + (at + 1) * width].astype(
                BF
            )
            q = take(0).astype(F32)
            k = take(1).astype(F32)
            value = take(2)
            d_out = da_acc[rows, head * width : (head + 1) * width].astype(BF)
            inv_q = lax.rsqrt(jnp.mean(q * q, -1, keepdims=True) + EPS)
            inv_k = lax.rsqrt(jnp.mean(k * k, -1, keepdims=True) + EPS)
            q_hat = q * inv_q
            k_hat = k * inv_k
            queries = (q_hat * gain_q).astype(BF)
            keys = (k_hat * gain_k).astype(BF)
            scores = dot_nt(queries, keys) * factor
            weights = jnp.where(mask, jnp.exp(scores), 0.0)
            probs = weights / jnp.sum(weights, -1, keepdims=True)
            probs_bf = probs.astype(BF)
            out = dot_nn(probs_bf, value)
            attended[rows, head * width : (head + 1) * width] = out.astype(BF)
            d_value = dot_tn(probs_bf, d_out)
            d_probs = dot_nt(d_out, value)
            d_scores = probs * (d_probs - jnp.sum(d_probs * probs, -1, keepdims=True))
            d_scores = (d_scores * factor).astype(BF)
            d_q = dot_nn(d_scores, keys) * gain_q
            d_k = dot_tn(d_scores, queries) * gain_k
            d_q = inv_q * (d_q - q_hat * jnp.mean(d_q * q_hat, -1, keepdims=True))
            d_k = inv_k * (d_k - k_hat * jnp.mean(d_k * k_hat, -1, keepdims=True))
            for at, item in enumerate((d_q, d_k, d_value)):
                dqkv[rows, base + at * width : base + (at + 1) * width] = item.astype(BF)

    hot = hot_ref[...]
    lanes = min(wide, 128)
    terms = jnp.zeros((tokens, lanes), F32)
    for lane in range(wide // lanes):
        cols = slice(lane * lanes, (lane + 1) * lanes)
        terms += dqkv[:tokens, cols].astype(F32) * qkv_acc[:tokens, cols]
    ones = jnp.ones((8, lanes), BF)
    high, low = halves(terms)
    terms = dot_nt(ones, high) + dot_nt(ones, low)
    moved = qkv_acc[tokens : tokens + codes] + qkv_acc[tokens + codes :]
    high, low = halves(moved)
    moved = dot_nt(high, dqkv[:tokens]) + dot_nt(low, dqkv[:tokens])
    terms -= jnp.sum(moved * hot.astype(F32), 0, keepdims=True)
    high, low = halves(dot_nn(hot, dqkv[:tokens]))
    dqkv[tokens:, :] = jnp.concatenate([high, low], 0)

    def outputs(stage, keep, give, base):
        result = []
        for step in range(ring):
            target = (spot_x + step) % ring
            for side, out in enumerate((keep, give)):
                result.append(
                    pltpu.make_async_copy(
                        stage.at[(core + side) % cores, target],
                        out.at[step],
                        out_sems.at[base, step, side],
                    )
                )
        return result

    block = min(quarter, 256)
    for part in range(parts):
        for at in range(quarter // block):
            cols = slice(at * block, (at + 1) * block)
            w_block = weight[part * quarter + at * block : part * quarter + (at + 1) * block, wide:]
            y_block = dot_nt(attended[...], w_block).astype(BF)
            for rep in range(replicas):
                rows = slice(rep * group, (rep + 1) * group)
                y_stage[part % cores, rep * along + part // cores, :, cols] = y_block[rows]
    y_copies = outputs(y_stage, y_keep, y_give, 0)
    for copy in y_copies:
        copy.start()

    for part in range(parts):
        for copy in second(part):
            copy.wait()
    tail = dh_stage.shape[2] - group
    for part in range(parts):
        for at in range(quarter // block):
            cols = slice(at * block, (at + 1) * block)
            w_block = weight[part * quarter + at * block : part * quarter + (at + 1) * block, :wide]
            d_block = dot_nt(dqkv[...], w_block)
            d_shift = d_block[tokens : tokens + codes] + d_block[tokens + codes :]
            d_block = d_block[:tokens]
            d_rounded = d_block.astype(BF)
            d_scale = dot_nn(hot, (d_block * normed[part, :, cols].astype(F32)).astype(BF))
            for rep, item in enumerate((d_scale, d_shift)):
                where = (part % cores, rep * along + part // cores)
                rows = slice(rep * group, (rep + 1) * group)
                dh_stage[where[0], where[1], 0:group, cols] = d_rounded[rows]
                dh_stage[where[0], where[1], group : group + codes, cols] = item.astype(BF)
    high, low = halves(terms)
    sub = lax.broadcasted_iota(jnp.int32, (8, group), 0)
    for rep in range(replicas):
        mine = slice(rep * group, (rep + 1) * group)
        both = jnp.where(
            sub == 0,
            high[:, mine].astype(F32),
            jnp.where(sub == 1, low[:, mine].astype(F32), 0.0),
        ).astype(BF)
        for part in range(parts):
            where = (part % cores, rep * along + part // cores)
            dh_stage[where[0], where[1], group + codes :, :] = jnp.zeros(
                (tail - codes, quarter), BF
            )
            dh_stage[where[0], where[1], group + codes : group + codes + 8, 0:group] = both
    dh_copies = outputs(dh_stage, dh_keep, dh_give, 1)
    for copy in dh_copies:
        copy.start()
    for copy in y_copies + dh_copies:
        copy.wait()


def finish_kernel(
    patch_dev,
    code_count,
    parts,
    yk_ref,
    yr_ref,
    ya_ref,
    yb_ref,
    dk_ref,
    dr_ref,
    da_ref,
    db_ref,
    coef_ref,
    xinv_ref,
    xown_ref,
    gown_ref,
    send_ref,
):
    group, quarter = xown_ref.shape
    y = (
        xown_ref[...].astype(F32)
        + (yk_ref[0].astype(F32) + yr_ref[0].astype(F32))
        + (ya_ref[...].astype(F32) + yb_ref[...].astype(F32))
    )
    total = (dk_ref[0].astype(F32) + dr_ref[0].astype(F32)) + (
        da_ref[...].astype(F32) + db_ref[...].astype(F32)
    )
    terms = total[group + code_count : group + code_count + 8, :group]
    term = (terms[0:1] + terms[1:2]) / (quarter * parts)
    term = jnp.broadcast_to(term, (group, group)).T[:, 0:1]
    dx = gown_ref[...].astype(F32) + (total[:group] * coef_ref[...] - xinv_ref[...] * term)
    grads = total[group : group + code_count].astype(BF)
    span = 2 * patch_dev + code_count
    rows = send_ref.shape[0]
    pick_y = selector(
        (rows, group),
        lambda m, n: (m % span < patch_dev) & (m // span * patch_dev + m % span == n),
    )
    pick_d = selector(
        (rows, group),
        lambda m, n: (m % span >= patch_dev)
        & (m % span < 2 * patch_dev)
        & (m // span * patch_dev + m % span - patch_dev == n),
    )
    pick_g = selector((rows, code_count), lambda m, n: m % span - 2 * patch_dev == n)
    send_ref[...] = (
        dot_nn(pick_y, y.astype(BF)) + dot_nn(pick_d, dx.astype(BF)) + dot_nn(pick_g, grads)
    ).astype(BF)


def unpack_kernel(patch_dev, factor, back_ref, y_ref, dx_ref, sum_ref):
    group = y_ref.shape[0]
    rows = back_ref.shape[0]
    codes = sum_ref.shape[0]
    span = 2 * patch_dev + codes
    back = back_ref[...]
    pick_y = selector((group, rows), lambda m, n: m // patch_dev * span + m % patch_dev == n)
    pick_d = selector(
        (group, rows), lambda m, n: m // patch_dev * span + m % patch_dev + patch_dev == n
    )
    pick_g = selector((codes, rows), lambda m, n: n % span - 2 * patch_dev == m)
    y_ref[...] = dot_nn(pick_y, back).astype(BF)
    dx_ref[...] = dot_nn(pick_d, back).astype(BF)
    sum_ref[...] = dot_nn(pick_g, back) * factor


NY = 4
NZ = 8
CORES = 2
VMEM = pl.BlockSpec(memory_space=pltpu.VMEM)
SMEM = pl.BlockSpec(memory_space=pltpu.SMEM)
ANY = pl.BlockSpec(memory_space=pl.ANY)


def fetch(value, dy, dz):
    pairs = []
    for y in range(NY):
        for z in range(NZ):
            pairs.append((((y + dy) % NY) * NZ + (z + dz) % NZ, y * NZ + z))
    return lax.ppermute(value, "tm", pairs)


def fetch_x(value, dx, ring):
    pairs = []
    for x in range(ring):
        for core in range(CORES):
            pairs.append((((x + dx) % ring) * CORES + core, x * CORES + core))
    return lax.ppermute(value, ("replica", "tensor"), pairs)


def swap_cores(value, ring):
    pairs = []
    for x in range(ring):
        for core in range(CORES):
            pairs.append((x * CORES + core, x * CORES + 1 - core))
    return lax.ppermute(value, ("replica", "tensor"), pairs)


def gate(*values):
    return lax.optimization_barrier(values)


def gather_weight(near, far, codes_in, tokens_in, tokens_ready):
    a = near.shape[0]
    b = far.shape[0]
    pieces = []
    plan = []

    def add(value, blocks):
        start = 0
        for size, dy, dz, place in blocks:
            plan.append((len(pieces), start, size, dy % NY, dz % NZ, place))
            start += size
        pieces.append(value)

    def line(dy, *dzs):
        return [(a, dy, dz, 0) for dz in dzs]

    def column(dz, ys=(0, 1, -1, 2)):
        return [(b, dy, dz, a) for dy in ys]

    def pair(value, dzs):
        up, dn = fetch(value, 1, 0), fetch(value, -1, 0)
        add(value, line(0, *dzs))
        add(up, line(1, *dzs))
        add(dn, line(-1, *dzs))
        return up, dn

    zu, zd = fetch(near, 0, 1), fetch(near, 0, -1)
    fu, fd, fo = fetch(far, 1, 0), fetch(far, -1, 0), fetch(far, 2, 0)
    codes = codes_in()
    near, far, zu, zd, fu, fd, fo, codes = gate(near, far, zu, zd, fu, fd, fo, codes)
    cols = jnp.concatenate([far, fu, fd, fo], 0)
    add(cols, column(0))
    first_at = (0, 1, -1)
    up1, dn1 = pair(jnp.concatenate([near, zu, zd], 0), first_at)
    zu2, zd2 = fetch(zu, 0, 1), fetch(zd, 0, -1)
    zu3, zd3 = fetch(zu2, 0, 1), fetch(zd2, 0, -1)
    z4 = fetch(zu3, 0, 1)
    up1, dn1, zu2, zd2, zu3, zd3, z4, cols = gate(up1, dn1, zu2, zd2, zu3, zd3, z4, cols)
    second_at = (2, -2, 3)
    up2, dn2 = pair(jnp.concatenate([zu2, zd2, zu3], 0), second_at)
    cu, cd = fetch(cols, 0, 1), fetch(cols, 0, -1)
    token = tokens_in(zu2)
    up2, dn2, cu, cd, token = gate(up2, dn2, cu, cd, token)
    add(cu, column(1))
    add(cd, column(-1))
    third_at = (-3, 4)
    up3, dn3 = pair(jnp.concatenate([zd3, z4], 0), third_at)
    cu2, cd2 = fetch(cu, 0, 1), fetch(cd, 0, -1)
    up3, dn3, cu2, cd2 = gate(up3, dn3, cu2, cd2)
    add(cu2, column(2))
    add(cd2, column(-2))
    cu3, cd3 = fetch(cu2, 0, 1), fetch(cd2, 0, -1)
    x1, x2 = fetch(up1, 1, 0), fetch(dn2, -1, 0)
    add(x1, line(2, *first_at))
    add(x2, line(2, *second_at))
    cu3, cd3, x1, x2 = gate(cu3, cd3, x1, x2)
    add(cu3, column(3))
    add(cd3, column(-3))
    add(fetch(cu3[: 2 * b], 0, 1), column(4, (0, 1)))
    add(fetch(cd3[2 * b :], 0, -1), column(4, (-1, 2)))
    add(fetch(up3[:a], 1, 0), line(2, -3))
    add(fetch(dn3[a:], -1, 0), line(2, 4))
    return pieces, tuple(plan), tokens_ready(token, codes)


def reduce_ring(keep, give, ring):
    got = swap_cores(give, ring)
    rows = keep.shape[1]
    half = rows // 32 * 16

    def both(at, rows_from, rows_to):
        return keep[at, rows_from:rows_to].astype(F32) + got[at, rows_from:rows_to].astype(F32)

    low = fetch_x(both(2, 0, half).astype(BF), -1, ring)
    high = fetch_x(both(2, half, rows).astype(BF), 1, ring)
    up = jnp.concatenate(
        [both(1, 0, half) + low.astype(F32), both(1, half, rows)], 0
    ).astype(BF)
    dn = jnp.concatenate(
        [both(3, 0, half), both(3, half, rows) + high.astype(F32)], 0
    ).astype(BF)
    return keep, got, fetch_x(up, -1, ring), fetch_x(dn, 1, ring)


def shards(
    activations,
    action_codes,
    norm_gain,
    action_scale,
    action_shift,
    qkv_weight,
    qk_gains,
    out_weight,
    grad_output,
):
    replicas = lax.axis_size("replica")
    shards_tm = lax.axis_size("tm")
    parts = lax.axis_size("tensor")
    ring = replicas * parts // CORES
    rep = lax.axis_index("replica")
    part = lax.axis_index("tensor")
    spot = lax.axis_index("tm")
    frames = action_codes.shape[1]
    quarter = activations.shape[2]
    patches = activations.shape[1]
    patch_dev = patches // shards_tm
    depth = qkv_weight.shape[0]
    heads = qkv_weight.shape[1] // replicas
    triple = qkv_weight.shape[2]
    width = triple // 3
    wide = heads * triple
    narrow = heads * width
    code_count = action_scale.shape[0]
    group = shards_tm * patch_dev
    tokens = replicas * group
    near = depth // 8 * 5
    place = jnp.stack(
        [
            rep,
            part,
            spot // NZ,
            spot % NZ,
            rep * (ring // replicas) + part // CORES,
            part % CORES,
        ]
    ).astype(jnp.int32)

    weight_near, weight_far = pl.pallas_call(
        pack_kernel,
        out_shape=(
            jax.ShapeDtypeStruct((near, wide + narrow), BF),
            jax.ShapeDtypeStruct((depth - near, wide + narrow), BF),
        ),
        in_specs=[SMEM] + [VMEM] * 2,
        out_specs=(VMEM, VMEM),
        compiler_params=pltpu.CompilerParams(vmem_limit_bytes=24 * 1024 * 1024),
        name="pack",
    )(place, qkv_weight.reshape(-1, triple), out_weight)

    def tokens_in(hold):
        both = pl.pallas_call(
            functools.partial(tokens_kernel, patch_dev),
            out_shape=jax.ShapeDtypeStruct((2 * patches, quarter), BF),
            in_specs=[VMEM] * 2 + [ANY],
            out_specs=VMEM,
            compiler_params=pltpu.CompilerParams(vmem_limit_bytes=24 * 1024 * 1024),
            name="tokens",
        )(activations.reshape(patches, quarter), grad_output.reshape(patches, quarter), hold)
        return lax.all_to_all(both, "tm", split_axis=0, concat_axis=0, tiled=True)

    def codes_in():
        return lax.ppermute(action_codes, "replica", [(i, 1 - i) for i in range(2)])

    def by_part(table):
        return table.reshape(table.shape[0], parts, quarter).transpose(1, 0, 2)

    big = jax.ShapeDtypeStruct((parts, tokens, quarter), BF)
    big_spec = pl.BlockSpec((parts, group, quarter), lambda i: (0, i, 0))
    own_spec = pl.BlockSpec((group, quarter), lambda i: (0, 0))

    def whole(*shape):
        return pl.BlockSpec(shape, lambda i: (0,) * len(shape))

    def tokens_ready(both, other):
        codes = jnp.where(
            rep == 0,
            jnp.concatenate([action_codes, other], 0),
            jnp.concatenate([other, action_codes], 0),
        ).reshape(-1)
        codes = jnp.repeat(codes, patch_dev)
        code_range = jnp.arange(code_count)
        hot = (codes[:, None] == code_range[None, :]).astype(BF)
        hot_t = (codes[None, :] == code_range[:, None]).astype(BF)
        full = lax.all_gather(both, ("replica", "tensor"), axis=0)
        full = full.reshape(replicas, parts, 2 * group, quarter)
        return hot_t, *pl.pallas_call(
            functools.partial(prep_kernel, patch_dev),
            grid=(replicas,),
            out_shape=(big, big, big)
            + (jax.ShapeDtypeStruct((group, quarter), F32),) * 2
            + (jax.ShapeDtypeStruct((group, quarter), BF),) * 2,
            in_specs=[
                SMEM,
                pl.BlockSpec((1, parts, 2 * group, quarter), lambda i: (i, 0, 0, 0)),
                pl.BlockSpec((group, code_count), lambda i: (i, 0)),
                whole(parts, 1, quarter),
                whole(parts, code_count, quarter),
                whole(parts, code_count, quarter),
            ],
            out_specs=(big_spec,) * 3 + (own_spec,) * 4,
            compiler_params=pltpu.CompilerParams(vmem_limit_bytes=48 * 1024 * 1024),
            name="prep",
        )(
            place,
            full,
            hot,
            by_part(norm_gain[None]),
            by_part(action_scale),
            by_part(action_shift),
        )

    pieces, plan, ready = gather_weight(
        weight_near, weight_far, codes_in, tokens_in, tokens_ready
    )
    hot_t, hidden, grad, normed, coef, xinv, x_own, g_own = ready

    shift_halves = jnp.concatenate(halves(by_part(action_shift)), 1)
    tail_rows = group + EXTRA
    y_shape = jax.ShapeDtypeStruct((ring, group, quarter), BF)
    dh_shape = jax.ShapeDtypeStruct((ring, tail_rows, quarter), BF)
    flops = 4 * tokens * parts * quarter * (wide + narrow)
    moved = 2 * parts * quarter * (wide + narrow + 5 * tokens)
    y_keep, y_give, dh_keep, dh_give = pl.pallas_call(
        functools.partial(block_kernel, patch_dev, frames, plan),
        out_shape=(y_shape, y_shape, dh_shape, dh_shape),
        in_specs=[SMEM, VMEM, VMEM, VMEM] + [ANY] * (3 + len(pieces)),
        out_specs=(ANY,) * 4,
        scratch_shapes=[
            pltpu.VMEM((parts, tokens + 2 * code_count, quarter), BF),
            pltpu.VMEM((parts, tokens, quarter), BF),
            pltpu.VMEM((parts, tokens, quarter), BF),
            pltpu.VMEM((parts * quarter, wide + narrow), BF),
            pltpu.VMEM((tokens + 2 * code_count, wide), F32),
            pltpu.VMEM((tokens, narrow), F32),
            pltpu.VMEM((tokens, narrow), BF),
            pltpu.VMEM((tokens + 2 * code_count, wide), BF),
            pltpu.VMEM((CORES, ring, group, quarter), BF),
            pltpu.VMEM((CORES, ring, tail_rows, quarter), BF),
            pltpu.SemaphoreType.DMA((parts, 3)),
            pltpu.SemaphoreType.DMA((len(plan),)),
            pltpu.SemaphoreType.DMA((2, ring, CORES)),
        ],
        compiler_params=pltpu.CompilerParams(vmem_limit_bytes=52 * 1024 * 1024),
        cost_estimate=pl.CostEstimate(flops=flops, bytes_accessed=moved, transcendentals=0),
        name="block",
    )(place, qk_gains, hot_t, shift_halves, hidden, grad, normed, *pieces)

    dh_terms = reduce_ring(dh_keep, dh_give, ring)
    y_terms = reduce_ring(y_keep, y_give, ring)
    first_y = pl.BlockSpec((1, group, quarter), lambda i: (0, 0, 0))
    first_dh = pl.BlockSpec((1, tail_rows, quarter), lambda i: (0, 0, 0))
    span = 2 * patch_dev + code_count
    send = pl.pallas_call(
        functools.partial(finish_kernel, patch_dev, code_count, parts),
        grid=(1,),
        out_shape=jax.ShapeDtypeStruct((shards_tm * span, quarter), BF),
        in_specs=[first_y] * 2
        + [whole(group, quarter)] * 2
        + [first_dh] * 2
        + [whole(tail_rows, quarter)] * 2
        + [whole(group, quarter)] * 4,
        out_specs=whole(shards_tm * span, quarter),
        compiler_params=pltpu.CompilerParams(vmem_limit_bytes=24 * 1024 * 1024),
        name="finish",
    )(*y_terms, *dh_terms, coef, xinv, x_own, g_own)
    back = lax.all_to_all(send, "tm", split_axis=0, concat_axis=0, tiled=True)
    token_total = tokens * shards_tm
    y_frames, dx_frames, grad_mine = pl.pallas_call(
        functools.partial(unpack_kernel, patch_dev, token_total ** (-0.5)),
        out_shape=(
            jax.ShapeDtypeStruct((group, quarter), BF),
            jax.ShapeDtypeStruct((group, quarter), BF),
            jax.ShapeDtypeStruct((code_count, quarter), F32),
        ),
        in_specs=[VMEM],
        out_specs=(VMEM, VMEM, VMEM),
        compiler_params=pltpu.CompilerParams(vmem_limit_bytes=24 * 1024 * 1024),
        name="unpack",
    )(back)
    grad_other = lax.ppermute(grad_mine, "replica", [(i, 1 - i) for i in range(2)])
    d_scale = jnp.where(rep == 0, grad_mine, grad_other)
    d_shift = jnp.where(rep == 0, grad_other, grad_mine)
    return (y_frames[None], dx_frames[None], d_scale, d_shift)


def solution(mesh):
    placed = (
        P(("replica", "tm"), None, "tensor"),
        P("replica", None),
        P(),
        P(),
        P(),
        P("tm", "tensor", None),
        P(),
        P("tensor", None, "tm"),
        P(("replica", "tm"), None, "tensor"),
    )
    return jax.shard_map(
        shards,
        mesh=mesh,
        in_specs=placed,
        out_specs=(
            P(("replica", "tm"), None, "tensor"),
            P(("replica", "tm"), None, "tensor"),
            P(None, "tensor"),
            P(None, "tensor"),
        ),
        check_vma=False,
    )
```

```python
import functools

import jax
import jax.numpy as jnp
from jax import lax
from jax.experimental import pallas as pl
from jax.experimental.pallas import tpu as pltpu
from jax.sharding import PartitionSpec as P

EPS = 1e-06
BF = jnp.bfloat16
F32 = jnp.float32
EXTRA = 16


def dot_nn(a, b):
    return lax.dot_general(a, b, (((1,), (0,)), ((), ())), preferred_element_type=F32)


def dot_nt(a, b):
    return lax.dot_general(a, b, (((1,), (1,)), ((), ())), preferred_element_type=F32)


def dot_tn(a, b):
    return lax.dot_general(a, b, (((0,), (0,)), ((), ())), preferred_element_type=F32)


def halves(value):
    high = value.astype(BF)
    return high, (value - high.astype(F32)).astype(BF)


def selector(shape, pick):
    row = lax.broadcasted_iota(jnp.int32, shape, 0)
    col = lax.broadcasted_iota(jnp.int32, shape, 1)
    return jnp.where(pick(row, col), 1.0, 0.0).astype(BF)


def tokens_kernel(patch_dev, x_ref, g_ref, hold_ref, both_ref):
    rows = x_ref.shape[0]
    pair = 2 * patch_dev
    pick_x = selector(
        (2 * rows, rows),
        lambda m, n: (m % pair < patch_dev) & (m // pair * patch_dev + m % pair == n),
    )
    pick_g = selector(
        (2 * rows, rows),
        lambda m, n: (m % pair >= patch_dev)
        & (m // pair * patch_dev + m % pair - patch_dev == n),
    )
    both_ref[...] = (dot_nn(pick_x, x_ref[...]) + dot_nn(pick_g, g_ref[...])).astype(BF)


def pack_kernel(place_ref, qkv_ref, out_ref, near_ref, far_ref):
    depth = near_ref.shape[0] + far_ref.shape[0]
    near = near_ref.shape[0]
    all_heads = qkv_ref.shape[0] // depth
    heads = out_ref.shape[0] // 2
    triple = qkv_ref.shape[1]
    width = triple // 3
    rep = place_ref[0]
    for head in range(heads):
        own = rep * heads + head
        pick = selector(
            (depth, all_heads * depth),
            lambda m, n: m * all_heads + own == n,
        )
        part = dot_nn(pick, qkv_ref[...]).astype(BF)
        cols = slice(head * triple, (head + 1) * triple)
        near_ref[:, cols] = part[:near]
        far_ref[:, cols] = part[near:]
        eye = selector((depth, depth), lambda m, n: m == n)
        part = dot_nt(eye, out_ref[own]).astype(BF)
        cols = slice(heads * triple + head * width, heads * triple + (head + 1) * width)
        near_ref[:, cols] = part[:near]
        far_ref[:, cols] = part[near:]


def prep_kernel(
    patch_dev,
    place_ref,
    full_ref,
    hot_ref,
    gain_ref,
    scale_ref,
    shift_ref,
    hidden_ref,
    grad_ref,
    normed_ref,
    coef_ref,
    xinv_ref,
    xown_ref,
    gown_ref,
):
    parts = full_ref.shape[1]
    group = hidden_ref.shape[1]
    quarter = full_ref.shape[3]
    pair = 2 * patch_dev
    pick_x = selector(
        (group, 2 * group), lambda m, n: m // patch_dev * pair + m % patch_dev == n
    )
    pick_g = selector(
        (group, 2 * group), lambda m, n: m // patch_dev * pair + m % patch_dev + patch_dev == n
    )
    hot = hot_ref[...]

    def rows_of(table):
        high, low = halves(table)
        return dot_nn(hot, high) + dot_nn(hot, low)

    square = jnp.zeros((group, 1), F32)
    for part in range(parts):
        x = dot_nn(pick_x, full_ref[0, part])
        square += jnp.sum(x * x, -1, keepdims=True)
    inverse = lax.rsqrt(square / (parts * quarter) + EPS)
    for part in range(parts):
        x = dot_nn(pick_x, full_ref[0, part])
        normed = x * inverse * gain_ref[part]
        scaled = normed * (1.0 + rows_of(scale_ref[part]))
        hidden_ref[part] = (scaled + rows_of(shift_ref[part])).astype(BF)
        normed_ref[part] = normed.astype(BF)
        grad_ref[part] = dot_nn(pick_g, full_ref[0, part]).astype(BF)

    @pl.when(pl.program_id(0) == place_ref[0])
    def _():
        own = place_ref[1]
        rows = full_ref[0, own]
        x = dot_nn(pick_x, rows)
        xown_ref[...] = x.astype(BF)
        gown_ref[...] = dot_nn(pick_g, rows).astype(BF)
        coef_ref[...] = inverse * (1.0 + rows_of(scale_ref[own])) * gain_ref[own]
        xinv_ref[...] = x * inverse * inverse


def block_kernel(
    patch_dev,
    frames,
    plan,
    place_ref,
    gains_ref,
    hot_ref,
    shift_ref,
    hidden_hbm,
    grad_hbm,
    normed_hbm,
    *refs,
):
    count = 1 + max(item[0] for item in plan)
    pieces = refs[:count]
    (
        y_keep,
        y_give,
        dh_keep,
        dh_give,
        hidden,
        grad,
        normed,
        weight,
        qkv_acc,
        da_acc,
        attended,
        dqkv,
        y_stage,
        dh_stage,
        sems,
        weight_sems,
        out_sems,
    ) = refs[count:]
    parts, tokens, quarter = grad.shape
    codes = hot_ref.shape[0]
    width = gains_ref.shape[1]
    wide = qkv_acc.shape[1]
    heads = wide // (3 * width)
    cores, ring, group, _ = y_stage.shape
    replicas = tokens // group
    along = ring // replicas
    rows_y = place_ref[2]
    rows_z = place_ref[3]
    spot_x = place_ref[4]
    core = place_ref[5]
    depth = weight.shape[0] // (NY * NZ)

    def inputs(at):
        part = (rows_y + at) % NY
        result = [
            pltpu.make_async_copy(
                hidden_hbm.at[part], hidden.at[part, pl.ds(0, tokens)], sems.at[at, 0]
            ),
            pltpu.make_async_copy(grad_hbm.at[part], grad.at[part], sems.at[at, 1]),
        ]
        for number, (index, start, size, dy, dz, place) in enumerate(plan):
            if dy == at:
                owner = part * NZ + (rows_z + dz) % NZ
                target = pl.multiple_of(owner * depth + place, 16)
                result.append(
                    pltpu.make_async_copy(
                        pieces[index].at[pl.ds(start, size)],
                        weight.at[pl.ds(target, size)],
                        weight_sems.at[number],
                    )
                )
        return result

    def second(part):
        return [pltpu.make_async_copy(normed_hbm.at[part], normed.at[part], sems.at[part, 2])]

    for at in range(NY):
        for copy in inputs(at):
            copy.start()
    for part in range(parts):
        for copy in second(part):
            copy.start()

    hidden[:, tokens:, :] = shift_ref[...]
    qkv_acc[...] = jnp.zeros_like(qkv_acc)
    da_acc[...] = jnp.zeros_like(da_acc)
    for at in range(NY):
        for copy in inputs(at):
            copy.wait()
        part = (rows_y + at) % NY
        rows = pl.ds(pl.multiple_of(part * quarter, quarter), quarter)
        qkv_acc[...] += dot_nn(hidden[part], weight[rows, :wide])
        da_acc[...] += dot_nn(grad[part], weight[rows, wide:])

    gain_q = gains_ref[0:1, :]
    gain_k = gains_ref[1:2, :]
    row = lax.broadcasted_iota(jnp.int32, (group, group), 0)
    col = lax.broadcasted_iota(jnp.int32, (group, group), 1)
    clip_tokens = frames * patch_dev
    mask = (
        (row % patch_dev == col % patch_dev)
        & (row // clip_tokens == col // clip_tokens)
        & (col <= row)
    )
    factor = width ** (-0.5)
    for rep in range(replicas):
        rows = slice(rep * group, (rep + 1) * group)
        for head in range(heads):
            base = head * 3 * width
            take = lambda at: qkv_acc[rows, base + at * width : base + (at + 1) * width].astype(
                BF
            )
            q = take(0).astype(F32)
            k = take(1).astype(F32)
            value = take(2)
            d_out = da_acc[rows, head * width : (head + 1) * width].astype(BF)
            inv_q = lax.rsqrt(jnp.mean(q * q, -1, keepdims=True) + EPS)
            inv_k = lax.rsqrt(jnp.mean(k * k, -1, keepdims=True) + EPS)
            q_hat = q * inv_q
            k_hat = k * inv_k
            queries = (q_hat * gain_q).astype(BF)
            keys = (k_hat * gain_k).astype(BF)
            scores = dot_nt(queries, keys) * factor
            weights = jnp.where(mask, jnp.exp(scores), 0.0)
            probs = weights / jnp.sum(weights, -1, keepdims=True)
            probs_bf = probs.astype(BF)
            out = dot_nn(probs_bf, value)
            attended[rows, head * width : (head + 1) * width] = out.astype(BF)
            d_value = dot_tn(probs_bf, d_out)
            d_probs = dot_nt(d_out, value)
            d_scores = probs * (d_probs - jnp.sum(d_probs * probs, -1, keepdims=True))
            d_scores = (d_scores * factor).astype(BF)
            d_q = dot_nn(d_scores, keys) * gain_q
            d_k = dot_tn(d_scores, queries) * gain_k
            d_q = inv_q * (d_q - q_hat * jnp.mean(d_q * q_hat, -1, keepdims=True))
            d_k = inv_k * (d_k - k_hat * jnp.mean(d_k * k_hat, -1, keepdims=True))
            for at, item in enumerate((d_q, d_k, d_value)):
                dqkv[rows, base + at * width : base + (at + 1) * width] = item.astype(BF)

    hot = hot_ref[...]
    lanes = min(wide, 128)
    terms = jnp.zeros((tokens, lanes), F32)
    for lane in range(wide // lanes):
        cols = slice(lane * lanes, (lane + 1) * lanes)
        terms += dqkv[:tokens, cols].astype(F32) * qkv_acc[:tokens, cols]
    ones = jnp.ones((8, lanes), BF)
    high, low = halves(terms)
    terms = dot_nt(ones, high) + dot_nt(ones, low)
    moved = qkv_acc[tokens : tokens + codes] + qkv_acc[tokens + codes :]
    high, low = halves(moved)
    moved = dot_nt(high, dqkv[:tokens]) + dot_nt(low, dqkv[:tokens])
    terms -= jnp.sum(moved * hot.astype(F32), 0, keepdims=True)
    high, low = halves(dot_nn(hot, dqkv[:tokens]))
    dqkv[tokens:, :] = jnp.concatenate([high, low], 0)

    def outputs(stage, keep, give, base):
        result = []
        for step in range(ring):
            target = (spot_x + step) % ring
            for side, out in enumerate((keep, give)):
                result.append(
                    pltpu.make_async_copy(
                        stage.at[(core + side) % cores, target],
                        out.at[step],
                        out_sems.at[base, step, side],
                    )
                )
        return result

    block = min(quarter, 512)
    for part in range(parts):
        for at in range(quarter // block):
            cols = slice(at * block, (at + 1) * block)
            w_block = weight[part * quarter + at * block : part * quarter + (at + 1) * block, wide:]
            y_block = dot_nt(attended[...], w_block).astype(BF)
            for rep in range(replicas):
                rows = slice(rep * group, (rep + 1) * group)
                y_stage[part % cores, rep * along + part // cores, :, cols] = y_block[rows]
    y_copies = outputs(y_stage, y_keep, y_give, 0)
    for copy in y_copies:
        copy.start()

    for part in range(parts):
        for copy in second(part):
            copy.wait()
    tail = dh_stage.shape[2] - group
    for part in range(parts):
        for at in range(quarter // block):
            cols = slice(at * block, (at + 1) * block)
            w_block = weight[part * quarter + at * block : part * quarter + (at + 1) * block, :wide]
            d_block = dot_nt(dqkv[...], w_block)
            d_shift = d_block[tokens : tokens + codes] + d_block[tokens + codes :]
            d_block = d_block[:tokens]
            d_rounded = d_block.astype(BF)
            d_scale = dot_nn(hot, (d_block * normed[part, :, cols].astype(F32)).astype(BF))
            for rep, item in enumerate((d_scale, d_shift)):
                where = (part % cores, rep * along + part // cores)
                rows = slice(rep * group, (rep + 1) * group)
                dh_stage[where[0], where[1], 0:group, cols] = d_rounded[rows]
                dh_stage[where[0], where[1], group : group + codes, cols] = item.astype(BF)
    high, low = halves(terms)
    sub = lax.broadcasted_iota(jnp.int32, (8, group), 0)
    for rep in range(replicas):
        mine = slice(rep * group, (rep + 1) * group)
        both = jnp.where(
            sub == 0,
            high[:, mine].astype(F32),
            jnp.where(sub == 1, low[:, mine].astype(F32), 0.0),
        ).astype(BF)
        for part in range(parts):
            where = (part % cores, rep * along + part // cores)
            dh_stage[where[0], where[1], group + codes :, :] = jnp.zeros(
                (tail - codes, quarter), BF
            )
            dh_stage[where[0], where[1], group + codes : group + codes + 8, 0:group] = both
    dh_copies = outputs(dh_stage, dh_keep, dh_give, 1)
    for copy in dh_copies:
        copy.start()
    for copy in y_copies + dh_copies:
        copy.wait()


def finish_kernel(
    patch_dev,
    code_count,
    parts,
    yk_ref,
    yr_ref,
    ya_ref,
    yb_ref,
    dk_ref,
    dr_ref,
    da_ref,
    db_ref,
    coef_ref,
    xinv_ref,
    xown_ref,
    gown_ref,
    send_ref,
):
    group, quarter = xown_ref.shape
    y = (
        xown_ref[...].astype(F32)
        + (yk_ref[0].astype(F32) + yr_ref[0].astype(F32))
        + (ya_ref[...].astype(F32) + yb_ref[...].astype(F32))
    )
    total = (dk_ref[0].astype(F32) + dr_ref[0].astype(F32)) + (
        da_ref[...].astype(F32) + db_ref[...].astype(F32)
    )
    terms = total[group + code_count : group + code_count + 8, :group]
    term = (terms[0:1] + terms[1:2]) / (quarter * parts)
    term = jnp.broadcast_to(term, (group, group)).T[:, 0:1]
    dx = gown_ref[...].astype(F32) + (total[:group] * coef_ref[...] - xinv_ref[...] * term)
    grads = total[group : group + code_count].astype(BF)
    span = 2 * patch_dev + code_count
    rows = send_ref.shape[0]
    pick_y = selector(
        (rows, group),
        lambda m, n: (m % span < patch_dev) & (m // span * patch_dev + m % span == n),
    )
    pick_d = selector(
        (rows, group),
        lambda m, n: (m % span >= patch_dev)
        & (m % span < 2 * patch_dev)
        & (m // span * patch_dev + m % span - patch_dev == n),
    )
    pick_g = selector((rows, code_count), lambda m, n: m % span - 2 * patch_dev == n)
    send_ref[...] = (
        dot_nn(pick_y, y.astype(BF)) + dot_nn(pick_d, dx.astype(BF)) + dot_nn(pick_g, grads)
    ).astype(BF)


def unpack_kernel(patch_dev, factor, back_ref, y_ref, dx_ref, sum_ref):
    group = y_ref.shape[0]
    rows = back_ref.shape[0]
    codes = sum_ref.shape[0]
    span = 2 * patch_dev + codes
    back = back_ref[...]
    pick_y = selector((group, rows), lambda m, n: m // patch_dev * span + m % patch_dev == n)
    pick_d = selector(
        (group, rows), lambda m, n: m // patch_dev * span + m % patch_dev + patch_dev == n
    )
    pick_g = selector((codes, rows), lambda m, n: n % span - 2 * patch_dev == m)
    y_ref[...] = dot_nn(pick_y, back).astype(BF)
    dx_ref[...] = dot_nn(pick_d, back).astype(BF)
    sum_ref[...] = dot_nn(pick_g, back) * factor


NY = 4
NZ = 8
CORES = 2
VMEM = pl.BlockSpec(memory_space=pltpu.VMEM)
SMEM = pl.BlockSpec(memory_space=pltpu.SMEM)
ANY = pl.BlockSpec(memory_space=pl.ANY)


def fetch(value, dy, dz):
    pairs = []
    for y in range(NY):
        for z in range(NZ):
            pairs.append((((y + dy) % NY) * NZ + (z + dz) % NZ, y * NZ + z))
    return lax.ppermute(value, "tm", pairs)


def fetch_x(value, dx, ring):
    pairs = []
    for x in range(ring):
        for core in range(CORES):
            pairs.append((((x + dx) % ring) * CORES + core, x * CORES + core))
    return lax.ppermute(value, ("replica", "tensor"), pairs)


def swap_cores(value, ring):
    pairs = []
    for x in range(ring):
        for core in range(CORES):
            pairs.append((x * CORES + core, x * CORES + 1 - core))
    return lax.ppermute(value, ("replica", "tensor"), pairs)


def gate(*values):
    return lax.optimization_barrier(values)


def gather_weight(near, far, codes_in, tokens_in, tokens_ready):
    a = near.shape[0]
    b = far.shape[0]
    pieces = []
    plan = []

    def add(value, blocks):
        start = 0
        for size, dy, dz, place in blocks:
            plan.append((len(pieces), start, size, dy % NY, dz % NZ, place))
            start += size
        pieces.append(value)

    def line(dy, *dzs):
        return [(a, dy, dz, 0) for dz in dzs]

    def column(dz, ys=(0, 1, -1, 2)):
        return [(b, dy, dz, a) for dy in ys]

    def pair(value, dzs):
        up, dn = fetch(value, 1, 0), fetch(value, -1, 0)
        add(value, line(0, *dzs))
        add(up, line(1, *dzs))
        add(dn, line(-1, *dzs))
        return up, dn

    zu, zd = fetch(near, 0, 1), fetch(near, 0, -1)
    fu, fd, fo = fetch(far, 1, 0), fetch(far, -1, 0), fetch(far, 2, 0)
    codes = codes_in()
    near, far, zu, zd, fu, fd, fo, codes = gate(near, far, zu, zd, fu, fd, fo, codes)
    cols = jnp.concatenate([far, fu, fd, fo], 0)
    add(cols, column(0))
    first_at = (0, 1, -1)
    up1, dn1 = pair(jnp.concatenate([near, zu, zd], 0), first_at)
    zu2, zd2 = fetch(zu, 0, 1), fetch(zd, 0, -1)
    zu3, zd3 = fetch(zu2, 0, 1), fetch(zd2, 0, -1)
    token = tokens_in(zu2)
    up1, dn1, zu2, zd2, zu3, zd3, cols, token = gate(
        up1, dn1, zu2, zd2, zu3, zd3, cols, token
    )
    second_at = (2, -2, 3)
    up2, dn2 = pair(jnp.concatenate([zu2, zd2, zu3], 0), second_at)
    cu, cd = fetch(cols, 0, 1), fetch(cols, 0, -1)
    z4 = fetch(zu3, 0, 1)
    up2, dn2, cu, cd, z4 = gate(up2, dn2, cu, cd, z4)
    add(cu, column(1))
    add(cd, column(-1))
    third_at = (-3, 4)
    up3, dn3 = pair(jnp.concatenate([zd3, z4], 0), third_at)
    cu2, cd2 = fetch(cu, 0, 1), fetch(cd, 0, -1)
    ready = tokens_ready(token, codes)
    up3, dn3, cu2, cd2, *ready = gate(up3, dn3, cu2, cd2, *ready)
    add(cu2, column(2))
    add(cd2, column(-2))
    cu3, cd3 = fetch(cu2, 0, 1), fetch(cd2, 0, -1)
    x1, x2 = fetch(up1, 1, 0), fetch(dn2, -1, 0)
    add(x1, line(2, *first_at))
    add(x2, line(2, *second_at))
    cu3, cd3, x1, x2 = gate(cu3, cd3, x1, x2)
    add(cu3, column(3))
    add(cd3, column(-3))
    add(fetch(cu3[: 2 * b], 0, 1), column(4, (0, 1)))
    add(fetch(cd3[2 * b :], 0, -1), column(4, (-1, 2)))
    add(fetch(up3[:a], 1, 0), line(2, -3))
    add(fetch(dn3[a:], -1, 0), line(2, 4))
    return pieces, tuple(plan), ready


def reduce_ring(keep, give, ring):
    got = swap_cores(give, ring)
    rows = keep.shape[1]
    half = rows // 32 * 16

    def both(at, rows_from, rows_to):
        return keep[at, rows_from:rows_to].astype(F32) + got[at, rows_from:rows_to].astype(F32)

    low = fetch_x(both(2, 0, half).astype(BF), -1, ring)
    high = fetch_x(both(2, half, rows).astype(BF), 1, ring)
    up = jnp.concatenate(
        [both(1, 0, half) + low.astype(F32), both(1, half, rows)], 0
    ).astype(BF)
    dn = jnp.concatenate(
        [both(3, 0, half), both(3, half, rows) + high.astype(F32)], 0
    ).astype(BF)
    return keep, got, fetch_x(up, -1, ring), fetch_x(dn, 1, ring)


def shards(
    activations,
    action_codes,
    norm_gain,
    action_scale,
    action_shift,
    qkv_weight,
    qk_gains,
    out_weight,
    grad_output,
):
    replicas = lax.axis_size("replica")
    shards_tm = lax.axis_size("tm")
    parts = lax.axis_size("tensor")
    ring = replicas * parts // CORES
    rep = lax.axis_index("replica")
    part = lax.axis_index("tensor")
    spot = lax.axis_index("tm")
    frames = action_codes.shape[1]
    quarter = activations.shape[2]
    patches = activations.shape[1]
    patch_dev = patches // shards_tm
    depth = qkv_weight.shape[0]
    heads = qkv_weight.shape[1] // replicas
    triple = qkv_weight.shape[2]
    width = triple // 3
    wide = heads * triple
    narrow = heads * width
    code_count = action_scale.shape[0]
    group = shards_tm * patch_dev
    tokens = replicas * group
    near = depth // 8 * 5
    place = jnp.stack(
        [
            rep,
            part,
            spot // NZ,
            spot % NZ,
            rep * (ring // replicas) + part // CORES,
            part % CORES,
        ]
    ).astype(jnp.int32)

    weight_near, weight_far = pl.pallas_call(
        pack_kernel,
        out_shape=(
            jax.ShapeDtypeStruct((near, wide + narrow), BF),
            jax.ShapeDtypeStruct((depth - near, wide + narrow), BF),
        ),
        in_specs=[SMEM] + [VMEM] * 2,
        out_specs=(VMEM, VMEM),
        compiler_params=pltpu.CompilerParams(vmem_limit_bytes=24 * 1024 * 1024),
        name="pack",
    )(place, qkv_weight.reshape(-1, triple), out_weight)

    def tokens_in(hold):
        both = pl.pallas_call(
            functools.partial(tokens_kernel, patch_dev),
            out_shape=jax.ShapeDtypeStruct((2 * patches, quarter), BF),
            in_specs=[VMEM] * 2 + [ANY],
            out_specs=VMEM,
            compiler_params=pltpu.CompilerParams(vmem_limit_bytes=24 * 1024 * 1024),
            name="tokens",
        )(activations.reshape(patches, quarter), grad_output.reshape(patches, quarter), hold)
        return lax.all_to_all(both, "tm", split_axis=0, concat_axis=0, tiled=True)

    def codes_in():
        return lax.ppermute(action_codes, "replica", [(i, 1 - i) for i in range(2)])

    def by_part(table):
        return table.reshape(table.shape[0], parts, quarter).transpose(1, 0, 2)

    big = jax.ShapeDtypeStruct((parts, tokens, quarter), BF)
    big_spec = pl.BlockSpec((parts, group, quarter), lambda i: (0, i, 0))
    own_spec = pl.BlockSpec((group, quarter), lambda i: (0, 0))

    def whole(*shape):
        return pl.BlockSpec(shape, lambda i: (0,) * len(shape))

    def tokens_ready(both, other):
        codes = jnp.where(
            rep == 0,
            jnp.concatenate([action_codes, other], 0),
            jnp.concatenate([other, action_codes], 0),
        ).reshape(-1)
        codes = jnp.repeat(codes, patch_dev)
        code_range = jnp.arange(code_count)
        hot = (codes[:, None] == code_range[None, :]).astype(BF)
        hot_t = (codes[None, :] == code_range[:, None]).astype(BF)
        full = lax.all_gather(both, ("replica", "tensor"), axis=0)
        full = full.reshape(replicas, parts, 2 * group, quarter)
        return hot_t, *pl.pallas_call(
            functools.partial(prep_kernel, patch_dev),
            grid=(replicas,),
            out_shape=(big, big, big)
            + (jax.ShapeDtypeStruct((group, quarter), F32),) * 2
            + (jax.ShapeDtypeStruct((group, quarter), BF),) * 2,
            in_specs=[
                SMEM,
                pl.BlockSpec((1, parts, 2 * group, quarter), lambda i: (i, 0, 0, 0)),
                pl.BlockSpec((group, code_count), lambda i: (i, 0)),
                whole(parts, 1, quarter),
                whole(parts, code_count, quarter),
                whole(parts, code_count, quarter),
            ],
            out_specs=(big_spec,) * 3 + (own_spec,) * 4,
            compiler_params=pltpu.CompilerParams(vmem_limit_bytes=48 * 1024 * 1024),
            name="prep",
        )(
            place,
            full,
            hot,
            by_part(norm_gain[None]),
            by_part(action_scale),
            by_part(action_shift),
        )

    pieces, plan, ready = gather_weight(
        weight_near, weight_far, codes_in, tokens_in, tokens_ready
    )
    hot_t, hidden, grad, normed, coef, xinv, x_own, g_own = ready

    shift_halves = jnp.concatenate(halves(by_part(action_shift)), 1)
    tail_rows = group + EXTRA
    y_shape = jax.ShapeDtypeStruct((ring, group, quarter), BF)
    dh_shape = jax.ShapeDtypeStruct((ring, tail_rows, quarter), BF)
    flops = 4 * tokens * parts * quarter * (wide + narrow)
    moved = 2 * parts * quarter * (wide + narrow + 5 * tokens)
    y_keep, y_give, dh_keep, dh_give = pl.pallas_call(
        functools.partial(block_kernel, patch_dev, frames, plan),
        out_shape=(y_shape, y_shape, dh_shape, dh_shape),
        in_specs=[SMEM, VMEM, VMEM, VMEM] + [ANY] * (3 + len(pieces)),
        out_specs=(ANY,) * 4,
        scratch_shapes=[
            pltpu.VMEM((parts, tokens + 2 * code_count, quarter), BF),
            pltpu.VMEM((parts, tokens, quarter), BF),
            pltpu.VMEM((parts, tokens, quarter), BF),
            pltpu.VMEM((parts * quarter, wide + narrow), BF),
            pltpu.VMEM((tokens + 2 * code_count, wide), F32),
            pltpu.VMEM((tokens, narrow), F32),
            pltpu.VMEM((tokens, narrow), BF),
            pltpu.VMEM((tokens + 2 * code_count, wide), BF),
            pltpu.VMEM((CORES, ring, group, quarter), BF),
            pltpu.VMEM((CORES, ring, tail_rows, quarter), BF),
            pltpu.SemaphoreType.DMA((parts, 3)),
            pltpu.SemaphoreType.DMA((len(plan),)),
            pltpu.SemaphoreType.DMA((2, ring, CORES)),
        ],
        compiler_params=pltpu.CompilerParams(vmem_limit_bytes=52 * 1024 * 1024),
        cost_estimate=pl.CostEstimate(flops=flops, bytes_accessed=moved, transcendentals=0),
        name="block",
    )(place, qk_gains, hot_t, shift_halves, hidden, grad, normed, *pieces)

    dh_terms = reduce_ring(dh_keep, dh_give, ring)
    y_terms = reduce_ring(y_keep, y_give, ring)
    first_y = pl.BlockSpec((1, group, quarter), lambda i: (0, 0, 0))
    first_dh = pl.BlockSpec((1, tail_rows, quarter), lambda i: (0, 0, 0))
    span = 2 * patch_dev + code_count
    send = pl.pallas_call(
        functools.partial(finish_kernel, patch_dev, code_count, parts),
        grid=(1,),
        out_shape=jax.ShapeDtypeStruct((shards_tm * span, quarter), BF),
        in_specs=[first_y] * 2
        + [whole(group, quarter)] * 2
        + [first_dh] * 2
        + [whole(tail_rows, quarter)] * 2
        + [whole(group, quarter)] * 4,
        out_specs=whole(shards_tm * span, quarter),
        compiler_params=pltpu.CompilerParams(vmem_limit_bytes=24 * 1024 * 1024),
        name="finish",
    )(*y_terms, *dh_terms, coef, xinv, x_own, g_own)
    back = lax.all_to_all(send, "tm", split_axis=0, concat_axis=0, tiled=True)
    token_total = tokens * shards_tm
    y_frames, dx_frames, grad_mine = pl.pallas_call(
        functools.partial(unpack_kernel, patch_dev, token_total ** (-0.5)),
        out_shape=(
            jax.ShapeDtypeStruct((group, quarter), BF),
            jax.ShapeDtypeStruct((group, quarter), BF),
            jax.ShapeDtypeStruct((code_count, quarter), F32),
        ),
        in_specs=[VMEM],
        out_specs=(VMEM, VMEM, VMEM),
        compiler_params=pltpu.CompilerParams(vmem_limit_bytes=24 * 1024 * 1024),
        name="unpack",
    )(back)
    grad_other = lax.ppermute(grad_mine, "replica", [(i, 1 - i) for i in range(2)])
    d_scale = jnp.where(rep == 0, grad_mine, grad_other)
    d_shift = jnp.where(rep == 0, grad_other, grad_mine)
    return (y_frames[None], dx_frames[None], d_scale, d_shift)


def solution(mesh):
    placed = (
        P(("replica", "tm"), None, "tensor"),
        P("replica", None),
        P(),
        P(),
        P(),
        P("tm", "tensor", None),
        P(),
        P("tensor", None, "tm"),
        P(("replica", "tm"), None, "tensor"),
    )
    return jax.shard_map(
        shards,
        mesh=mesh,
        in_specs=placed,
        out_specs=(
            P(("replica", "tm"), None, "tensor"),
            P(("replica", "tm"), None, "tensor"),
            P(None, "tensor"),
            P(None, "tensor"),
        ),
        check_vma=False,
    )
```

```python
import functools

import jax
import jax.numpy as jnp
from jax import lax
from jax.experimental import pallas as pl
from jax.experimental.pallas import tpu as pltpu
from jax.sharding import PartitionSpec as P

EPS = 1e-06
BF = jnp.bfloat16
F32 = jnp.float32
EXTRA = 16


def dot_nn(a, b):
    return lax.dot_general(a, b, (((1,), (0,)), ((), ())), preferred_element_type=F32)


def dot_nt(a, b):
    return lax.dot_general(a, b, (((1,), (1,)), ((), ())), preferred_element_type=F32)


def dot_tn(a, b):
    return lax.dot_general(a, b, (((0,), (0,)), ((), ())), preferred_element_type=F32)


def halves(value):
    high = value.astype(BF)
    return high, (value - high.astype(F32)).astype(BF)


def selector(shape, pick):
    row = lax.broadcasted_iota(jnp.int32, shape, 0)
    col = lax.broadcasted_iota(jnp.int32, shape, 1)
    return jnp.where(pick(row, col), 1.0, 0.0).astype(BF)


def tokens_kernel(patch_dev, x_ref, g_ref, hold_ref, both_ref):
    rows = x_ref.shape[0]
    pair = 2 * patch_dev
    pick_x = selector(
        (2 * rows, rows),
        lambda m, n: (m % pair < patch_dev) & (m // pair * patch_dev + m % pair == n),
    )
    pick_g = selector(
        (2 * rows, rows),
        lambda m, n: (m % pair >= patch_dev)
        & (m // pair * patch_dev + m % pair - patch_dev == n),
    )
    both_ref[...] = (dot_nn(pick_x, x_ref[...]) + dot_nn(pick_g, g_ref[...])).astype(BF)


def pack_kernel(place_ref, qkv_ref, out_ref, near_ref, far_ref):
    depth = near_ref.shape[0] + far_ref.shape[0]
    near = near_ref.shape[0]
    all_heads = qkv_ref.shape[0] // depth
    heads = out_ref.shape[0] // 2
    triple = qkv_ref.shape[1]
    width = triple // 3
    rep = place_ref[0]
    for head in range(heads):
        own = rep * heads + head
        pick = selector(
            (depth, all_heads * depth),
            lambda m, n: m * all_heads + own == n,
        )
        part = dot_nn(pick, qkv_ref[...]).astype(BF)
        cols = slice(head * triple, (head + 1) * triple)
        near_ref[:, cols] = part[:near]
        far_ref[:, cols] = part[near:]
        eye = selector((depth, depth), lambda m, n: m == n)
        part = dot_nt(eye, out_ref[own]).astype(BF)
        cols = slice(heads * triple + head * width, heads * triple + (head + 1) * width)
        near_ref[:, cols] = part[:near]
        far_ref[:, cols] = part[near:]


def prep_kernel(
    patch_dev,
    place_ref,
    full_ref,
    hot_ref,
    gain_ref,
    scale_ref,
    shift_ref,
    hidden_ref,
    grad_ref,
    normed_ref,
    coef_ref,
    xinv_ref,
    xown_ref,
    gown_ref,
):
    parts = full_ref.shape[1]
    group = hidden_ref.shape[1]
    quarter = full_ref.shape[3]
    pair = 2 * patch_dev
    pick_x = selector(
        (group, 2 * group), lambda m, n: m // patch_dev * pair + m % patch_dev == n
    )
    pick_g = selector(
        (group, 2 * group), lambda m, n: m // patch_dev * pair + m % patch_dev + patch_dev == n
    )
    hot = hot_ref[...]

    def rows_of(table):
        high, low = halves(table)
        return dot_nn(hot, high) + dot_nn(hot, low)

    square = jnp.zeros((group, 1), F32)
    for part in range(parts):
        x = dot_nn(pick_x, full_ref[0, part])
        square += jnp.sum(x * x, -1, keepdims=True)
    inverse = lax.rsqrt(square / (parts * quarter) + EPS)
    for part in range(parts):
        x = dot_nn(pick_x, full_ref[0, part])
        normed = x * inverse * gain_ref[part]
        scaled = normed * (1.0 + rows_of(scale_ref[part]))
        hidden_ref[part] = (scaled + rows_of(shift_ref[part])).astype(BF)
        normed_ref[part] = normed.astype(BF)
        grad_ref[part] = dot_nn(pick_g, full_ref[0, part]).astype(BF)

    @pl.when(pl.program_id(0) == place_ref[0])
    def _():
        own = place_ref[1]
        rows = full_ref[0, own]
        x = dot_nn(pick_x, rows)
        xown_ref[...] = x.astype(BF)
        gown_ref[...] = dot_nn(pick_g, rows).astype(BF)
        coef_ref[...] = inverse * (1.0 + rows_of(scale_ref[own])) * gain_ref[own]
        xinv_ref[...] = x * inverse * inverse


def block_kernel(
    patch_dev,
    frames,
    plan,
    place_ref,
    gains_ref,
    hot_ref,
    shift_ref,
    hidden_hbm,
    grad_hbm,
    normed_hbm,
    *refs,
):
    count = 1 + max(item[0] for item in plan)
    pieces = refs[:count]
    (
        y_keep,
        y_give,
        dh_keep,
        dh_give,
        hidden,
        grad,
        normed,
        weight,
        qkv_acc,
        da_acc,
        attended,
        dqkv,
        y_stage,
        dh_stage,
        sems,
        weight_sems,
        out_sems,
    ) = refs[count:]
    parts, tokens, quarter = grad.shape
    codes = hot_ref.shape[0]
    width = gains_ref.shape[1]
    wide = qkv_acc.shape[1]
    heads = wide // (3 * width)
    cores, ring, group, _ = y_stage.shape
    replicas = tokens // group
    along = ring // replicas
    rows_y = place_ref[2]
    rows_z = place_ref[3]
    spot_x = place_ref[4]
    core = place_ref[5]
    depth = weight.shape[0] // (NY * NZ)

    def inputs(at):
        part = (rows_y + at) % NY
        result = [
            pltpu.make_async_copy(
                hidden_hbm.at[part], hidden.at[part, pl.ds(0, tokens)], sems.at[at, 0]
            ),
            pltpu.make_async_copy(grad_hbm.at[part], grad.at[part], sems.at[at, 1]),
        ]
        for number, (index, start, size, dy, dz, place) in enumerate(plan):
            if dy == at:
                owner = part * NZ + (rows_z + dz) % NZ
                target = pl.multiple_of(owner * depth + place, 16)
                result.append(
                    pltpu.make_async_copy(
                        pieces[index].at[pl.ds(start, size)],
                        weight.at[pl.ds(target, size)],
                        weight_sems.at[number],
                    )
                )
        return result

    def second(part):
        return [pltpu.make_async_copy(normed_hbm.at[part], normed.at[part], sems.at[part, 2])]

    for at in range(NY):
        for copy in inputs(at):
            copy.start()
    for part in range(parts):
        for copy in second(part):
            copy.start()

    hidden[:, tokens:, :] = shift_ref[...]
    qkv_acc[...] = jnp.zeros_like(qkv_acc)
    da_acc[...] = jnp.zeros_like(da_acc)
    for at in range(NY):
        for copy in inputs(at):
            copy.wait()
        part = (rows_y + at) % NY
        rows = pl.ds(pl.multiple_of(part * quarter, quarter), quarter)
        qkv_acc[...] += dot_nn(hidden[part], weight[rows, :wide])
        da_acc[...] += dot_nn(grad[part], weight[rows, wide:])

    gain_q = gains_ref[0:1, :]
    gain_k = gains_ref[1:2, :]
    row = lax.broadcasted_iota(jnp.int32, (group, group), 0)
    col = lax.broadcasted_iota(jnp.int32, (group, group), 1)
    clip_tokens = frames * patch_dev
    mask = (
        (row % patch_dev == col % patch_dev)
        & (row // clip_tokens == col // clip_tokens)
        & (col <= row)
    )
    factor = width ** (-0.5)
    for rep in range(replicas):
        rows = slice(rep * group, (rep + 1) * group)
        for head in range(heads):
            base = head * 3 * width
            take = lambda at: qkv_acc[rows, base + at * width : base + (at + 1) * width].astype(
                BF
            )
            q = take(0).astype(F32)
            k = take(1).astype(F32)
            value = take(2)
            d_out = da_acc[rows, head * width : (head + 1) * width].astype(BF)
            inv_q = lax.rsqrt(jnp.mean(q * q, -1, keepdims=True) + EPS)
            inv_k = lax.rsqrt(jnp.mean(k * k, -1, keepdims=True) + EPS)
            q_hat = q * inv_q
            k_hat = k * inv_k
            queries = (q_hat * gain_q).astype(BF)
            keys = (k_hat * gain_k).astype(BF)
            scores = dot_nt(queries, keys) * factor
            weights = jnp.where(mask, jnp.exp(scores), 0.0)
            probs = weights / jnp.sum(weights, -1, keepdims=True)
            probs_bf = probs.astype(BF)
            out = dot_nn(probs_bf, value)
            attended[rows, head * width : (head + 1) * width] = out.astype(BF)
            d_value = dot_tn(probs_bf, d_out)
            d_probs = dot_nt(d_out, value)
            d_scores = probs * (d_probs - jnp.sum(d_probs * probs, -1, keepdims=True))
            d_scores = (d_scores * factor).astype(BF)
            d_q = dot_nn(d_scores, keys) * gain_q
            d_k = dot_tn(d_scores, queries) * gain_k
            d_q = inv_q * (d_q - q_hat * jnp.mean(d_q * q_hat, -1, keepdims=True))
            d_k = inv_k * (d_k - k_hat * jnp.mean(d_k * k_hat, -1, keepdims=True))
            for at, item in enumerate((d_q, d_k, d_value)):
                dqkv[rows, base + at * width : base + (at + 1) * width] = item.astype(BF)

    hot = hot_ref[...]
    lanes = min(wide, 128)
    terms = jnp.zeros((tokens, lanes), F32)
    for lane in range(wide // lanes):
        cols = slice(lane * lanes, (lane + 1) * lanes)
        terms += dqkv[:tokens, cols].astype(F32) * qkv_acc[:tokens, cols]
    ones = jnp.ones((8, lanes), BF)
    high, low = halves(terms)
    terms = dot_nt(ones, high) + dot_nt(ones, low)
    moved = qkv_acc[tokens : tokens + codes] + qkv_acc[tokens + codes :]
    high, low = halves(moved)
    moved = dot_nt(high, dqkv[:tokens]) + dot_nt(low, dqkv[:tokens])
    terms -= jnp.sum(moved * hot.astype(F32), 0, keepdims=True)
    high, low = halves(dot_nn(hot, dqkv[:tokens]))
    dqkv[tokens:, :] = jnp.concatenate([high, low], 0)

    def outputs(stage, keep, give, base):
        result = []
        for step in range(ring):
            target = (spot_x + step) % ring
            for side, out in enumerate((keep, give)):
                result.append(
                    pltpu.make_async_copy(
                        stage.at[(core + side) % cores, target],
                        out.at[step],
                        out_sems.at[base, step, side],
                    )
                )
        return result

    block = min(quarter, 512)
    for part in range(parts):
        for at in range(quarter // block):
            cols = slice(at * block, (at + 1) * block)
            w_block = weight[part * quarter + at * block : part * quarter + (at + 1) * block, wide:]
            y_block = dot_nt(attended[...], w_block).astype(BF)
            for rep in range(replicas):
                rows = slice(rep * group, (rep + 1) * group)
                y_stage[part % cores, rep * along + part // cores, :, cols] = y_block[rows]
    y_copies = outputs(y_stage, y_keep, y_give, 0)
    for copy in y_copies:
        copy.start()

    for part in range(parts):
        for copy in second(part):
            copy.wait()
    tail = dh_stage.shape[2] - group
    for part in range(parts):
        for at in range(quarter // block):
            cols = slice(at * block, (at + 1) * block)
            w_block = weight[part * quarter + at * block : part * quarter + (at + 1) * block, :wide]
            d_block = dot_nt(dqkv[...], w_block)
            d_shift = d_block[tokens : tokens + codes] + d_block[tokens + codes :]
            d_block = d_block[:tokens]
            d_rounded = d_block.astype(BF)
            d_scale = dot_nn(hot, (d_block * normed[part, :, cols].astype(F32)).astype(BF))
            for rep, item in enumerate((d_scale, d_shift)):
                where = (part % cores, rep * along + part // cores)
                rows = slice(rep * group, (rep + 1) * group)
                dh_stage[where[0], where[1], 0:group, cols] = d_rounded[rows]
                dh_stage[where[0], where[1], group : group + codes, cols] = item.astype(BF)
    high, low = halves(terms)
    sub = lax.broadcasted_iota(jnp.int32, (8, group), 0)
    for rep in range(replicas):
        mine = slice(rep * group, (rep + 1) * group)
        both = jnp.where(
            sub == 0,
            high[:, mine].astype(F32),
            jnp.where(sub == 1, low[:, mine].astype(F32), 0.0),
        ).astype(BF)
        for part in range(parts):
            where = (part % cores, rep * along + part // cores)
            dh_stage[where[0], where[1], group + codes :, :] = jnp.zeros(
                (tail - codes, quarter), BF
            )
            dh_stage[where[0], where[1], group + codes : group + codes + 8, 0:group] = both
    dh_copies = outputs(dh_stage, dh_keep, dh_give, 1)
    for copy in dh_copies:
        copy.start()
    for copy in y_copies + dh_copies:
        copy.wait()


def finish_kernel(
    patch_dev,
    code_count,
    parts,
    yk_ref,
    yr_ref,
    ya_ref,
    yb_ref,
    dk_ref,
    dr_ref,
    da_ref,
    db_ref,
    coef_ref,
    xinv_ref,
    xown_ref,
    gown_ref,
    send_ref,
):
    group, quarter = xown_ref.shape
    y = (
        xown_ref[...].astype(F32)
        + (yk_ref[0].astype(F32) + yr_ref[0].astype(F32))
        + (ya_ref[...].astype(F32) + yb_ref[...].astype(F32))
    )
    total = (dk_ref[0].astype(F32) + dr_ref[0].astype(F32)) + (
        da_ref[...].astype(F32) + db_ref[...].astype(F32)
    )
    terms = total[group + code_count : group + code_count + 8, :group]
    term = (terms[0:1] + terms[1:2]) / (quarter * parts)
    term = jnp.broadcast_to(term, (group, group)).T[:, 0:1]
    dx = gown_ref[...].astype(F32) + (total[:group] * coef_ref[...] - xinv_ref[...] * term)
    grads = total[group : group + code_count].astype(BF)
    span = 2 * patch_dev + code_count
    rows = send_ref.shape[0]
    pick_y = selector(
        (rows, group),
        lambda m, n: (m % span < patch_dev) & (m // span * patch_dev + m % span == n),
    )
    pick_d = selector(
        (rows, group),
        lambda m, n: (m % span >= patch_dev)
        & (m % span < 2 * patch_dev)
        & (m // span * patch_dev + m % span - patch_dev == n),
    )
    pick_g = selector((rows, code_count), lambda m, n: m % span - 2 * patch_dev == n)
    send_ref[...] = (
        dot_nn(pick_y, y.astype(BF)) + dot_nn(pick_d, dx.astype(BF)) + dot_nn(pick_g, grads)
    ).astype(BF)


def unpack_kernel(patch_dev, factor, back_ref, y_ref, dx_ref, sum_ref):
    group = y_ref.shape[0]
    rows = back_ref.shape[0]
    codes = sum_ref.shape[0]
    span = 2 * patch_dev + codes
    back = back_ref[...]
    pick_y = selector((group, rows), lambda m, n: m // patch_dev * span + m % patch_dev == n)
    pick_d = selector(
        (group, rows), lambda m, n: m // patch_dev * span + m % patch_dev + patch_dev == n
    )
    pick_g = selector((codes, rows), lambda m, n: n % span - 2 * patch_dev == m)
    y_ref[...] = dot_nn(pick_y, back).astype(BF)
    dx_ref[...] = dot_nn(pick_d, back).astype(BF)
    sum_ref[...] = dot_nn(pick_g, back) * factor


NY = 4
NZ = 8
CORES = 2
VMEM = pl.BlockSpec(memory_space=pltpu.VMEM)
SMEM = pl.BlockSpec(memory_space=pltpu.SMEM)
ANY = pl.BlockSpec(memory_space=pl.ANY)


def fetch(value, dy, dz):
    pairs = []
    for y in range(NY):
        for z in range(NZ):
            pairs.append((((y + dy) % NY) * NZ + (z + dz) % NZ, y * NZ + z))
    return lax.ppermute(value, "tm", pairs)


def fetch_x(value, dx, ring):
    pairs = []
    for x in range(ring):
        for core in range(CORES):
            pairs.append((((x + dx) % ring) * CORES + core, x * CORES + core))
    return lax.ppermute(value, ("replica", "tensor"), pairs)


def swap_cores(value, ring):
    pairs = []
    for x in range(ring):
        for core in range(CORES):
            pairs.append((x * CORES + core, x * CORES + 1 - core))
    return lax.ppermute(value, ("replica", "tensor"), pairs)


def gate(*values):
    return lax.optimization_barrier(values)


def gather_weight(near, far, codes_in, tokens_in, tokens_ready):
    a = near.shape[0]
    b = far.shape[0]
    pieces = []
    plan = []

    def add(value, blocks):
        start = 0
        for size, dy, dz, place in blocks:
            plan.append((len(pieces), start, size, dy % NY, dz % NZ, place))
            start += size
        pieces.append(value)

    def line(dy, *dzs):
        return [(a, dy, dz, 0) for dz in dzs]

    def column(dz, ys=(0, 1, -1, 2)):
        return [(b, dy, dz, a) for dy in ys]

    def pair(value, dzs):
        up, dn = fetch(value, 1, 0), fetch(value, -1, 0)
        add(value, line(0, *dzs))
        add(up, line(1, *dzs))
        add(dn, line(-1, *dzs))
        return up, dn

    zu, zd = fetch(near, 0, 1), fetch(near, 0, -1)
    fu, fd, fo = fetch(far, 1, 0), fetch(far, -1, 0), fetch(far, 2, 0)
    codes = codes_in()
    near, far, zu, zd, fu, fd, fo, codes = gate(near, far, zu, zd, fu, fd, fo, codes)
    cols = jnp.concatenate([far, fu, fd, fo], 0)
    add(cols, column(0))
    first_at = (0, 1, -1)
    up1, dn1 = pair(jnp.concatenate([near, zu, zd], 0), first_at)
    zu2, zd2 = fetch(zu, 0, 1), fetch(zd, 0, -1)
    zu3, zd3 = fetch(zu2, 0, 1), fetch(zd2, 0, -1)
    z4 = fetch(zu3, 0, 1)
    up1, dn1, zu2, zd2, zu3, zd3, z4, cols = gate(up1, dn1, zu2, zd2, zu3, zd3, z4, cols)
    second_at = (2, -2, 3)
    up2, dn2 = pair(jnp.concatenate([zu2, zd2, zu3], 0), second_at)
    cu, cd = fetch(cols, 0, 1), fetch(cols, 0, -1)
    token = tokens_in(zu2)
    up2, dn2, cu, cd, token = gate(up2, dn2, cu, cd, token)
    add(cu, column(1))
    add(cd, column(-1))
    third_at = (-3, 4)
    up3, dn3 = pair(jnp.concatenate([zd3, z4], 0), third_at)
    cu2, cd2 = fetch(cu, 0, 1), fetch(cd, 0, -1)
    up3, dn3, cu2, cd2 = gate(up3, dn3, cu2, cd2)
    add(cu2, column(2))
    add(cd2, column(-2))
    cu3, cd3 = fetch(cu2, 0, 1), fetch(cd2, 0, -1)
    x1, x2 = fetch(up1, 1, 0), fetch(dn2, -1, 0)
    add(x1, line(2, *first_at))
    add(x2, line(2, *second_at))
    ready = tokens_ready(token, codes)
    cu3, cd3, x1, x2, *ready = gate(cu3, cd3, x1, x2, *ready)
    add(cu3, column(3))
    add(cd3, column(-3))
    add(fetch(cu3[: 2 * b], 0, 1), column(4, (0, 1)))
    add(fetch(cd3[2 * b :], 0, -1), column(4, (-1, 2)))
    add(fetch(up3[:a], 1, 0), line(2, -3))
    add(fetch(dn3[a:], -1, 0), line(2, 4))
    return pieces, tuple(plan), ready


def reduce_ring(keep, give, ring):
    got = swap_cores(give, ring)
    rows = keep.shape[1]
    half = rows // 32 * 16

    def both(at, rows_from, rows_to):
        return keep[at, rows_from:rows_to].astype(F32) + got[at, rows_from:rows_to].astype(F32)

    low = fetch_x(both(2, 0, half).astype(BF), -1, ring)
    high = fetch_x(both(2, half, rows).astype(BF), 1, ring)
    up = jnp.concatenate(
        [both(1, 0, half) + low.astype(F32), both(1, half, rows)], 0
    ).astype(BF)
    dn = jnp.concatenate(
        [both(3, 0, half), both(3, half, rows) + high.astype(F32)], 0
    ).astype(BF)
    return keep, got, fetch_x(up, -1, ring), fetch_x(dn, 1, ring)


def shards(
    activations,
    action_codes,
    norm_gain,
    action_scale,
    action_shift,
    qkv_weight,
    qk_gains,
    out_weight,
    grad_output,
):
    replicas = lax.axis_size("replica")
    shards_tm = lax.axis_size("tm")
    parts = lax.axis_size("tensor")
    ring = replicas * parts // CORES
    rep = lax.axis_index("replica")
    part = lax.axis_index("tensor")
    spot = lax.axis_index("tm")
    frames = action_codes.shape[1]
    quarter = activations.shape[2]
    patches = activations.shape[1]
    patch_dev = patches // shards_tm
    depth = qkv_weight.shape[0]
    heads = qkv_weight.shape[1] // replicas
    triple = qkv_weight.shape[2]
    width = triple // 3
    wide = heads * triple
    narrow = heads * width
    code_count = action_scale.shape[0]
    group = shards_tm * patch_dev
    tokens = replicas * group
    near = depth // 8 * 5
    place = jnp.stack(
        [
            rep,
            part,
            spot // NZ,
            spot % NZ,
            rep * (ring // replicas) + part // CORES,
            part % CORES,
        ]
    ).astype(jnp.int32)

    weight_near, weight_far = pl.pallas_call(
        pack_kernel,
        out_shape=(
            jax.ShapeDtypeStruct((near, wide + narrow), BF),
            jax.ShapeDtypeStruct((depth - near, wide + narrow), BF),
        ),
        in_specs=[SMEM] + [VMEM] * 2,
        out_specs=(VMEM, VMEM),
        compiler_params=pltpu.CompilerParams(vmem_limit_bytes=24 * 1024 * 1024),
        name="pack",
    )(place, qkv_weight.reshape(-1, triple), out_weight)

    def tokens_in(hold):
        both = pl.pallas_call(
            functools.partial(tokens_kernel, patch_dev),
            out_shape=jax.ShapeDtypeStruct((2 * patches, quarter), BF),
            in_specs=[VMEM] * 2 + [ANY],
            out_specs=VMEM,
            compiler_params=pltpu.CompilerParams(vmem_limit_bytes=24 * 1024 * 1024),
            name="tokens",
        )(activations.reshape(patches, quarter), grad_output.reshape(patches, quarter), hold)
        return lax.all_to_all(both, "tm", split_axis=0, concat_axis=0, tiled=True)

    def codes_in():
        return lax.ppermute(action_codes, "replica", [(i, 1 - i) for i in range(2)])

    def by_part(table):
        return table.reshape(table.shape[0], parts, quarter).transpose(1, 0, 2)

    big = jax.ShapeDtypeStruct((parts, tokens, quarter), BF)
    big_spec = pl.BlockSpec((parts, group, quarter), lambda i: (0, i, 0))
    own_spec = pl.BlockSpec((group, quarter), lambda i: (0, 0))

    def whole(*shape):
        return pl.BlockSpec(shape, lambda i: (0,) * len(shape))

    def tokens_ready(both, other):
        codes = jnp.where(
            rep == 0,
            jnp.concatenate([action_codes, other], 0),
            jnp.concatenate([other, action_codes], 0),
        ).reshape(-1)
        codes = jnp.repeat(codes, patch_dev)
        code_range = jnp.arange(code_count)
        hot = (codes[:, None] == code_range[None, :]).astype(BF)
        hot_t = (codes[None, :] == code_range[:, None]).astype(BF)
        full = lax.all_gather(both, ("replica", "tensor"), axis=0)
        full = full.reshape(replicas, parts, 2 * group, quarter)
        return hot_t, *pl.pallas_call(
            functools.partial(prep_kernel, patch_dev),
            grid=(replicas,),
            out_shape=(big, big, big)
            + (jax.ShapeDtypeStruct((group, quarter), F32),) * 2
            + (jax.ShapeDtypeStruct((group, quarter), BF),) * 2,
            in_specs=[
                SMEM,
                pl.BlockSpec((1, parts, 2 * group, quarter), lambda i: (i, 0, 0, 0)),
                pl.BlockSpec((group, code_count), lambda i: (i, 0)),
                whole(parts, 1, quarter),
                whole(parts, code_count, quarter),
                whole(parts, code_count, quarter),
            ],
            out_specs=(big_spec,) * 3 + (own_spec,) * 4,
            compiler_params=pltpu.CompilerParams(vmem_limit_bytes=48 * 1024 * 1024),
            name="prep",
        )(
            place,
            full,
            hot,
            by_part(norm_gain[None]),
            by_part(action_scale),
            by_part(action_shift),
        )

    pieces, plan, ready = gather_weight(
        weight_near, weight_far, codes_in, tokens_in, tokens_ready
    )
    hot_t, hidden, grad, normed, coef, xinv, x_own, g_own = ready

    shift_halves = jnp.concatenate(halves(by_part(action_shift)), 1)
    tail_rows = group + EXTRA
    y_shape = jax.ShapeDtypeStruct((ring, group, quarter), BF)
    dh_shape = jax.ShapeDtypeStruct((ring, tail_rows, quarter), BF)
    flops = 4 * tokens * parts * quarter * (wide + narrow)
    moved = 2 * parts * quarter * (wide + narrow + 5 * tokens)
    y_keep, y_give, dh_keep, dh_give = pl.pallas_call(
        functools.partial(block_kernel, patch_dev, frames, plan),
        out_shape=(y_shape, y_shape, dh_shape, dh_shape),
        in_specs=[SMEM, VMEM, VMEM, VMEM] + [ANY] * (3 + len(pieces)),
        out_specs=(ANY,) * 4,
        scratch_shapes=[
            pltpu.VMEM((parts, tokens + 2 * code_count, quarter), BF),
            pltpu.VMEM((parts, tokens, quarter), BF),
            pltpu.VMEM((parts, tokens, quarter), BF),
            pltpu.VMEM((parts * quarter, wide + narrow), BF),
            pltpu.VMEM((tokens + 2 * code_count, wide), F32),
            pltpu.VMEM((tokens, narrow), F32),
            pltpu.VMEM((tokens, narrow), BF),
            pltpu.VMEM((tokens + 2 * code_count, wide), BF),
            pltpu.VMEM((CORES, ring, group, quarter), BF),
            pltpu.VMEM((CORES, ring, tail_rows, quarter), BF),
            pltpu.SemaphoreType.DMA((parts, 3)),
            pltpu.SemaphoreType.DMA((len(plan),)),
            pltpu.SemaphoreType.DMA((2, ring, CORES)),
        ],
        compiler_params=pltpu.CompilerParams(vmem_limit_bytes=52 * 1024 * 1024),
        cost_estimate=pl.CostEstimate(flops=flops, bytes_accessed=moved, transcendentals=0),
        name="block",
    )(place, qk_gains, hot_t, shift_halves, hidden, grad, normed, *pieces)

    dh_terms = reduce_ring(dh_keep, dh_give, ring)
    y_terms = reduce_ring(y_keep, y_give, ring)
    first_y = pl.BlockSpec((1, group, quarter), lambda i: (0, 0, 0))
    first_dh = pl.BlockSpec((1, tail_rows, quarter), lambda i: (0, 0, 0))
    span = 2 * patch_dev + code_count
    send = pl.pallas_call(
        functools.partial(finish_kernel, patch_dev, code_count, parts),
        grid=(1,),
        out_shape=jax.ShapeDtypeStruct((shards_tm * span, quarter), BF),
        in_specs=[first_y] * 2
        + [whole(group, quarter)] * 2
        + [first_dh] * 2
        + [whole(tail_rows, quarter)] * 2
        + [whole(group, quarter)] * 4,
        out_specs=whole(shards_tm * span, quarter),
        compiler_params=pltpu.CompilerParams(vmem_limit_bytes=24 * 1024 * 1024),
        name="finish",
    )(*y_terms, *dh_terms, coef, xinv, x_own, g_own)
    back = lax.all_to_all(send, "tm", split_axis=0, concat_axis=0, tiled=True)
    token_total = tokens * shards_tm
    y_frames, dx_frames, grad_mine = pl.pallas_call(
        functools.partial(unpack_kernel, patch_dev, token_total ** (-0.5)),
        out_shape=(
            jax.ShapeDtypeStruct((group, quarter), BF),
            jax.ShapeDtypeStruct((group, quarter), BF),
            jax.ShapeDtypeStruct((code_count, quarter), F32),
        ),
        in_specs=[VMEM],
        out_specs=(VMEM, VMEM, VMEM),
        compiler_params=pltpu.CompilerParams(vmem_limit_bytes=24 * 1024 * 1024),
        name="unpack",
    )(back)
    grad_other = lax.ppermute(grad_mine, "replica", [(i, 1 - i) for i in range(2)])
    d_scale = jnp.where(rep == 0, grad_mine, grad_other)
    d_shift = jnp.where(rep == 0, grad_other, grad_mine)
    return (y_frames[None], dx_frames[None], d_scale, d_shift)


def solution(mesh):
    placed = (
        P(("replica", "tm"), None, "tensor"),
        P("replica", None),
        P(),
        P(),
        P(),
        P("tm", "tensor", None),
        P(),
        P("tensor", None, "tm"),
        P(("replica", "tm"), None, "tensor"),
    )
    return jax.shard_map(
        shards,
        mesh=mesh,
        in_specs=placed,
        out_specs=(
            P(("replica", "tm"), None, "tensor"),
            P(("replica", "tm"), None, "tensor"),
            P(None, "tensor"),
            P(None, "tensor"),
        ),
        check_vma=False,
    )
```

```python
import functools

import jax
import jax.numpy as jnp
from jax import lax
from jax.experimental import pallas as pl
from jax.experimental.pallas import tpu as pltpu
from jax.sharding import PartitionSpec as P

EPS = 1e-06
BF = jnp.bfloat16
F32 = jnp.float32
EXTRA = 16


def dot_nn(a, b):
    return lax.dot_general(a, b, (((1,), (0,)), ((), ())), preferred_element_type=F32)


def dot_nt(a, b):
    return lax.dot_general(a, b, (((1,), (1,)), ((), ())), preferred_element_type=F32)


def dot_tn(a, b):
    return lax.dot_general(a, b, (((0,), (0,)), ((), ())), preferred_element_type=F32)


def halves(value):
    high = value.astype(BF)
    return high, (value - high.astype(F32)).astype(BF)


def selector(shape, pick):
    row = lax.broadcasted_iota(jnp.int32, shape, 0)
    col = lax.broadcasted_iota(jnp.int32, shape, 1)
    return jnp.where(pick(row, col), 1.0, 0.0).astype(BF)


def tokens_kernel(patch_dev, x_ref, g_ref, hold_ref, both_ref):
    rows = x_ref.shape[0]
    pair = 2 * patch_dev
    pick_x = selector(
        (2 * rows, rows),
        lambda m, n: (m % pair < patch_dev) & (m // pair * patch_dev + m % pair == n),
    )
    pick_g = selector(
        (2 * rows, rows),
        lambda m, n: (m % pair >= patch_dev)
        & (m // pair * patch_dev + m % pair - patch_dev == n),
    )
    both_ref[...] = (dot_nn(pick_x, x_ref[...]) + dot_nn(pick_g, g_ref[...])).astype(BF)


def pack_kernel(place_ref, qkv_ref, out_ref, near_ref, far_ref):
    depth = near_ref.shape[0] + far_ref.shape[0]
    near = near_ref.shape[0]
    all_heads = qkv_ref.shape[0] // depth
    heads = out_ref.shape[0] // 2
    triple = qkv_ref.shape[1]
    width = triple // 3
    rep = place_ref[0]
    for head in range(heads):
        own = rep * heads + head
        pick = selector(
            (depth, all_heads * depth),
            lambda m, n: m * all_heads + own == n,
        )
        part = dot_nn(pick, qkv_ref[...]).astype(BF)
        cols = slice(head * triple, (head + 1) * triple)
        near_ref[:, cols] = part[:near]
        far_ref[:, cols] = part[near:]
        eye = selector((depth, depth), lambda m, n: m == n)
        part = dot_nt(eye, out_ref[own]).astype(BF)
        cols = slice(heads * triple + head * width, heads * triple + (head + 1) * width)
        near_ref[:, cols] = part[:near]
        far_ref[:, cols] = part[near:]


def prep_kernel(
    patch_dev,
    place_ref,
    full_ref,
    hot_ref,
    gain_ref,
    scale_ref,
    shift_ref,
    hidden_ref,
    grad_ref,
    normed_ref,
    coef_ref,
    xinv_ref,
    xown_ref,
    gown_ref,
):
    parts = full_ref.shape[1]
    group = hidden_ref.shape[1]
    quarter = full_ref.shape[3]
    pair = 2 * patch_dev
    pick_x = selector(
        (group, 2 * group), lambda m, n: m // patch_dev * pair + m % patch_dev == n
    )
    pick_g = selector(
        (group, 2 * group), lambda m, n: m // patch_dev * pair + m % patch_dev + patch_dev == n
    )
    hot = hot_ref[...]

    def rows_of(table):
        high, low = halves(table)
        return dot_nn(hot, high) + dot_nn(hot, low)

    square = jnp.zeros((group, 1), F32)
    for part in range(parts):
        x = dot_nn(pick_x, full_ref[0, part])
        square += jnp.sum(x * x, -1, keepdims=True)
    inverse = lax.rsqrt(square / (parts * quarter) + EPS)
    for part in range(parts):
        x = dot_nn(pick_x, full_ref[0, part])
        normed = x * inverse * gain_ref[part]
        scaled = normed * (1.0 + rows_of(scale_ref[part]))
        hidden_ref[part] = (scaled + rows_of(shift_ref[part])).astype(BF)
        normed_ref[part] = normed.astype(BF)
        grad_ref[part] = dot_nn(pick_g, full_ref[0, part]).astype(BF)

    @pl.when(pl.program_id(0) == place_ref[0])
    def _():
        own = place_ref[1]
        rows = full_ref[0, own]
        x = dot_nn(pick_x, rows)
        xown_ref[...] = x.astype(BF)
        gown_ref[...] = dot_nn(pick_g, rows).astype(BF)
        coef_ref[...] = inverse * (1.0 + rows_of(scale_ref[own])) * gain_ref[own]
        xinv_ref[...] = x * inverse * inverse


def block_kernel(
    patch_dev,
    frames,
    plan,
    place_ref,
    gains_ref,
    hot_ref,
    shift_ref,
    hidden_hbm,
    grad_hbm,
    normed_hbm,
    *refs,
):
    count = 1 + max(item[0] for item in plan)
    pieces = refs[:count]
    (
        y_keep,
        y_give,
        dh_keep,
        dh_give,
        hidden,
        grad,
        normed,
        weight,
        qkv_acc,
        da_acc,
        attended,
        dqkv,
        y_stage,
        dh_stage,
        sems,
        weight_sems,
        out_sems,
    ) = refs[count:]
    parts, tokens, quarter = grad.shape
    codes = hot_ref.shape[0]
    width = gains_ref.shape[1]
    wide = qkv_acc.shape[1]
    heads = wide // (3 * width)
    cores, ring, group, _ = y_stage.shape
    replicas = tokens // group
    along = ring // replicas
    rows_y = place_ref[2]
    rows_z = place_ref[3]
    spot_x = place_ref[4]
    core = place_ref[5]
    depth = weight.shape[0] // (NY * NZ)

    def inputs(at):
        part = (rows_y + at) % NY
        result = [
            pltpu.make_async_copy(
                hidden_hbm.at[part], hidden.at[part, pl.ds(0, tokens)], sems.at[at, 0]
            ),
            pltpu.make_async_copy(grad_hbm.at[part], grad.at[part], sems.at[at, 1]),
        ]
        for number, (index, start, size, dy, dz, place) in enumerate(plan):
            if dy == at:
                owner = part * NZ + (rows_z + dz) % NZ
                target = pl.multiple_of(owner * depth + place, 16)
                result.append(
                    pltpu.make_async_copy(
                        pieces[index].at[pl.ds(start, size)],
                        weight.at[pl.ds(target, size)],
                        weight_sems.at[number],
                    )
                )
        return result

    def second(part):
        return [pltpu.make_async_copy(normed_hbm.at[part], normed.at[part], sems.at[part, 2])]

    for at in range(NY):
        for copy in inputs(at):
            copy.start()
    for part in range(parts):
        for copy in second(part):
            copy.start()

    hidden[:, tokens:, :] = shift_ref[...]
    qkv_acc[...] = jnp.zeros_like(qkv_acc)
    da_acc[...] = jnp.zeros_like(da_acc)
    for at in range(NY):
        for copy in inputs(at):
            copy.wait()
        part = (rows_y + at) % NY
        rows = pl.ds(pl.multiple_of(part * quarter, quarter), quarter)
        qkv_acc[...] += dot_nn(hidden[part], weight[rows, :wide])
        da_acc[...] += dot_nn(grad[part], weight[rows, wide:])

    gain_q = gains_ref[0:1, :]
    gain_k = gains_ref[1:2, :]
    row = lax.broadcasted_iota(jnp.int32, (group, group), 0)
    col = lax.broadcasted_iota(jnp.int32, (group, group), 1)
    clip_tokens = frames * patch_dev
    mask = (
        (row % patch_dev == col % patch_dev)
        & (row // clip_tokens == col // clip_tokens)
        & (col <= row)
    )
    factor = width ** (-0.5)
    for rep in range(replicas):
        rows = slice(rep * group, (rep + 1) * group)
        for head in range(heads):
            base = head * 3 * width
            take = lambda at: qkv_acc[rows, base + at * width : base + (at + 1) * width].astype(
                BF
            )
            q = take(0).astype(F32)
            k = take(1).astype(F32)
            value = take(2)
            d_out = da_acc[rows, head * width : (head + 1) * width].astype(BF)
            inv_q = lax.rsqrt(jnp.mean(q * q, -1, keepdims=True) + EPS)
            inv_k = lax.rsqrt(jnp.mean(k * k, -1, keepdims=True) + EPS)
            q_hat = q * inv_q
            k_hat = k * inv_k
            queries = (q_hat * gain_q).astype(BF)
            keys = (k_hat * gain_k).astype(BF)
            scores = dot_nt(queries, keys) * factor
            weights = jnp.where(mask, jnp.exp(scores), 0.0)
            probs = weights / jnp.sum(weights, -1, keepdims=True)
            probs_bf = probs.astype(BF)
            out = dot_nn(probs_bf, value)
            attended[rows, head * width : (head + 1) * width] = out.astype(BF)
            d_value = dot_tn(probs_bf, d_out)
            d_probs = dot_nt(d_out, value)
            d_scores = probs * (d_probs - jnp.sum(d_probs * probs, -1, keepdims=True))
            d_scores = (d_scores * factor).astype(BF)
            d_q = dot_nn(d_scores, keys) * gain_q
            d_k = dot_tn(d_scores, queries) * gain_k
            d_q = inv_q * (d_q - q_hat * jnp.mean(d_q * q_hat, -1, keepdims=True))
            d_k = inv_k * (d_k - k_hat * jnp.mean(d_k * k_hat, -1, keepdims=True))
            for at, item in enumerate((d_q, d_k, d_value)):
                dqkv[rows, base + at * width : base + (at + 1) * width] = item.astype(BF)

    hot = hot_ref[...]
    lanes = min(wide, 128)
    terms = jnp.zeros((tokens, lanes), F32)
    for lane in range(wide // lanes):
        cols = slice(lane * lanes, (lane + 1) * lanes)
        terms += dqkv[:tokens, cols].astype(F32) * qkv_acc[:tokens, cols]
    ones = jnp.ones((8, lanes), BF)
    high, low = halves(terms)
    terms = dot_nt(ones, high) + dot_nt(ones, low)
    moved = qkv_acc[tokens : tokens + codes] + qkv_acc[tokens + codes :]
    high, low = halves(moved)
    moved = dot_nt(high, dqkv[:tokens]) + dot_nt(low, dqkv[:tokens])
    terms -= jnp.sum(moved * hot.astype(F32), 0, keepdims=True)
    high, low = halves(dot_nn(hot, dqkv[:tokens]))
    dqkv[tokens:, :] = jnp.concatenate([high, low], 0)

    def outputs(stage, keep, give, base):
        result = []
        for step in range(ring):
            target = (spot_x + step) % ring
            for side, out in enumerate((keep, give)):
                result.append(
                    pltpu.make_async_copy(
                        stage.at[(core + side) % cores, target],
                        out.at[step],
                        out_sems.at[base, step, side],
                    )
                )
        return result

    block = min(quarter, 512)
    for part in range(parts):
        for at in range(quarter // block):
            cols = slice(at * block, (at + 1) * block)
            w_block = weight[part * quarter + at * block : part * quarter + (at + 1) * block, wide:]
            y_block = dot_nt(attended[...], w_block).astype(BF)
            for rep in range(replicas):
                rows = slice(rep * group, (rep + 1) * group)
                y_stage[part % cores, rep * along + part // cores, :, cols] = y_block[rows]
    y_copies = outputs(y_stage, y_keep, y_give, 0)
    for copy in y_copies:
        copy.start()

    for part in range(parts):
        for copy in second(part):
            copy.wait()
    tail = dh_stage.shape[2] - group
    for part in range(parts):
        for at in range(quarter // block):
            cols = slice(at * block, (at + 1) * block)
            w_block = weight[part * quarter + at * block : part * quarter + (at + 1) * block, :wide]
            d_block = dot_nt(dqkv[...], w_block)
            d_shift = d_block[tokens : tokens + codes] + d_block[tokens + codes :]
            d_block = d_block[:tokens]
            d_rounded = d_block.astype(BF)
            d_scale = dot_nn(hot, (d_block * normed[part, :, cols].astype(F32)).astype(BF))
            for rep, item in enumerate((d_scale, d_shift)):
                where = (part % cores, rep * along + part // cores)
                rows = slice(rep * group, (rep + 1) * group)
                dh_stage[where[0], where[1], 0:group, cols] = d_rounded[rows]
                dh_stage[where[0], where[1], group : group + codes, cols] = item.astype(BF)
    high, low = halves(terms)
    sub = lax.broadcasted_iota(jnp.int32, (8, group), 0)
    for rep in range(replicas):
        mine = slice(rep * group, (rep + 1) * group)
        both = jnp.where(
            sub == 0,
            high[:, mine].astype(F32),
            jnp.where(sub == 1, low[:, mine].astype(F32), 0.0),
        ).astype(BF)
        for part in range(parts):
            where = (part % cores, rep * along + part // cores)
            dh_stage[where[0], where[1], group + codes :, :] = jnp.zeros(
                (tail - codes, quarter), BF
            )
            dh_stage[where[0], where[1], group + codes : group + codes + 8, 0:group] = both
    dh_copies = outputs(dh_stage, dh_keep, dh_give, 1)
    for copy in dh_copies:
        copy.start()
    for copy in y_copies + dh_copies:
        copy.wait()


def finish_kernel(
    patch_dev,
    code_count,
    parts,
    yk_ref,
    yr_ref,
    ya_ref,
    yb_ref,
    dk_ref,
    dr_ref,
    da_ref,
    db_ref,
    coef_ref,
    xinv_ref,
    xown_ref,
    gown_ref,
    send_ref,
):
    group, quarter = xown_ref.shape
    y = (
        xown_ref[...].astype(F32)
        + (yk_ref[0].astype(F32) + yr_ref[0].astype(F32))
        + (ya_ref[...].astype(F32) + yb_ref[...].astype(F32))
    )
    total = (dk_ref[0].astype(F32) + dr_ref[0].astype(F32)) + (
        da_ref[...].astype(F32) + db_ref[...].astype(F32)
    )
    terms = total[group + code_count : group + code_count + 8, :group]
    term = (terms[0:1] + terms[1:2]) / (quarter * parts)
    term = jnp.broadcast_to(term, (group, group)).T[:, 0:1]
    dx = gown_ref[...].astype(F32) + (total[:group] * coef_ref[...] - xinv_ref[...] * term)
    grads = total[group : group + code_count].astype(BF)
    span = 2 * patch_dev + code_count
    rows = send_ref.shape[0]
    pick_y = selector(
        (rows, group),
        lambda m, n: (m % span < patch_dev) & (m // span * patch_dev + m % span == n),
    )
    pick_d = selector(
        (rows, group),
        lambda m, n: (m % span >= patch_dev)
        & (m % span < 2 * patch_dev)
        & (m // span * patch_dev + m % span - patch_dev == n),
    )
    pick_g = selector((rows, code_count), lambda m, n: m % span - 2 * patch_dev == n)
    send_ref[...] = (
        dot_nn(pick_y, y.astype(BF)) + dot_nn(pick_d, dx.astype(BF)) + dot_nn(pick_g, grads)
    ).astype(BF)


def unpack_kernel(patch_dev, factor, back_ref, y_ref, dx_ref, sum_ref):
    group = y_ref.shape[0]
    rows = back_ref.shape[0]
    codes = sum_ref.shape[0]
    span = 2 * patch_dev + codes
    back = back_ref[...]
    pick_y = selector((group, rows), lambda m, n: m // patch_dev * span + m % patch_dev == n)
    pick_d = selector(
        (group, rows), lambda m, n: m // patch_dev * span + m % patch_dev + patch_dev == n
    )
    pick_g = selector((codes, rows), lambda m, n: n % span - 2 * patch_dev == m)
    y_ref[...] = dot_nn(pick_y, back).astype(BF)
    dx_ref[...] = dot_nn(pick_d, back).astype(BF)
    sum_ref[...] = dot_nn(pick_g, back) * factor


NY = 4
NZ = 8
CORES = 2
VMEM = pl.BlockSpec(memory_space=pltpu.VMEM)
SMEM = pl.BlockSpec(memory_space=pltpu.SMEM)
ANY = pl.BlockSpec(memory_space=pl.ANY)


def fetch(value, dy, dz):
    pairs = []
    for y in range(NY):
        for z in range(NZ):
            pairs.append((((y + dy) % NY) * NZ + (z + dz) % NZ, y * NZ + z))
    return lax.ppermute(value, "tm", pairs)


def fetch_x(value, dx, ring):
    pairs = []
    for x in range(ring):
        for core in range(CORES):
            pairs.append((((x + dx) % ring) * CORES + core, x * CORES + core))
    return lax.ppermute(value, ("replica", "tensor"), pairs)


def swap_cores(value, ring):
    pairs = []
    for x in range(ring):
        for core in range(CORES):
            pairs.append((x * CORES + core, x * CORES + 1 - core))
    return lax.ppermute(value, ("replica", "tensor"), pairs)


def gate(*values):
    return lax.optimization_barrier(values)


def gather_weight(near, far, codes, codes_in, tokens_in, tokens_ready):
    a = near.shape[0]
    b = far.shape[0]
    pieces = []
    plan = []

    def add(value, blocks):
        start = 0
        for size, dy, dz, place in blocks:
            plan.append((len(pieces), start, size, dy % NY, dz % NZ, place))
            start += size
        pieces.append(value)

    def line(dy, *dzs):
        return [(a, dy, dz, 0) for dz in dzs]

    def column(dz, ys=(0, 1, -1, 2)):
        return [(b, dy, dz, a) for dy in ys]

    def pair(value, dzs):
        up, dn = fetch(value, 1, 0), fetch(value, -1, 0)
        add(value, line(0, *dzs))
        add(up, line(1, *dzs))
        add(dn, line(-1, *dzs))
        return up, dn

    zu, zd = fetch(near, 0, 1), fetch(near, 0, -1)
    fu, fd, fo = fetch(far, 1, 0), fetch(far, -1, 0), fetch(far, 2, 0)
    near, far, zu, zd, fu, fd, fo = gate(near, far, zu, zd, fu, fd, fo)
    cols = jnp.concatenate([far, fu, fd, fo], 0)
    add(cols, column(0))
    first_at = (0, 1, -1)
    up1, dn1 = pair(jnp.concatenate([near, zu, zd], 0), first_at)
    zu2, zd2 = fetch(zu, 0, 1), fetch(zd, 0, -1)
    zu3, zd3 = fetch(zu2, 0, 1), fetch(zd2, 0, -1)
    z4 = fetch(zu3, 0, 1)
    up1, dn1, zu2, zd2, zu3, zd3, z4, cols, codes = gate(
        up1, dn1, zu2, zd2, zu3, zd3, z4, cols, codes
    )
    second_at = (2, -2, 3)
    up2, dn2 = pair(jnp.concatenate([zu2, zd2, zu3], 0), second_at)
    cu, cd = fetch(cols, 0, 1), fetch(cols, 0, -1)
    codes = codes_in(codes)
    token = tokens_in(codes)
    up2, dn2, cu, cd, token = gate(up2, dn2, cu, cd, token)
    add(cu, column(1))
    add(cd, column(-1))
    third_at = (-3, 4)
    up3, dn3 = pair(jnp.concatenate([zd3, z4], 0), third_at)
    cu2, cd2 = fetch(cu, 0, 1), fetch(cd, 0, -1)
    up3, dn3, cu2, cd2 = gate(up3, dn3, cu2, cd2)
    add(cu2, column(2))
    add(cd2, column(-2))
    cu3, cd3 = fetch(cu2, 0, 1), fetch(cd2, 0, -1)
    x1, x2 = fetch(up1, 1, 0), fetch(dn2, -1, 0)
    add(x1, line(2, *first_at))
    add(x2, line(2, *second_at))
    ready = tokens_ready(token, codes)
    cu3, cd3, x1, x2, *ready = gate(cu3, cd3, x1, x2, *ready)
    add(cu3, column(3))
    add(cd3, column(-3))
    add(fetch(cu3[: 2 * b], 0, 1), column(4, (0, 1)))
    add(fetch(cd3[2 * b :], 0, -1), column(4, (-1, 2)))
    add(fetch(up3[:a], 1, 0), line(2, -3))
    add(fetch(dn3[a:], -1, 0), line(2, 4))
    return pieces, tuple(plan), ready


def reduce_ring(keep, give, ring):
    got = swap_cores(give, ring)
    rows = keep.shape[1]
    half = rows // 32 * 16

    def both(at, rows_from, rows_to):
        return keep[at, rows_from:rows_to].astype(F32) + got[at, rows_from:rows_to].astype(F32)

    low = fetch_x(both(2, 0, half).astype(BF), -1, ring)
    high = fetch_x(both(2, half, rows).astype(BF), 1, ring)
    up = jnp.concatenate(
        [both(1, 0, half) + low.astype(F32), both(1, half, rows)], 0
    ).astype(BF)
    dn = jnp.concatenate(
        [both(3, 0, half), both(3, half, rows) + high.astype(F32)], 0
    ).astype(BF)
    return keep, got, fetch_x(up, -1, ring), fetch_x(dn, 1, ring)


def shards(
    activations,
    action_codes,
    norm_gain,
    action_scale,
    action_shift,
    qkv_weight,
    qk_gains,
    out_weight,
    grad_output,
):
    replicas = lax.axis_size("replica")
    shards_tm = lax.axis_size("tm")
    parts = lax.axis_size("tensor")
    ring = replicas * parts // CORES
    rep = lax.axis_index("replica")
    part = lax.axis_index("tensor")
    spot = lax.axis_index("tm")
    frames = action_codes.shape[1]
    quarter = activations.shape[2]
    patches = activations.shape[1]
    patch_dev = patches // shards_tm
    depth = qkv_weight.shape[0]
    heads = qkv_weight.shape[1] // replicas
    triple = qkv_weight.shape[2]
    width = triple // 3
    wide = heads * triple
    narrow = heads * width
    code_count = action_scale.shape[0]
    group = shards_tm * patch_dev
    tokens = replicas * group
    near = depth // 8 * 5
    place = jnp.stack(
        [
            rep,
            part,
            spot // NZ,
            spot % NZ,
            rep * (ring // replicas) + part // CORES,
            part % CORES,
        ]
    ).astype(jnp.int32)

    weight_near, weight_far = pl.pallas_call(
        pack_kernel,
        out_shape=(
            jax.ShapeDtypeStruct((near, wide + narrow), BF),
            jax.ShapeDtypeStruct((depth - near, wide + narrow), BF),
        ),
        in_specs=[SMEM] + [VMEM] * 2,
        out_specs=(VMEM, VMEM),
        compiler_params=pltpu.CompilerParams(vmem_limit_bytes=24 * 1024 * 1024),
        name="pack",
    )(place, qkv_weight.reshape(-1, triple), out_weight)

    def tokens_in(hold):
        both = pl.pallas_call(
            functools.partial(tokens_kernel, patch_dev),
            out_shape=jax.ShapeDtypeStruct((2 * patches, quarter), BF),
            in_specs=[VMEM] * 2 + [ANY],
            out_specs=VMEM,
            compiler_params=pltpu.CompilerParams(vmem_limit_bytes=24 * 1024 * 1024),
            name="tokens",
        )(activations.reshape(patches, quarter), grad_output.reshape(patches, quarter), hold)
        return lax.all_to_all(both, "tm", split_axis=0, concat_axis=0, tiled=True)

    def codes_in(value):
        return lax.ppermute(value, "replica", [(i, 1 - i) for i in range(2)])

    def by_part(table):
        return table.reshape(table.shape[0], parts, quarter).transpose(1, 0, 2)

    big = jax.ShapeDtypeStruct((parts, tokens, quarter), BF)
    big_spec = pl.BlockSpec((parts, group, quarter), lambda i: (0, i, 0))
    own_spec = pl.BlockSpec((group, quarter), lambda i: (0, 0))

    def whole(*shape):
        return pl.BlockSpec(shape, lambda i: (0,) * len(shape))

    def tokens_ready(both, other):
        codes = jnp.where(
            rep == 0,
            jnp.concatenate([action_codes, other], 0),
            jnp.concatenate([other, action_codes], 0),
        ).reshape(-1)
        codes = jnp.repeat(codes, patch_dev)
        code_range = jnp.arange(code_count)
        hot = (codes[:, None] == code_range[None, :]).astype(BF)
        hot_t = (codes[None, :] == code_range[:, None]).astype(BF)
        full = lax.all_gather(both, ("replica", "tensor"), axis=0)
        full = full.reshape(replicas, parts, 2 * group, quarter)
        return hot_t, *pl.pallas_call(
            functools.partial(prep_kernel, patch_dev),
            grid=(replicas,),
            out_shape=(big, big, big)
            + (jax.ShapeDtypeStruct((group, quarter), F32),) * 2
            + (jax.ShapeDtypeStruct((group, quarter), BF),) * 2,
            in_specs=[
                SMEM,
                pl.BlockSpec((1, parts, 2 * group, quarter), lambda i: (i, 0, 0, 0)),
                pl.BlockSpec((group, code_count), lambda i: (i, 0)),
                whole(parts, 1, quarter),
                whole(parts, code_count, quarter),
                whole(parts, code_count, quarter),
            ],
            out_specs=(big_spec,) * 3 + (own_spec,) * 4,
            compiler_params=pltpu.CompilerParams(vmem_limit_bytes=48 * 1024 * 1024),
            name="prep",
        )(
            place,
            full,
            hot,
            by_part(norm_gain[None]),
            by_part(action_scale),
            by_part(action_shift),
        )

    pieces, plan, ready = gather_weight(
        weight_near, weight_far, action_codes, codes_in, tokens_in, tokens_ready
    )
    hot_t, hidden, grad, normed, coef, xinv, x_own, g_own = ready

    shift_halves = jnp.concatenate(halves(by_part(action_shift)), 1)
    tail_rows = group + EXTRA
    y_shape = jax.ShapeDtypeStruct((ring, group, quarter), BF)
    dh_shape = jax.ShapeDtypeStruct((ring, tail_rows, quarter), BF)
    flops = 4 * tokens * parts * quarter * (wide + narrow)
    moved = 2 * parts * quarter * (wide + narrow + 5 * tokens)
    y_keep, y_give, dh_keep, dh_give = pl.pallas_call(
        functools.partial(block_kernel, patch_dev, frames, plan),
        out_shape=(y_shape, y_shape, dh_shape, dh_shape),
        in_specs=[SMEM, VMEM, VMEM, VMEM] + [ANY] * (3 + len(pieces)),
        out_specs=(ANY,) * 4,
        scratch_shapes=[
            pltpu.VMEM((parts, tokens + 2 * code_count, quarter), BF),
            pltpu.VMEM((parts, tokens, quarter), BF),
            pltpu.VMEM((parts, tokens, quarter), BF),
            pltpu.VMEM((parts * quarter, wide + narrow), BF),
            pltpu.VMEM((tokens + 2 * code_count, wide), F32),
            pltpu.VMEM((tokens, narrow), F32),
            pltpu.VMEM((tokens, narrow), BF),
            pltpu.VMEM((tokens + 2 * code_count, wide), BF),
            pltpu.VMEM((CORES, ring, group, quarter), BF),
            pltpu.VMEM((CORES, ring, tail_rows, quarter), BF),
            pltpu.SemaphoreType.DMA((parts, 3)),
            pltpu.SemaphoreType.DMA((len(plan),)),
            pltpu.SemaphoreType.DMA((2, ring, CORES)),
        ],
        compiler_params=pltpu.CompilerParams(vmem_limit_bytes=52 * 1024 * 1024),
        cost_estimate=pl.CostEstimate(flops=flops, bytes_accessed=moved, transcendentals=0),
        name="block",
    )(place, qk_gains, hot_t, shift_halves, hidden, grad, normed, *pieces)

    dh_terms = reduce_ring(dh_keep, dh_give, ring)
    y_terms = reduce_ring(y_keep, y_give, ring)
    first_y = pl.BlockSpec((1, group, quarter), lambda i: (0, 0, 0))
    first_dh = pl.BlockSpec((1, tail_rows, quarter), lambda i: (0, 0, 0))
    span = 2 * patch_dev + code_count
    send = pl.pallas_call(
        functools.partial(finish_kernel, patch_dev, code_count, parts),
        grid=(1,),
        out_shape=jax.ShapeDtypeStruct((shards_tm * span, quarter), BF),
        in_specs=[first_y] * 2
        + [whole(group, quarter)] * 2
        + [first_dh] * 2
        + [whole(tail_rows, quarter)] * 2
        + [whole(group, quarter)] * 4,
        out_specs=whole(shards_tm * span, quarter),
        compiler_params=pltpu.CompilerParams(vmem_limit_bytes=24 * 1024 * 1024),
        name="finish",
    )(*y_terms, *dh_terms, coef, xinv, x_own, g_own)
    back = lax.all_to_all(send, "tm", split_axis=0, concat_axis=0, tiled=True)
    token_total = tokens * shards_tm
    y_frames, dx_frames, grad_mine = pl.pallas_call(
        functools.partial(unpack_kernel, patch_dev, token_total ** (-0.5)),
        out_shape=(
            jax.ShapeDtypeStruct((group, quarter), BF),
            jax.ShapeDtypeStruct((group, quarter), BF),
            jax.ShapeDtypeStruct((code_count, quarter), F32),
        ),
        in_specs=[VMEM],
        out_specs=(VMEM, VMEM, VMEM),
        compiler_params=pltpu.CompilerParams(vmem_limit_bytes=24 * 1024 * 1024),
        name="unpack",
    )(back)
    grad_other = lax.ppermute(grad_mine, "replica", [(i, 1 - i) for i in range(2)])
    d_scale = jnp.where(rep == 0, grad_mine, grad_other)
    d_shift = jnp.where(rep == 0, grad_other, grad_mine)
    return (y_frames[None], dx_frames[None], d_scale, d_shift)


def solution(mesh):
    placed = (
        P(("replica", "tm"), None, "tensor"),
        P("replica", None),
        P(),
        P(),
        P(),
        P("tm", "tensor", None),
        P(),
        P("tensor", None, "tm"),
        P(("replica", "tm"), None, "tensor"),
    )
    return jax.shard_map(
        shards,
        mesh=mesh,
        in_specs=placed,
        out_specs=(
            P(("replica", "tm"), None, "tensor"),
            P(("replica", "tm"), None, "tensor"),
            P(None, "tensor"),
            P(None, "tensor"),
        ),
        check_vma=False,
    )
```
